768 devices in a mesh: dp: 48 (over y_lo, z, core), mp: 16 (over y_hi, x).
Axes of the slice: x: 4, y: 8 (y_hi: 4, y_lo: 2; y = y_hi * 2 + y_lo), z: 12, core: 2. Of those that a mesh axis runs over, the one named last changes fastest.
Arguments:
- layer_entry_matrix: bfloat16 [12288, 8192], P('dp', 'mp'), may hold values from -6 to 6
- stored_projector: bfloat16 [8448, 1024], P(('dp', 'mp')), may hold values from -0.0625 to 0.0625
- projection_adjoint: bfloat16 [12288, 1024], P('dp', 'mp'), may hold values from -2 to 2
- active_mask: int32 [96], P('dp'), may hold values from 0 to 1, as said below
Outputs:
- kv_values: bfloat16 [12288, 1024], P('dp', 'mp')
- activation_grad: bfloat16 [12288, 8192], P('dp', 'mp')
- weight_grad: float32 [8448, 1024], P(('dp', 'mp'))
The draws below stay inside these ranges and needn't reach their ends.
Inputs may be any that keep to these rules, and one draw needn't show every extreme that they name: `active_mask`: sequence j of the dp index i is entry 2 * i + j. The dp indices i and i + 24 together hold exactly 2 surviving sequences, and some dp index holds 2 survivors.
All inputs are finite; a program needn't handle non-finite values.
Results may differ from the reference program's by a relative error of at most 0.018.
Values may be sent and summed in bfloat16 or wider, within the bound.
No kernel may reach another device: no remote copies, remote signals or barrier semaphores. Data moves between devices by JAX's collectives and lax.ppermute only.
A program may use at most 32 MiB of HBM per device.

```python
import jax
import jax.numpy as jnp

D = 8192
KVW = 1024
CONTEXT_SPAN = 128
N_SEQ = 96
TOKENS = 12288
DM = 512
WROWS = 11
WALL = 8448
N_DP = 48
N_MP = 16


def draw_active_mask(key, part):
    key = jax.random.fold_in(key, 7)
    key_count, key_force, key_side = jax.random.split(key, 3)
    pair_count = N_DP // 2
    counts = jax.random.randint(key_count, (pair_count,), 0, 3)
    forced = jax.random.randint(key_force, (), 0, pair_count)
    counts = jnp.where(jnp.arange(pair_count) == forced, 2, counts)
    all_counts = jnp.concatenate([counts, 2 - counts])
    side_bit = jax.random.randint(key_side, (N_DP,), 0, 2)
    first_alive = (all_counts == 2) | (all_counts == 1) & (side_bit == 0)
    second_alive = (all_counts == 2) | (all_counts == 1) & (side_bit == 1)
    return jnp.stack([first_alive, second_alive], 1).reshape(N_SEQ).astype(jnp.int32)


def level_of(own_key, dims, shards, low, largest):
    loudness, own = 1.0, jax.random.fold_in(own_key, 6)
    for dim, blocks in shards:
        steps = jnp.exp(jax.random.uniform(jax.random.fold_in(own, dim), (blocks,), jnp.float32, low / len(shards), largest / len(shards)))
        loudness = loudness * jnp.repeat(steps, dims[dim] // blocks).reshape([-1 if axis == dim else 1 for axis in range(len(dims))])
    return loudness


def normal_values(stream_key, dims, spread, bound, cuts=(), dtype=jnp.bfloat16):
    drawn = jax.random.normal(stream_key, dims, jnp.float32) * spread
    if len(cuts) > 0:
        drawn = level_of(stream_key, dims, cuts, -0.22, 0.18) * drawn
    return jnp.clip(drawn, min=-bound, max=bound).astype(dtype)


def setup_inputs(seed: int = 0) -> dict:
    key_list = jax.random.split(jax.random.key(seed), 5)
    return {
        "layer_entry_matrix": normal_values(key_list[0], (TOKENS, D), 1.0, 6.0, ((0, 48), (1, 16))),
        "stored_projector": normal_values(key_list[1], (WALL, KVW), D ** -0.5, 0.0625, ((0, 768),)),
        "projection_adjoint": normal_values(key_list[2], (TOKENS, KVW), 0.15, 2.0, ((0, 48), (1, 16))),
        "active_mask": draw_active_mask(jax.random.fold_in(key_list[4], 71), 0),
    }


def reference(layer_entry_matrix, stored_projector, projection_adjoint, active_mask):
    stacked = stored_projector.reshape(N_DP, N_MP, WROWS, KVW).transpose(1, 0, 2, 3)
    stacked = stacked.reshape(N_MP, N_DP * WROWS, KVW)[:, :DM]
    full_weight = stacked.reshape(D, KVW)
    kept_lines = jnp.repeat(active_mask, CONTEXT_SPAN)[:, None]
    keep_float = kept_lines.astype(jnp.float32)
    projected = jnp.zeros((TOKENS, KVW), jnp.float32)
    for group in range(N_MP):
        group_partial = jnp.dot(layer_entry_matrix[:, group * DM:(group + 1) * DM], stacked[group], preferred_element_type=jnp.float32).astype(jnp.bfloat16)
        projected = projected + group_partial.astype(jnp.float32)
    kv_values = (keep_float * projected).astype(jnp.bfloat16)
    grad_kv = projection_adjoint * kept_lines.astype(jnp.bfloat16)
    activation_grad = jnp.dot(grad_kv, full_weight.T, preferred_element_type=jnp.float32).astype(jnp.bfloat16)
    dense_grad = jnp.dot(layer_entry_matrix.T, grad_kv, preferred_element_type=jnp.float32)
    grouped = dense_grad.reshape(N_MP, DM, KVW)
    grouped = jnp.pad(grouped, ((0, 0), (0, N_DP * WROWS - DM), (0, 0)))
    grouped = grouped.reshape(N_MP, N_DP, WROWS, KVW).transpose(1, 0, 2, 3)
    weight_grad = grouped.reshape(WALL, KVW)
    return kv_values, activation_grad, weight_grad
```

```python
import jax
import jax.numpy as jnp
from jax import lax
from jax.sharding import Mesh, PartitionSpec as P

BF16 = jnp.bfloat16
F32 = jnp.float32
SWAP = [(0, 1), (1, 0)]


def swap_pair(value):
    return lax.ppermute(value, "pair", SWAP)


def swap_core(value):
    return lax.ppermute(value, "core", SWAP)


def on_device(x, w, adjoint, mask):
    seqs = mask.shape[0]
    tokens, feats = x.shape
    span = tokens // seqs
    wrows, cols = w.shape
    n_z = lax.axis_size("z")
    n_mp = lax.axis_size("mp")
    own_cols = cols // n_mp
    half = own_cols // 2
    side = lax.axis_index("pair")
    core = lax.axis_index("core")

    alive = mask != 0
    count = jnp.sum(mask)
    first_count = jnp.where(side == 0, count, 2 - count)
    skip_first = jnp.logical_not(alive[0])

    def survivor_first(value):
        return jnp.where(skip_first, value[::-1], value)

    def compact(own, other):
        a0 = jnp.where(side == 0, own[0], other[0])
        a1 = jnp.where(side == 0, own[1], other[1])
        b0 = jnp.where(side == 0, other[0], own[0])
        b1 = jnp.where(side == 0, other[1], own[1])
        slot0 = jnp.where(first_count >= 1, a0, b0)
        slot1 = jnp.where(first_count == 2, a1, jnp.where(first_count == 1, b0, b1))
        return jnp.stack([slot0, slot1])

    start = jnp.where(side == 0, 0, 2 - count)

    def home(slots):
        second = start + mask[0]
        rows0 = jnp.where(start == 0, slots[0], slots[1])
        rows1 = jnp.where(second == 0, slots[0], slots[1])
        zero = jnp.zeros_like(rows0)
        return jnp.stack([jnp.where(alive[0], rows0, zero), jnp.where(alive[1], rows1, zero)])

    w_parts = w.reshape(wrows, n_mp, 2, half)
    w_mine = jnp.where(side == 0, w_parts[:, :, 0], w_parts[:, :, 1]).reshape(wrows, n_mp * half)
    w_theirs = jnp.where(side == 0, w_parts[:, :, 1], w_parts[:, :, 0]).reshape(wrows, n_mp * half)
    g = survivor_first(adjoint.T.reshape(2, half, seqs, span).transpose(2, 0, 1, 3))
    g_mine = jnp.where(side == 0, g[:, 0], g[:, 1])
    g_theirs = jnp.where(side == 0, g[:, 1], g[:, 0])
    xs = survivor_first(x.reshape(seqs, span, feats))

    w_other = swap_pair(w_theirs)
    g_other = swap_pair(g_theirs)
    x_other = swap_pair(xs)

    w_block = jnp.where(side == 0, jnp.stack([w_mine, w_other]), jnp.stack([w_other, w_mine]))
    w_block = w_block.reshape(1, 2 * wrows, n_mp * half)
    w_z = lax.all_to_all(jnp.broadcast_to(w_block, (n_z,) + w_block.shape[1:]), "z", 0, 0, tiled=True)
    w_z_other = swap_core(w_z)

    g_pair = compact(g_mine, g_other)
    g_cols = g_pair.transpose(1, 0, 2).reshape(1, half, tokens)
    g_all = lax.all_to_all(jnp.broadcast_to(g_cols, (n_mp, half, tokens)), "mp", 0, 0, tiled=True)
    g_all = g_all.reshape(n_mp * half, tokens)
    x_pair = compact(xs, x_other).reshape(tokens, feats)

    w_cores = jnp.where(core == 0, jnp.stack([w_z, w_z_other]), jnp.stack([w_z_other, w_z]))
    w_full = w_cores.reshape(2, n_z, 2, wrows, n_mp * half).transpose(2, 1, 0, 3, 4)
    w_full = w_full.reshape(4 * n_z * wrows, n_mp * half)[:feats]

    dw = lax.dot_general(x_pair, g_all, (((0,), (1,)), ((), ())), preferred_element_type=F32)
    dw = jnp.pad(dw, ((0, 4 * n_z * wrows - feats), (0, 0)))
    dw = dw.reshape(2, n_z, 2, wrows, n_mp * half).transpose(2, 1, 0, 3, 4)
    dw_mine = jnp.where(core == 0, dw[0], dw[1])
    dw_theirs = jnp.where(core == 0, dw[1], dw[0]).astype(BF16)
    dw_sum = dw_mine + swap_core(dw_theirs).astype(F32)
    dw_z = dw_sum.astype(BF16).reshape(n_z, 2 * wrows, n_mp * half)
    dw_z = lax.all_to_all(dw_z, "z", 0, 0, tiled=True)
    dw_rows = jnp.sum(dw_z.astype(F32), axis=0).reshape(2, wrows, n_mp * half)
    dw_own = jnp.where(side == 0, dw_rows[0], dw_rows[1])
    dw_send = jnp.where(side == 0, dw_rows[1], dw_rows[0])
    dw_other = swap_pair(dw_send)
    dw_own = dw_own.reshape(wrows, n_mp, 1, half)
    dw_other = dw_other.reshape(wrows, n_mp, 1, half)
    weight_grad = jnp.where(
        side == 0,
        jnp.concatenate([dw_own, dw_other], axis=2),
        jnp.concatenate([dw_other, dw_own], axis=2),
    ).reshape(wrows, cols)

    kv = lax.dot_general(w_full, x_pair, (((0,), (1,)), ((), ())), preferred_element_type=F32)
    kv = lax.all_to_all(kv.astype(BF16).reshape(n_mp, half, tokens), "mp", 0, 0, tiled=True)
    kv = jnp.sum(kv.astype(F32), axis=0).astype(BF16)
    kv_other = swap_pair(kv)
    kv_cols = jnp.where(side == 0, jnp.concatenate([kv, kv_other]), jnp.concatenate([kv_other, kv]))
    kv_home = home(kv_cols.reshape(own_cols, seqs, span).transpose(1, 0, 2))
    kv_values = kv_home.transpose(0, 2, 1).reshape(tokens, own_cols)

    dx = lax.dot_general(g_all, w_full, (((0,), (1,)), ((), ())), preferred_element_type=F32)
    dx_other = swap_pair(dx.astype(BF16))
    dx = (dx + dx_other.astype(F32)).astype(BF16)
    activation_grad = home(dx.reshape(seqs, span, feats)).reshape(tokens, feats)
    return kv_values, activation_grad, weight_grad


def solution(mesh):
    n_dp, n_mp = mesh.devices.shape
    names = ("pair", "z", "core", "mp")
    split = Mesh(mesh.devices.reshape(2, n_dp // 4, 2, n_mp), names)
    dp = ("pair", "z", "core")
    return jax.shard_map(
        on_device,
        mesh=split,
        in_specs=(P(dp, "mp"), P((*dp, "mp"), None), P(dp, "mp"), P(dp)),
        out_specs=(P(dp, "mp"), P(dp, "mp"), P((*dp, "mp"), None)),
        check_vma=False,
    )
```

```python
import jax
import jax.numpy as jnp
from jax import lax
from jax.sharding import Mesh, PartitionSpec as P

BF16 = jnp.bfloat16
F32 = jnp.float32
SWAP = [(0, 1), (1, 0)]


def swap_pair(value):
    return lax.ppermute(value, "pair", SWAP)


def swap_core(value):
    return lax.ppermute(value, "core", SWAP)


def on_device(x, w, adjoint, mask):
    seqs = mask.shape[0]
    tokens, feats = x.shape
    span = tokens // seqs
    wrows, cols = w.shape
    n_z = lax.axis_size("z")
    n_mp = lax.axis_size("mp")
    own_cols = cols // n_mp
    half = own_cols // 2
    side = lax.axis_index("pair")
    core = lax.axis_index("core")

    alive = mask != 0
    count = jnp.sum(mask)
    first_count = jnp.where(side == 0, count, 2 - count)
    skip_first = jnp.logical_not(alive[0])

    def survivor_first(value):
        return jnp.where(skip_first, value[::-1], value)

    def compact(own, other):
        a0 = jnp.where(side == 0, own[0], other[0])
        a1 = jnp.where(side == 0, own[1], other[1])
        b0 = jnp.where(side == 0, other[0], own[0])
        b1 = jnp.where(side == 0, other[1], own[1])
        slot0 = jnp.where(first_count >= 1, a0, b0)
        slot1 = jnp.where(first_count == 2, a1, jnp.where(first_count == 1, b0, b1))
        return jnp.stack([slot0, slot1])

    start = jnp.where(side == 0, 0, 2 - count)

    def home(slots):
        second = start + mask[0]
        rows0 = jnp.where(start == 0, slots[0], slots[1])
        rows1 = jnp.where(second == 0, slots[0], slots[1])
        zero = jnp.zeros_like(rows0)
        return jnp.stack([jnp.where(alive[0], rows0, zero), jnp.where(alive[1], rows1, zero)])

    w_parts = w.reshape(wrows, n_mp, 2, half)
    w_mine = jnp.where(side == 0, w_parts[:, :, 0], w_parts[:, :, 1]).reshape(wrows, n_mp * half)
    w_theirs = jnp.where(side == 0, w_parts[:, :, 1], w_parts[:, :, 0]).reshape(wrows, n_mp * half)
    g = survivor_first(adjoint.T.reshape(2, half, seqs, span).transpose(2, 0, 1, 3))
    g_mine = jnp.where(side == 0, g[:, 0], g[:, 1])
    g_theirs = jnp.where(side == 0, g[:, 1], g[:, 0])
    xs = survivor_first(x.reshape(seqs, span, feats))

    w_other = swap_pair(w_theirs)
    g_other = swap_pair(g_theirs)
    x_other = swap_pair(xs)

    w_block = jnp.where(side == 0, jnp.stack([w_mine, w_other]), jnp.stack([w_other, w_mine]))

    g_pair = compact(g_mine, g_other)
    g_cols = g_pair.transpose(1, 0, 2).reshape(1, half, tokens)
    g_send = jnp.broadcast_to(g_cols, (n_mp, half, tokens))
    w_block = w_block.reshape(1, 2 * wrows, n_mp * half)
    g_send, w_block = lax.optimization_barrier((g_send, w_block))
    g_all = lax.all_to_all(g_send, "mp", 0, 0, tiled=True)
    w_z = lax.all_gather(w_block, "z", axis=0, tiled=True)
    w_z_other = swap_core(w_z)
    g_all = g_all.reshape(n_mp * half, tokens)
    x_pair = compact(xs, x_other).reshape(tokens, feats)

    w_cores = jnp.where(core == 0, jnp.stack([w_z, w_z_other]), jnp.stack([w_z_other, w_z]))
    w_full = w_cores.reshape(2, n_z, 2, wrows, n_mp * half).transpose(2, 1, 0, 3, 4)
    w_full = w_full.reshape(4 * n_z * wrows, n_mp * half)[:feats]

    dw = lax.dot_general(x_pair, g_all, (((0,), (1,)), ((), ())), preferred_element_type=F32)
    dw = jnp.pad(dw, ((0, 4 * n_z * wrows - feats), (0, 0)))
    dw = dw.reshape(2, n_z, 2, wrows, n_mp * half).transpose(2, 1, 0, 3, 4)
    dw_mine = jnp.where(core == 0, dw[0], dw[1])
    dw_theirs = jnp.where(core == 0, dw[1], dw[0]).astype(BF16)
    dw_sum = dw_mine + swap_core(dw_theirs).astype(F32)
    dw_z = dw_sum.astype(BF16).reshape(n_z, 2 * wrows, n_mp * half)
    dw_z = lax.all_to_all(dw_z, "z", 0, 0, tiled=True)
    dw_rows = jnp.sum(dw_z.astype(F32), axis=0).reshape(2, wrows, n_mp * half)
    dw_own = jnp.where(side == 0, dw_rows[0], dw_rows[1])
    dw_send = jnp.where(side == 0, dw_rows[1], dw_rows[0])
    dw_other = swap_pair(dw_send)
    dw_own = dw_own.reshape(wrows, n_mp, 1, half)
    dw_other = dw_other.reshape(wrows, n_mp, 1, half)
    weight_grad = jnp.where(
        side == 0,
        jnp.concatenate([dw_own, dw_other], axis=2),
        jnp.concatenate([dw_other, dw_own], axis=2),
    ).reshape(wrows, cols)

    kv = lax.dot_general(w_full, x_pair, (((0,), (1,)), ((), ())), preferred_element_type=F32)
    kv = lax.all_to_all(kv.astype(BF16).reshape(n_mp, half, tokens), "mp", 0, 0, tiled=True)
    kv = jnp.sum(kv.astype(F32), axis=0).astype(BF16)
    kv_other = swap_pair(kv)
    kv_cols = jnp.where(side == 0, jnp.concatenate([kv, kv_other]), jnp.concatenate([kv_other, kv]))
    kv_home = home(kv_cols.reshape(own_cols, seqs, span).transpose(1, 0, 2))
    kv_values = kv_home.transpose(0, 2, 1).reshape(tokens, own_cols)

    dx = lax.dot_general(g_all, w_full, (((0,), (1,)), ((), ())), preferred_element_type=F32)
    dx_other = swap_pair(dx.astype(BF16))
    dx = (dx + dx_other.astype(F32)).astype(BF16)
    activation_grad = home(dx.reshape(seqs, span, feats)).reshape(tokens, feats)
    return kv_values, activation_grad, weight_grad


def solution(mesh):
    n_dp, n_mp = mesh.devices.shape
    names = ("pair", "z", "core", "mp")
    split = Mesh(mesh.devices.reshape(2, n_dp // 4, 2, n_mp), names)
    dp = ("pair", "z", "core")
    return jax.shard_map(
        on_device,
        mesh=split,
        in_specs=(P(dp, "mp"), P((*dp, "mp"), None), P(dp, "mp"), P(dp)),
        out_specs=(P(dp, "mp"), P(dp, "mp"), P((*dp, "mp"), None)),
        check_vma=False,
    )
```

```python
import jax
import jax.numpy as jnp
from jax import lax
from jax.sharding import Mesh, PartitionSpec as P

BF16 = jnp.bfloat16
F32 = jnp.float32
SWAP = [(0, 1), (1, 0)]


def swap_pair(value):
    return lax.ppermute(value, "pair", SWAP)


def swap_core(value):
    return lax.ppermute(value, "core", SWAP)


def on_device(x, w, adjoint, mask):
    seqs = mask.shape[0]
    tokens, feats = x.shape
    span = tokens // seqs
    wrows, cols = w.shape
    n_z = lax.axis_size("z")
    n_mp = lax.axis_size("mp")
    own_cols = cols // n_mp
    half = own_cols // 2
    side = lax.axis_index("pair")
    core = lax.axis_index("core")

    alive = mask != 0
    count = jnp.sum(mask)
    first_count = jnp.where(side == 0, count, 2 - count)
    skip_first = jnp.logical_not(alive[0])

    def survivor_first(value):
        return jnp.where(skip_first, value[::-1], value)

    def compact(own, other):
        a0 = jnp.where(side == 0, own[0], other[0])
        a1 = jnp.where(side == 0, own[1], other[1])
        b0 = jnp.where(side == 0, other[0], own[0])
        b1 = jnp.where(side == 0, other[1], own[1])
        slot0 = jnp.where(first_count >= 1, a0, b0)
        slot1 = jnp.where(first_count == 2, a1, jnp.where(first_count == 1, b0, b1))
        return jnp.stack([slot0, slot1])

    start = jnp.where(side == 0, 0, 2 - count)

    def home(slots):
        second = start + mask[0]
        rows0 = jnp.where(start == 0, slots[0], slots[1])
        rows1 = jnp.where(second == 0, slots[0], slots[1])
        zero = jnp.zeros_like(rows0)
        return jnp.stack([jnp.where(alive[0], rows0, zero), jnp.where(alive[1], rows1, zero)])

    def pack(value):
        lead = value.shape[:-2]
        value = value.reshape(*lead, wrows, 2, n_mp * half // 2)
        return jnp.swapaxes(value, -3, -2).reshape(*lead, 2 * wrows, n_mp * half // 2)

    def unpack(value):
        lead = value.shape[:-2]
        value = value.reshape(*lead, 2, wrows, n_mp * half // 2)
        return jnp.swapaxes(value, -3, -2).reshape(*lead, wrows, n_mp * half)

    w_halves = w.reshape(wrows, n_mp, 2, half).transpose(2, 0, 1, 3).reshape(2, 1, wrows, n_mp * half)
    w_send = pack(w_halves)
    w_send = jnp.broadcast_to(w_send, (2, n_z) + w_send.shape[2:])
    w_mine = lax.all_to_all(
        w_send.reshape(2 * n_z, 2 * wrows, n_mp * half // 2), ("pair", "z"), 0, 0, tiled=True
    )

    g = survivor_first(adjoint.T.reshape(2, half, seqs, span).transpose(2, 0, 1, 3))
    g_mine = jnp.where(side == 0, g[:, 0], g[:, 1])
    g_theirs = jnp.where(side == 0, g[:, 1], g[:, 0])
    xs = survivor_first(x.reshape(seqs, span, feats))
    g_other = swap_pair(g_theirs)
    x_other = swap_pair(xs)
    g_pair = compact(g_mine, g_other)
    g_cols = g_pair.transpose(1, 0, 2).reshape(1, half, tokens)
    x_pair = compact(xs, x_other).reshape(tokens, feats)

    w_theirs = swap_core(w_mine)
    w_cores = jnp.where(core == 0, jnp.stack([w_mine, w_theirs], 1), jnp.stack([w_theirs, w_mine], 1))
    w_full = unpack(w_cores).reshape(4 * n_z * wrows, n_mp * half)[:feats]

    kv = lax.dot_general(w_full, x_pair, (((0,), (1,)), ((), ())), preferred_element_type=F32)
    kv = kv.astype(BF16).reshape(n_mp, half, tokens)
    both = jnp.concatenate([kv, jnp.broadcast_to(g_cols, (n_mp, half, tokens))], axis=1)
    both = lax.all_to_all(both, "mp", 0, 0, tiled=True)
    g_all = both[:, half:].reshape(n_mp * half, tokens)

    dw = lax.dot_general(x_pair, g_all, (((0,), (1,)), ((), ())), preferred_element_type=F32)
    dw = jnp.pad(dw, ((0, 4 * n_z * wrows - feats), (0, 0)))
    dw = dw.reshape(2 * n_z, 2, wrows, n_mp * half)
    dw_mine = pack(jnp.where(core == 0, dw[:, 0], dw[:, 1]))
    dw_theirs = pack(jnp.where(core == 0, dw[:, 1], dw[:, 0]).astype(BF16))
    dw_sum = dw_mine + swap_core(dw_theirs).astype(F32)
    dw_parts = lax.all_to_all(dw_sum.astype(BF16), ("pair", "z"), 0, 0, tiled=True)
    dw_parts = dw_parts.reshape(2, n_z, 2 * wrows, n_mp * half // 2)
    dw_rows = unpack(jnp.sum(dw_parts.astype(F32), axis=1)).reshape(2, wrows, n_mp, half)
    weight_grad = dw_rows.transpose(1, 2, 0, 3).reshape(wrows, cols)

    kv = jnp.sum(both[:, :half].astype(F32), axis=0).astype(BF16)
    kv_other = swap_pair(kv)
    kv_cols = jnp.where(side == 0, jnp.concatenate([kv, kv_other]), jnp.concatenate([kv_other, kv]))
    kv_home = home(kv_cols.reshape(own_cols, seqs, span).transpose(1, 0, 2))
    kv_values = kv_home.transpose(0, 2, 1).reshape(tokens, own_cols)

    dx = lax.dot_general(g_all, w_full, (((0,), (1,)), ((), ())), preferred_element_type=F32)
    dx_other = swap_pair(dx.astype(BF16))
    dx = (dx + dx_other.astype(F32)).astype(BF16)
    activation_grad = home(dx.reshape(seqs, span, feats)).reshape(tokens, feats)
    return kv_values, activation_grad, weight_grad


def solution(mesh):
    n_dp, n_mp = mesh.devices.shape
    names = ("pair", "z", "core", "mp")
    split = Mesh(mesh.devices.reshape(2, n_dp // 4, 2, n_mp), names)
    dp = ("pair", "z", "core")
    return jax.shard_map(
        on_device,
        mesh=split,
        in_specs=(P(dp, "mp"), P((*dp, "mp"), None), P(dp, "mp"), P(dp)),
        out_specs=(P(dp, "mp"), P(dp, "mp"), P((*dp, "mp"), None)),
        check_vma=False,
    )
```

```python
import jax
import jax.numpy as jnp
from jax import lax
from jax.sharding import Mesh, PartitionSpec as P

BF16 = jnp.bfloat16
F32 = jnp.float32
SWAP = [(0, 1), (1, 0)]


def swap_pair(value):
    return lax.ppermute(value, "pair", SWAP)


def swap_core(value):
    return lax.ppermute(value, "core", SWAP)


def on_device(x, w, adjoint, mask):
    seqs = mask.shape[0]
    tokens, feats = x.shape
    span = tokens // seqs
    wrows, cols = w.shape
    n_z = lax.axis_size("z")
    n_mp = lax.axis_size("mp")
    own_cols = cols // n_mp
    half = own_cols // 2
    side = lax.axis_index("pair")
    core = lax.axis_index("core")

    alive = mask != 0
    count = jnp.sum(mask)
    first_count = jnp.where(side == 0, count, 2 - count)
    skip_first = jnp.logical_not(alive[0])

    def survivor_first(value):
        return jnp.where(skip_first, value[::-1], value)

    def compact(own, other):
        a0 = jnp.where(side == 0, own[0], other[0])
        a1 = jnp.where(side == 0, own[1], other[1])
        b0 = jnp.where(side == 0, other[0], own[0])
        b1 = jnp.where(side == 0, other[1], own[1])
        slot0 = jnp.where(first_count >= 1, a0, b0)
        slot1 = jnp.where(first_count == 2, a1, jnp.where(first_count == 1, b0, b1))
        return jnp.stack([slot0, slot1])

    start = jnp.where(side == 0, 0, 2 - count)

    def home(slots):
        second = start + mask[0]
        rows0 = jnp.where(start == 0, slots[0], slots[1])
        rows1 = jnp.where(second == 0, slots[0], slots[1])
        zero = jnp.zeros_like(rows0)
        return jnp.stack([jnp.where(alive[0], rows0, zero), jnp.where(alive[1], rows1, zero)])

    def pack(value):
        lead = value.shape[:-2]
        value = value.reshape(*lead, wrows, 2, n_mp * half // 2)
        return jnp.swapaxes(value, -3, -2).reshape(*lead, 2 * wrows, n_mp * half // 2)

    def unpack(value):
        lead = value.shape[:-2]
        value = value.reshape(*lead, 2, wrows, n_mp * half // 2)
        return jnp.swapaxes(value, -3, -2).reshape(*lead, wrows, n_mp * half)

    w_halves = w.reshape(wrows, n_mp, 2, half).transpose(2, 0, 1, 3).reshape(2, 1, wrows, n_mp * half)
    w_send = pack(w_halves)
    w_send = jnp.broadcast_to(w_send, (2, n_z) + w_send.shape[2:])
    w_mine = lax.all_to_all(
        w_send.reshape(2 * n_z, 2 * wrows, n_mp * half // 2), ("pair", "z"), 0, 0, tiled=True
    )

    g = survivor_first(adjoint.T.reshape(2, half, seqs, span).transpose(2, 0, 1, 3))
    g_mine = jnp.where(side == 0, g[:, 0], g[:, 1])
    g_theirs = jnp.where(side == 0, g[:, 1], g[:, 0])
    xs = survivor_first(x.reshape(seqs, span, feats))
    g_other = swap_pair(g_theirs)
    x_other = swap_pair(xs)
    g_pair = compact(g_mine, g_other)
    g_cols = g_pair.transpose(1, 0, 2).reshape(1, half, tokens)
    x_pair = compact(xs, x_other).reshape(tokens, feats)

    w_theirs = swap_core(w_mine)
    w_cores = jnp.where(core == 0, jnp.stack([w_mine, w_theirs], 1), jnp.stack([w_theirs, w_mine], 1))
    w_full = unpack(w_cores).reshape(4 * n_z * wrows, n_mp * half)[:feats]

    kv = lax.dot_general(w_full, x_pair, (((0,), (1,)), ((), ())), preferred_element_type=F32)
    kv = kv.astype(BF16).reshape(n_mp, half, tokens)
    both = jnp.concatenate([kv, jnp.broadcast_to(g_cols, (n_mp, half, tokens))], axis=1)
    both = lax.all_to_all(both, "mp", 0, 0, tiled=True)
    g_all = both[:, half:].reshape(n_mp * half, tokens)

    dw = lax.dot_general(x_pair, g_all, (((0,), (1,)), ((), ())), preferred_element_type=F32)
    dw = jnp.pad(dw, ((0, 4 * n_z * wrows - feats), (0, 0)))
    dw = dw.reshape(2 * n_z, 2, wrows, n_mp * half)
    dw_mine = pack(jnp.where(core == 0, dw[:, 0], dw[:, 1]))
    dw_theirs = pack(jnp.where(core == 0, dw[:, 1], dw[:, 0]).astype(BF16))
    dw_sum = dw_mine + swap_core(dw_theirs).astype(F32)
    dw_send, both, g_all, w_full = lax.optimization_barrier((dw_sum.astype(BF16), both, g_all, w_full))
    dw_parts = lax.all_to_all(dw_send, ("pair", "z"), 0, 0, tiled=True)
    dw_parts = dw_parts.reshape(2, n_z, 2 * wrows, n_mp * half // 2)
    dw_rows = unpack(jnp.sum(dw_parts.astype(F32), axis=1)).reshape(2, wrows, n_mp, half)
    weight_grad = dw_rows.transpose(1, 2, 0, 3).reshape(wrows, cols)

    kv = jnp.sum(both[:, :half].astype(F32), axis=0).astype(BF16)
    kv_other = swap_pair(kv)
    kv_cols = jnp.where(side == 0, jnp.concatenate([kv, kv_other]), jnp.concatenate([kv_other, kv]))
    kv_home = home(kv_cols.reshape(own_cols, seqs, span).transpose(1, 0, 2))
    kv_values = kv_home.transpose(0, 2, 1).reshape(tokens, own_cols)

    dx = lax.dot_general(g_all, w_full, (((0,), (1,)), ((), ())), preferred_element_type=F32)
    dx_other = swap_pair(dx.astype(BF16))
    dx = (dx + dx_other.astype(F32)).astype(BF16)
    activation_grad = home(dx.reshape(seqs, span, feats)).reshape(tokens, feats)
    return kv_values, activation_grad, weight_grad


def solution(mesh):
    n_dp, n_mp = mesh.devices.shape
    names = ("pair", "z", "core", "mp")
    split = Mesh(mesh.devices.reshape(2, n_dp // 4, 2, n_mp), names)
    dp = ("pair", "z", "core")
    return jax.shard_map(
        on_device,
        mesh=split,
        in_specs=(P(dp, "mp"), P((*dp, "mp"), None), P(dp, "mp"), P(dp)),
        out_specs=(P(dp, "mp"), P(dp, "mp"), P((*dp, "mp"), None)),
        check_vma=False,
    )
```

```python
import jax
import jax.numpy as jnp
from jax import lax
from jax.sharding import Mesh, PartitionSpec as P

BF16 = jnp.bfloat16
F32 = jnp.float32
SWAP = [(0, 1), (1, 0)]


def swap_pair(value):
    return lax.ppermute(value, "pair", SWAP)


def swap_core(value):
    return lax.ppermute(value, "core", SWAP)


def doubling_rounds(value, n, first, last):
    index = lax.axis_index("mp")
    for axis in range(first, last):
        step = n >> (axis + 1)
        other = lax.ppermute(value, "mp", [(i, i ^ step) for i in range(n)])
        upper = (index & step) != 0
        value = jnp.concatenate(
            [jnp.where(upper, other, value), jnp.where(upper, value, other)], axis=axis
        )
    return value


def on_device(x, w, adjoint, mask):
    seqs = mask.shape[0]
    tokens, feats = x.shape
    span = tokens // seqs
    wrows, cols = w.shape
    n_z = lax.axis_size("z")
    n_mp = lax.axis_size("mp")
    own_cols = cols // n_mp
    half = own_cols // 2
    side = lax.axis_index("pair")
    core = lax.axis_index("core")

    alive = mask != 0
    count = jnp.sum(mask)
    first_count = jnp.where(side == 0, count, 2 - count)
    skip_first = jnp.logical_not(alive[0])

    def survivor_first(value):
        return jnp.where(skip_first, value[::-1], value)

    def compact(own, other):
        a0 = jnp.where(side == 0, own[0], other[0])
        a1 = jnp.where(side == 0, own[1], other[1])
        b0 = jnp.where(side == 0, other[0], own[0])
        b1 = jnp.where(side == 0, other[1], own[1])
        slot0 = jnp.where(first_count >= 1, a0, b0)
        slot1 = jnp.where(first_count == 2, a1, jnp.where(first_count == 1, b0, b1))
        return jnp.stack([slot0, slot1])

    start = jnp.where(side == 0, 0, 2 - count)

    def home(slots):
        second = start + mask[0]
        rows0 = jnp.where(start == 0, slots[0], slots[1])
        rows1 = jnp.where(second == 0, slots[0], slots[1])
        zero = jnp.zeros_like(rows0)
        return jnp.stack([jnp.where(alive[0], rows0, zero), jnp.where(alive[1], rows1, zero)])

    def pack(value):
        lead = value.shape[:-2]
        value = value.reshape(*lead, wrows, 2, n_mp * half // 2)
        return jnp.swapaxes(value, -3, -2).reshape(*lead, 2 * wrows, n_mp * half // 2)

    def unpack(value):
        lead = value.shape[:-2]
        value = value.reshape(*lead, 2, wrows, n_mp * half // 2)
        return jnp.swapaxes(value, -3, -2).reshape(*lead, wrows, n_mp * half)

    w_halves = w.reshape(wrows, n_mp, 2, half).transpose(2, 0, 1, 3).reshape(2, 1, wrows, n_mp * half)
    w_send = pack(w_halves)
    w_send = jnp.broadcast_to(w_send, (2, n_z) + w_send.shape[2:])
    w_mine = lax.all_to_all(
        w_send.reshape(2 * n_z, 2 * wrows, n_mp * half // 2), ("pair", "z"), 0, 0, tiled=True
    )

    g = survivor_first(adjoint.T.reshape(2, half, seqs, span).transpose(2, 0, 1, 3))
    g_mine = jnp.where(side == 0, g[:, 0], g[:, 1])
    g_theirs = jnp.where(side == 0, g[:, 1], g[:, 0])
    xs = survivor_first(x.reshape(seqs, span, feats))
    g_other = swap_pair(g_theirs)
    x_other = swap_pair(xs)
    g_pair = compact(g_mine, g_other)
    g_cols = g_pair.transpose(1, 0, 2).reshape(half, tokens)
    rounds = n_mp.bit_length() - 1
    g_cols = g_cols.reshape((1,) * rounds + g_cols.shape)
    g_near = doubling_rounds(g_cols, n_mp, 0, rounds // 2)
    x_pair = compact(xs, x_other).reshape(tokens, feats)

    w_theirs = swap_core(w_mine)
    w_cores = jnp.where(core == 0, jnp.stack([w_mine, w_theirs], 1), jnp.stack([w_theirs, w_mine], 1))
    w_full = unpack(w_cores).reshape(4 * n_z * wrows, n_mp * half)[:feats]

    kv = lax.dot_general(w_full, x_pair, (((0,), (1,)), ((), ())), preferred_element_type=F32)
    kv, g_near = lax.optimization_barrier((kv.astype(BF16), g_near))
    kv_parts = lax.all_to_all(kv.reshape(n_mp, half, tokens), "mp", 0, 0, tiled=True)
    g_all = doubling_rounds(g_near, n_mp, rounds // 2, rounds).reshape(n_mp * half, tokens)

    dw = lax.dot_general(x_pair, g_all, (((0,), (1,)), ((), ())), preferred_element_type=F32)
    dw = jnp.pad(dw, ((0, 4 * n_z * wrows - feats), (0, 0)))
    dw = dw.reshape(2 * n_z, 2, wrows, n_mp * half)
    dw_mine = pack(jnp.where(core == 0, dw[:, 0], dw[:, 1]))
    dw_theirs = pack(jnp.where(core == 0, dw[:, 1], dw[:, 0]).astype(BF16))
    dw_sum = dw_mine + swap_core(dw_theirs).astype(F32)
    dw_send, kv_parts = lax.optimization_barrier((dw_sum.astype(BF16), kv_parts))
    dw_parts = lax.all_to_all(dw_send, ("pair", "z"), 0, 0, tiled=True)
    dw_parts = dw_parts.reshape(2, n_z, 2 * wrows, n_mp * half // 2)
    dw_rows = unpack(jnp.sum(dw_parts.astype(F32), axis=1)).reshape(2, wrows, n_mp, half)
    weight_grad = dw_rows.transpose(1, 2, 0, 3).reshape(wrows, cols)

    kv = jnp.sum(kv_parts.astype(F32), axis=0).astype(BF16)
    kv_other = swap_pair(kv)
    kv_cols = jnp.where(side == 0, jnp.concatenate([kv, kv_other]), jnp.concatenate([kv_other, kv]))
    kv_home = home(kv_cols.reshape(own_cols, seqs, span).transpose(1, 0, 2))
    kv_values = kv_home.transpose(0, 2, 1).reshape(tokens, own_cols)

    dx = lax.dot_general(g_all, w_full, (((0,), (1,)), ((), ())), preferred_element_type=F32)
    dx_other = swap_pair(dx.astype(BF16))
    dx = (dx + dx_other.astype(F32)).astype(BF16)
    activation_grad = home(dx.reshape(seqs, span, feats)).reshape(tokens, feats)
    return kv_values, activation_grad, weight_grad


def solution(mesh):
    n_dp, n_mp = mesh.devices.shape
    names = ("pair", "z", "core", "mp")
    split = Mesh(mesh.devices.reshape(2, n_dp // 4, 2, n_mp), names)
    dp = ("pair", "z", "core")
    return jax.shard_map(
        on_device,
        mesh=split,
        in_specs=(P(dp, "mp"), P((*dp, "mp"), None), P(dp, "mp"), P(dp)),
        out_specs=(P(dp, "mp"), P(dp, "mp"), P((*dp, "mp"), None)),
        check_vma=False,
    )
```

```python
import functools

import jax
import jax.numpy as jnp
from jax import lax
from jax.experimental import pallas as pl
from jax.experimental.pallas import tpu as pltpu
from jax.sharding import Mesh, PartitionSpec as P

BF16 = jnp.bfloat16
F32 = jnp.float32
SWAP = [(0, 1), (1, 0)]


def swap_pair(value):
    return lax.ppermute(value, "pair", SWAP)


def swap_core(value):
    return lax.ppermute(value, "core", SWAP)


def weight_kernel(blocks, wrows, core_ref, both_ref, x_ref, mine_ref, theirs_ref, acc_ref, stage_ref):
    tokens, feats = x_ref.shape
    n_mp, rows, _ = both_ref.shape
    half = rows // 2
    width = acc_ref.shape[2]
    groups = width // half
    first_core = core_ref[0] == 0
    x_turned = x_ref[...].T
    for part in range(2):
        g = both_ref[part * groups : (part + 1) * groups, half:, :].reshape(width, tokens)
        acc_ref[part, :feats] = lax.dot_general(
            x_turned, g, (((1,), (1,)), ((), ())), preferred_element_type=F32
        )
        acc_ref[part, feats:] = jnp.zeros_like(acc_ref[part, feats:])
    stage_ref[:, 2 * wrows :] = jnp.zeros_like(stage_ref[:, 2 * wrows :])
    for block in range(blocks):
        for part in range(2):
            top = acc_ref[part, pl.ds(2 * block * wrows, wrows)]
            bottom = acc_ref[part, pl.ds((2 * block + 1) * wrows, wrows)]
            mine_ref[block, pl.ds(part * wrows, wrows)] = jnp.where(first_core, top, bottom)
            stage_ref[block, pl.ds(part * wrows, wrows)] = jnp.where(first_core, bottom, top)
        theirs_ref[block] = stage_ref[block, : 2 * wrows].astype(BF16)


def weight_blocks(core, both, x_pair, blocks, wrows):
    tokens, feats = x_pair.shape
    n_mp, rows, _ = both.shape
    width = n_mp * rows // 4
    vmem = pl.BlockSpec(memory_space=pltpu.VMEM)
    padded = -(-2 * wrows // 16) * 16
    shape = (blocks, 2 * wrows, width)
    return pl.pallas_call(
        functools.partial(weight_kernel, blocks, wrows),
        out_shape=(jax.ShapeDtypeStruct(shape, F32), jax.ShapeDtypeStruct(shape, BF16)),
        in_specs=[pl.BlockSpec(memory_space=pltpu.SMEM), vmem, vmem],
        out_specs=(vmem, vmem),
        scratch_shapes=[
            pltpu.VMEM((2, 2 * blocks * wrows, width), F32),
            pltpu.VMEM((blocks, padded, width), F32),
        ],
        compiler_params=pltpu.CompilerParams(vmem_limit_bytes=32 * 2**20),
        cost_estimate=pl.CostEstimate(
            flops=2 * feats * tokens * 2 * width, bytes_accessed=3 * 2**20, transcendentals=0
        ),
    )(core.reshape(1), both, x_pair)


def on_device(x, w, adjoint, mask):
    seqs = mask.shape[0]
    tokens, feats = x.shape
    span = tokens // seqs
    wrows, cols = w.shape
    n_z = lax.axis_size("z")
    n_mp = lax.axis_size("mp")
    own_cols = cols // n_mp
    half = own_cols // 2
    side = lax.axis_index("pair")
    core = lax.axis_index("core")

    alive = mask != 0
    count = jnp.sum(mask)
    first_count = jnp.where(side == 0, count, 2 - count)
    skip_first = jnp.logical_not(alive[0])

    def survivor_first(value):
        return jnp.where(skip_first, value[::-1], value)

    def compact(own, other):
        a0 = jnp.where(side == 0, own[0], other[0])
        a1 = jnp.where(side == 0, own[1], other[1])
        b0 = jnp.where(side == 0, other[0], own[0])
        b1 = jnp.where(side == 0, other[1], own[1])
        slot0 = jnp.where(first_count >= 1, a0, b0)
        slot1 = jnp.where(first_count == 2, a1, jnp.where(first_count == 1, b0, b1))
        return jnp.stack([slot0, slot1])

    start = jnp.where(side == 0, 0, 2 - count)

    def home(slots):
        second = start + mask[0]
        rows0 = jnp.where(start == 0, slots[0], slots[1])
        rows1 = jnp.where(second == 0, slots[0], slots[1])
        zero = jnp.zeros_like(rows0)
        return jnp.stack([jnp.where(alive[0], rows0, zero), jnp.where(alive[1], rows1, zero)])

    def pack(value):
        lead = value.shape[:-2]
        value = value.reshape(*lead, wrows, 2, n_mp * half // 2)
        return jnp.swapaxes(value, -3, -2).reshape(*lead, 2 * wrows, n_mp * half // 2)

    def unpack(value):
        lead = value.shape[:-2]
        value = value.reshape(*lead, 2, wrows, n_mp * half // 2)
        return jnp.swapaxes(value, -3, -2).reshape(*lead, wrows, n_mp * half)

    w_halves = w.reshape(wrows, n_mp, 2, half).transpose(2, 0, 1, 3).reshape(2, 1, wrows, n_mp * half)
    w_send = pack(w_halves)
    w_send = jnp.broadcast_to(w_send, (2, n_z) + w_send.shape[2:])
    w_mine = lax.all_to_all(
        w_send.reshape(2 * n_z, 2 * wrows, n_mp * half // 2), ("pair", "z"), 0, 0, tiled=True
    )

    g = survivor_first(adjoint.T.reshape(2, half, seqs, span).transpose(2, 0, 1, 3))
    g_mine = jnp.where(side == 0, g[:, 0], g[:, 1])
    g_theirs = jnp.where(side == 0, g[:, 1], g[:, 0])
    xs = survivor_first(x.reshape(seqs, span, feats))
    g_other = swap_pair(g_theirs)
    x_other = swap_pair(xs)
    g_pair = compact(g_mine, g_other)
    g_cols = g_pair.transpose(1, 0, 2).reshape(1, half, tokens)
    x_pair = compact(xs, x_other).reshape(tokens, feats)

    w_theirs = swap_core(w_mine)
    w_cores = jnp.where(core == 0, jnp.stack([w_mine, w_theirs], 1), jnp.stack([w_theirs, w_mine], 1))
    w_full = unpack(w_cores).reshape(4 * n_z * wrows, n_mp * half)[:feats]

    kv = lax.dot_general(w_full, x_pair, (((0,), (1,)), ((), ())), preferred_element_type=F32)
    kv = kv.astype(BF16).reshape(n_mp, half, tokens)
    both = jnp.concatenate([kv, jnp.broadcast_to(g_cols, (n_mp, half, tokens))], axis=1)
    both = lax.all_to_all(both, "mp", 0, 0, tiled=True)
    g_all = both[:, half:].reshape(n_mp * half, tokens)

    dw_mine, dw_theirs = weight_blocks(core, both, x_pair, 2 * n_z, wrows)
    dw_theirs, both = lax.optimization_barrier((dw_theirs, both))
    dw_sum = dw_mine + swap_core(dw_theirs).astype(F32)
    dw_send, g_all, w_full = lax.optimization_barrier((dw_sum.astype(BF16), g_all, w_full))
    dw_parts = lax.all_to_all(dw_send, ("pair", "z"), 0, 0, tiled=True)
    dw_parts = dw_parts.reshape(2, n_z, 2 * wrows, n_mp * half // 2)
    dw_rows = unpack(jnp.sum(dw_parts.astype(F32), axis=1)).reshape(2, wrows, n_mp, half)
    weight_grad = dw_rows.transpose(1, 2, 0, 3).reshape(wrows, cols)

    kv = jnp.sum(both[:, :half].astype(F32), axis=0).astype(BF16)
    kv_other = swap_pair(kv)
    kv_cols = jnp.where(side == 0, jnp.concatenate([kv, kv_other]), jnp.concatenate([kv_other, kv]))
    kv_home = home(kv_cols.reshape(own_cols, seqs, span).transpose(1, 0, 2))
    kv_values = kv_home.transpose(0, 2, 1).reshape(tokens, own_cols)

    dx = lax.dot_general(g_all, w_full, (((0,), (1,)), ((), ())), preferred_element_type=F32)
    dx_other = swap_pair(dx.astype(BF16))
    dx = (dx + dx_other.astype(F32)).astype(BF16)
    activation_grad = home(dx.reshape(seqs, span, feats)).reshape(tokens, feats)
    return kv_values, activation_grad, weight_grad


def solution(mesh):
    n_dp, n_mp = mesh.devices.shape
    names = ("pair", "z", "core", "mp")
    split = Mesh(mesh.devices.reshape(2, n_dp // 4, 2, n_mp), names)
    dp = ("pair", "z", "core")
    return jax.shard_map(
        on_device,
        mesh=split,
        in_specs=(P(dp, "mp"), P((*dp, "mp"), None), P(dp, "mp"), P(dp)),
        out_specs=(P(dp, "mp"), P(dp, "mp"), P((*dp, "mp"), None)),
        check_vma=False,
    )
```

```python
import functools

import jax
import jax.numpy as jnp
from jax import lax
from jax.experimental import pallas as pl
from jax.experimental.pallas import tpu as pltpu
from jax.sharding import Mesh, PartitionSpec as P

BF16 = jnp.bfloat16
F32 = jnp.float32
SWAP = [(0, 1), (1, 0)]


def swap_pair(value):
    return lax.ppermute(value, "pair", SWAP)


def swap_core(value):
    return lax.ppermute(value, "core", SWAP)


def weight_kernel(blocks, wrows, core_ref, both_ref, x_ref, mine_ref, theirs_ref, acc_ref, stage_ref):
    tokens, feats = x_ref.shape
    n_mp, rows, _ = both_ref.shape
    half = rows // 2
    width = acc_ref.shape[2]
    groups = width // half
    first_core = core_ref[0] == 0
    x_turned = x_ref[...].T
    for part in range(2):
        g = both_ref[part * groups : (part + 1) * groups, half:, :].reshape(width, tokens)
        acc_ref[part, :feats] = lax.dot_general(
            x_turned, g, (((1,), (1,)), ((), ())), preferred_element_type=F32
        )
        acc_ref[part, feats:] = jnp.zeros_like(acc_ref[part, feats:])
    stage_ref[:, 2 * wrows :] = jnp.zeros_like(stage_ref[:, 2 * wrows :])
    for block in range(blocks):
        for part in range(2):
            top = acc_ref[part, pl.ds(2 * block * wrows, wrows)]
            bottom = acc_ref[part, pl.ds((2 * block + 1) * wrows, wrows)]
            mine_ref[block, pl.ds(part * wrows, wrows)] = jnp.where(first_core, top, bottom)
            stage_ref[block, pl.ds(part * wrows, wrows)] = jnp.where(first_core, bottom, top)
        theirs_ref[block] = stage_ref[block, : 2 * wrows].astype(BF16)


def weight_blocks(core, both, x_pair, blocks, wrows):
    tokens, feats = x_pair.shape
    n_mp, rows, _ = both.shape
    width = n_mp * rows // 4
    vmem = pl.BlockSpec(memory_space=pltpu.VMEM)
    padded = -(-2 * wrows // 16) * 16
    shape = (blocks, 2 * wrows, width)
    return pl.pallas_call(
        functools.partial(weight_kernel, blocks, wrows),
        out_shape=(jax.ShapeDtypeStruct(shape, F32), jax.ShapeDtypeStruct(shape, BF16)),
        in_specs=[pl.BlockSpec(memory_space=pltpu.SMEM), vmem, vmem],
        out_specs=(vmem, vmem),
        scratch_shapes=[
            pltpu.VMEM((2, 2 * blocks * wrows, width), F32),
            pltpu.VMEM((blocks, padded, width), F32),
        ],
        compiler_params=pltpu.CompilerParams(vmem_limit_bytes=32 * 2**20),
        cost_estimate=pl.CostEstimate(
            flops=2 * feats * tokens * 2 * width, bytes_accessed=3 * 2**20, transcendentals=0
        ),
    )(core.reshape(1), both, x_pair)


def return_kernel(both_ref, w_ref, send_ref, keep_ref, kv_ref):
    n_mp, rows, tokens = both_ref.shape
    feats = w_ref.shape[0]
    half = rows // 2
    g = both_ref[:, half:, :].reshape(n_mp * half, tokens)
    dx = lax.dot_general(g.T, w_ref[...], (((1,), (1,)), ((), ())), preferred_element_type=F32)
    keep_ref[...] = dx
    send_ref[:tokens] = dx.astype(BF16)
    kv = jnp.sum(both_ref[:, :half, :].astype(F32), axis=0).astype(BF16)
    kv_ref[...] = kv
    lanes = feats // tokens
    deep = half // lanes
    for part in range(lanes):
        send_ref[tokens:, part * tokens : (part + 1) * tokens] = kv[part * deep : (part + 1) * deep]


def return_parts(both, w_full):
    n_mp, rows, tokens = both.shape
    feats, width = w_full.shape
    half = rows // 2
    vmem = pl.BlockSpec(memory_space=pltpu.VMEM)
    return pl.pallas_call(
        return_kernel,
        out_shape=(
            jax.ShapeDtypeStruct((tokens + half * tokens // feats, feats), BF16),
            jax.ShapeDtypeStruct((tokens, feats), F32),
            jax.ShapeDtypeStruct((half, tokens), BF16),
        ),
        in_specs=[vmem, vmem],
        out_specs=(vmem, vmem, vmem),
        compiler_params=pltpu.CompilerParams(vmem_limit_bytes=32 * 2**20),
        cost_estimate=pl.CostEstimate(
            flops=2 * feats * tokens * width, bytes_accessed=2 * 2**20, transcendentals=0
        ),
    )(both, w_full)


def home_kernel(seqs, place_ref, keep_ref, recv_ref, kv_ref, dx_ref, out_ref):
    tokens, feats = keep_ref.shape
    half = kv_ref.shape[0]
    span = tokens // seqs
    lanes = feats // tokens
    deep = half // lanes
    left = place_ref[2 * seqs] == 0
    own = kv_ref[...].astype(F32)
    other = jnp.concatenate(
        [
            recv_ref[tokens:, part * tokens : (part + 1) * tokens].astype(F32)
            for part in range(lanes)
        ],
        axis=0,
    )
    low = jnp.where(left, own, other)
    high = jnp.where(left, other, own)
    for seq in range(seqs):
        alive = place_ref[seq] != 0
        slot = place_ref[seqs + seq]
        rows = pl.ds(pl.multiple_of(slot * span, span), span)
        total = keep_ref[rows] + recv_ref[rows].astype(F32)
        here = slice(seq * span, (seq + 1) * span)
        dx_ref[here] = jnp.where(alive, total, 0.0).astype(BF16)
        for at, value in ((0, low), (half, high)):
            picked = jnp.where(slot == 0, value[:, :span], value[:, span : 2 * span])
            out_ref[at : at + half, here] = jnp.where(alive, picked, 0.0).astype(BF16)


def bring_home(place, keep, received, kv, seqs):
    tokens, feats = keep.shape
    half = kv.shape[0]
    vmem = pl.BlockSpec(memory_space=pltpu.VMEM)
    return pl.pallas_call(
        functools.partial(home_kernel, seqs),
        out_shape=(
            jax.ShapeDtypeStruct((tokens, feats), BF16),
            jax.ShapeDtypeStruct((2 * half, tokens), BF16),
        ),
        in_specs=[pl.BlockSpec(memory_space=pltpu.SMEM), vmem, vmem, vmem],
        out_specs=(vmem, vmem),
        compiler_params=pltpu.CompilerParams(vmem_limit_bytes=32 * 2**20),
        cost_estimate=pl.CostEstimate(flops=tokens * feats, bytes_accessed=2**20, transcendentals=0),
    )(place, keep, received, kv)


def on_device(x, w, adjoint, mask):
    seqs = mask.shape[0]
    tokens, feats = x.shape
    span = tokens // seqs
    wrows, cols = w.shape
    n_z = lax.axis_size("z")
    n_mp = lax.axis_size("mp")
    half = cols // n_mp // 2
    side = lax.axis_index("pair")
    core = lax.axis_index("core")

    alive = mask != 0
    count = jnp.sum(mask)
    first_count = jnp.where(side == 0, count, 2 - count)
    skip_first = jnp.logical_not(alive[0])

    def survivor_first(value):
        return jnp.where(skip_first, value[::-1], value)

    def compact(own, other):
        a0 = jnp.where(side == 0, own[0], other[0])
        a1 = jnp.where(side == 0, own[1], other[1])
        b0 = jnp.where(side == 0, other[0], own[0])
        b1 = jnp.where(side == 0, other[1], own[1])
        slot0 = jnp.where(first_count >= 1, a0, b0)
        slot1 = jnp.where(first_count == 2, a1, jnp.where(first_count == 1, b0, b1))
        return jnp.stack([slot0, slot1])

    def pack(value):
        lead = value.shape[:-2]
        value = value.reshape(*lead, wrows, 2, n_mp * half // 2)
        return jnp.swapaxes(value, -3, -2).reshape(*lead, 2 * wrows, n_mp * half // 2)

    def unpack(value):
        lead = value.shape[:-2]
        value = value.reshape(*lead, 2, wrows, n_mp * half // 2)
        return jnp.swapaxes(value, -3, -2).reshape(*lead, wrows, n_mp * half)

    w_halves = w.reshape(wrows, n_mp, 2, half).transpose(2, 0, 1, 3).reshape(2, 1, wrows, n_mp * half)
    w_send = pack(w_halves)
    w_send = jnp.broadcast_to(w_send, (2, n_z) + w_send.shape[2:])
    w_mine = lax.all_to_all(
        w_send.reshape(2 * n_z, 2 * wrows, n_mp * half // 2), ("pair", "z"), 0, 0, tiled=True
    )

    g = survivor_first(adjoint.T.reshape(2, half, seqs, span).transpose(2, 0, 1, 3))
    g_mine = jnp.where(side == 0, g[:, 0], g[:, 1])
    g_theirs = jnp.where(side == 0, g[:, 1], g[:, 0])
    xs = survivor_first(x.reshape(seqs, span, feats))
    g_other = swap_pair(g_theirs)
    x_other = swap_pair(xs)
    g_pair = compact(g_mine, g_other)
    g_cols = g_pair.transpose(1, 0, 2).reshape(1, half, tokens)
    x_pair = compact(xs, x_other).reshape(tokens, feats)

    w_theirs = swap_core(w_mine)
    w_cores = jnp.where(core == 0, jnp.stack([w_mine, w_theirs], 1), jnp.stack([w_theirs, w_mine], 1))
    w_full = unpack(w_cores).reshape(4 * n_z * wrows, n_mp * half)[:feats]

    kv = lax.dot_general(w_full, x_pair, (((0,), (1,)), ((), ())), preferred_element_type=F32)
    kv = kv.astype(BF16).reshape(n_mp, half, tokens)
    both = jnp.concatenate([kv, jnp.broadcast_to(g_cols, (n_mp, half, tokens))], axis=1)
    both = lax.all_to_all(both, "mp", 0, 0, tiled=True)

    dw_mine, dw_theirs = weight_blocks(core, both, x_pair, 2 * n_z, wrows)
    dw_theirs, both = lax.optimization_barrier((dw_theirs, both))
    dw_sum = dw_mine + swap_core(dw_theirs).astype(F32)

    send, keep, kv = return_parts(both, w_full)
    received = swap_pair(send)
    dw_send, keep = lax.optimization_barrier((dw_sum.astype(BF16), keep))
    dw_parts = lax.all_to_all(dw_send, ("pair", "z"), 0, 0, tiled=True)
    dw_parts = dw_parts.reshape(2, n_z, 2 * wrows, n_mp * half // 2)
    dw_rows = unpack(jnp.sum(dw_parts.astype(F32), axis=1)).reshape(2, wrows, n_mp, half)
    weight_grad = dw_rows.transpose(1, 2, 0, 3).reshape(wrows, cols)

    start = jnp.where(side == 0, 0, 2 - count)
    slots = jnp.minimum(jnp.stack([start, start + mask[0]]), 1)
    place = jnp.concatenate([mask, slots, side.reshape(1)])
    activation_grad, kv_home = bring_home(place, keep, received, kv, seqs)
    return kv_home.T, activation_grad, weight_grad


def solution(mesh):
    n_dp, n_mp = mesh.devices.shape
    names = ("pair", "z", "core", "mp")
    split = Mesh(mesh.devices.reshape(2, n_dp // 4, 2, n_mp), names)
    dp = ("pair", "z", "core")
    return jax.shard_map(
        on_device,
        mesh=split,
        in_specs=(P(dp, "mp"), P((*dp, "mp"), None), P(dp, "mp"), P(dp)),
        out_specs=(P(dp, "mp"), P(dp, "mp"), P((*dp, "mp"), None)),
        check_vma=False,
    )
```

```python
import functools

import jax
import jax.numpy as jnp
from jax import lax
from jax.experimental import pallas as pl
from jax.experimental.pallas import tpu as pltpu
from jax.sharding import Mesh, PartitionSpec as P

BF16 = jnp.bfloat16
F32 = jnp.float32
SWAP = [(0, 1), (1, 0)]


def swap_pair(value):
    return lax.ppermute(value, "pair", SWAP)


def swap_core(value):
    return lax.ppermute(value, "core", SWAP)


def weight_kernel(blocks, wrows, core_ref, both_ref, x_ref, mine_ref, theirs_ref, acc_ref, stage_ref):
    tokens, feats = x_ref.shape
    n_mp, rows, _ = both_ref.shape
    half = rows // 2
    width = acc_ref.shape[2]
    groups = width // half
    first_core = core_ref[0] == 0
    x_turned = x_ref[...].T
    for part in range(2):
        g = both_ref[part * groups : (part + 1) * groups, half:, :].reshape(width, tokens)
        acc_ref[part, :feats] = lax.dot_general(
            x_turned, g, (((1,), (1,)), ((), ())), preferred_element_type=F32
        )
        acc_ref[part, feats:] = jnp.zeros_like(acc_ref[part, feats:])
    stage_ref[:, 2 * wrows :] = jnp.zeros_like(stage_ref[:, 2 * wrows :])
    for block in range(blocks):
        for part in range(2):
            top = acc_ref[part, pl.ds(2 * block * wrows, wrows)]
            bottom = acc_ref[part, pl.ds((2 * block + 1) * wrows, wrows)]
            mine_ref[block, pl.ds(part * wrows, wrows)] = jnp.where(first_core, top, bottom)
            stage_ref[block, pl.ds(part * wrows, wrows)] = jnp.where(first_core, bottom, top)
        theirs_ref[block] = stage_ref[block, : 2 * wrows].astype(BF16)


def weight_blocks(core, both, x_pair, blocks, wrows):
    tokens, feats = x_pair.shape
    n_mp, rows, _ = both.shape
    width = n_mp * rows // 4
    vmem = pl.BlockSpec(memory_space=pltpu.VMEM)
    padded = -(-2 * wrows // 16) * 16
    shape = (blocks, 2 * wrows, width)
    return pl.pallas_call(
        functools.partial(weight_kernel, blocks, wrows),
        out_shape=(jax.ShapeDtypeStruct(shape, F32), jax.ShapeDtypeStruct(shape, BF16)),
        in_specs=[pl.BlockSpec(memory_space=pltpu.SMEM), vmem, vmem],
        out_specs=(vmem, vmem),
        scratch_shapes=[
            pltpu.VMEM((2, 2 * blocks * wrows, width), F32),
            pltpu.VMEM((blocks, padded, width), F32),
        ],
        compiler_params=pltpu.CompilerParams(vmem_limit_bytes=32 * 2**20),
        cost_estimate=pl.CostEstimate(
            flops=2 * feats * tokens * 2 * width, bytes_accessed=3 * 2**20, transcendentals=0
        ),
    )(core.reshape(1), both, x_pair)


def return_kernel(both_ref, w_ref, send_ref, keep_ref, kv_ref):
    n_mp, rows, tokens = both_ref.shape
    feats = w_ref.shape[0]
    half = rows // 2
    g = both_ref[:, half:, :].reshape(n_mp * half, tokens)
    dx = lax.dot_general(g.T, w_ref[...], (((1,), (1,)), ((), ())), preferred_element_type=F32)
    keep_ref[...] = dx
    send_ref[:tokens] = dx.astype(BF16)
    kv = jnp.sum(both_ref[:, :half, :].astype(F32), axis=0).astype(BF16)
    kv_ref[...] = kv
    lanes = feats // tokens
    deep = half // lanes
    for part in range(lanes):
        send_ref[tokens:, part * tokens : (part + 1) * tokens] = kv[part * deep : (part + 1) * deep]


def return_parts(both, w_full):
    n_mp, rows, tokens = both.shape
    feats, width = w_full.shape
    half = rows // 2
    vmem = pl.BlockSpec(memory_space=pltpu.VMEM)
    return pl.pallas_call(
        return_kernel,
        out_shape=(
            jax.ShapeDtypeStruct((tokens + half * tokens // feats, feats), BF16),
            jax.ShapeDtypeStruct((tokens, feats), F32),
            jax.ShapeDtypeStruct((half, tokens), BF16),
        ),
        in_specs=[vmem, vmem],
        out_specs=(vmem, vmem, vmem),
        compiler_params=pltpu.CompilerParams(vmem_limit_bytes=32 * 2**20),
        cost_estimate=pl.CostEstimate(
            flops=2 * feats * tokens * width, bytes_accessed=2 * 2**20, transcendentals=0
        ),
    )(both, w_full)


def home_kernel(seqs, place_ref, keep_ref, recv_ref, kv_ref, dx_ref, out_ref):
    tokens, feats = keep_ref.shape
    half = kv_ref.shape[0]
    span = tokens // seqs
    lanes = feats // tokens
    deep = half // lanes
    left = place_ref[2 * seqs] == 0
    own = kv_ref[...].astype(F32)
    other = jnp.concatenate(
        [
            recv_ref[tokens:, part * tokens : (part + 1) * tokens].astype(F32)
            for part in range(lanes)
        ],
        axis=0,
    )
    low = jnp.where(left, own, other)
    high = jnp.where(left, other, own)
    for seq in range(seqs):
        alive = place_ref[seq] != 0
        slot = place_ref[seqs + seq]
        rows = pl.ds(pl.multiple_of(slot * span, span), span)
        total = keep_ref[rows] + recv_ref[rows].astype(F32)
        here = slice(seq * span, (seq + 1) * span)
        dx_ref[here] = jnp.where(alive, total, 0.0).astype(BF16)
        for at, value in ((0, low), (half, high)):
            picked = jnp.where(slot == 0, value[:, :span], value[:, span : 2 * span])
            out_ref[at : at + half, here] = jnp.where(alive, picked, 0.0).astype(BF16)


def bring_home(place, keep, received, kv, seqs):
    tokens, feats = keep.shape
    half = kv.shape[0]
    vmem = pl.BlockSpec(memory_space=pltpu.VMEM)
    return pl.pallas_call(
        functools.partial(home_kernel, seqs),
        out_shape=(
            jax.ShapeDtypeStruct((tokens, feats), BF16),
            jax.ShapeDtypeStruct((2 * half, tokens), BF16),
        ),
        in_specs=[pl.BlockSpec(memory_space=pltpu.SMEM), vmem, vmem, vmem],
        out_specs=(vmem, vmem),
        compiler_params=pltpu.CompilerParams(vmem_limit_bytes=32 * 2**20),
        cost_estimate=pl.CostEstimate(flops=tokens * feats, bytes_accessed=2**20, transcendentals=0),
    )(place, keep, received, kv)


def halves_matrix(size, half, transposed):
    here = lax.broadcasted_iota(jnp.int32, (size, size), 1 if transposed else 0)
    there = lax.broadcasted_iota(jnp.int32, (size, size), 0 if transposed else 1)
    rest = there % (size // 2)
    source = (rest // half) * (2 * half) + (there // (size // 2)) * half + rest % half
    return (here == source).astype(F32).astype(BF16)


def spread_kernel(half, n_z, w_ref, out_ref, stage_ref):
    wrows, cols = w_ref.shape
    width = cols // 4
    size = min(256, 2 * width)
    matrix = halves_matrix(size, half, False)
    stage_ref[:, 2 * wrows :] = jnp.zeros_like(stage_ref[:, 2 * wrows :])
    for part in range(2):
        for group in range(2 * width // size):
            at = part * 2 * width + group * size
            split = jnp.dot(w_ref[:, at : at + size], matrix, preferred_element_type=F32)
            lanes = slice(group * size // 2, (group + 1) * size // 2)
            for side in range(2):
                stage_ref[side, pl.ds(part * wrows, wrows), lanes] = split[
                    :, side * size // 2 : (side + 1) * size // 2
                ]
    for side in range(2):
        block = stage_ref[side, : 2 * wrows].astype(BF16)
        for z in range(n_z):
            out_ref[side * n_z + z] = block


def spread_weight(w, half, n_z):
    wrows, cols = w.shape
    vmem = pl.BlockSpec(memory_space=pltpu.VMEM)
    padded = -(-2 * wrows // 16) * 16
    return pl.pallas_call(
        functools.partial(spread_kernel, half, n_z),
        out_shape=jax.ShapeDtypeStruct((2 * n_z, 2 * wrows, cols // 4), BF16),
        in_specs=[vmem],
        out_specs=vmem,
        scratch_shapes=[pltpu.VMEM((2, padded, cols // 4), F32)],
        compiler_params=pltpu.CompilerParams(vmem_limit_bytes=32 * 2**20),
        cost_estimate=pl.CostEstimate(
            flops=2 * wrows * cols * 256, bytes_accessed=2**19, transcendentals=0
        ),
    )(w)


def sum_kernel(half, parts_ref, out_ref, stage_ref):
    blocks = parts_ref.shape[0]
    wrows, cols = out_ref.shape
    width = cols // 4
    size = min(256, 2 * width)
    matrix = halves_matrix(size, half, True)
    for side in range(2):
        first = side * blocks // 2
        total = parts_ref[first].astype(F32)
        for block in range(first + 1, first + blocks // 2):
            total = total + parts_ref[block].astype(F32)
        stage_ref[side, pl.ds(0, 2 * wrows)] = total
    for part in range(2):
        for group in range(2 * width // size):
            lanes = slice(group * size // 2, (group + 1) * size // 2)
            both = jnp.concatenate(
                [stage_ref[side, pl.ds(part * wrows, wrows), lanes] for side in range(2)], axis=1
            )
            top = both.astype(BF16)
            rest = both - top.astype(F32)
            middle = rest.astype(BF16)
            bottom = (rest - middle.astype(F32)).astype(BF16)
            value = jnp.dot(top, matrix, preferred_element_type=F32)
            value = value + jnp.dot(middle, matrix, preferred_element_type=F32)
            value = value + jnp.dot(bottom, matrix, preferred_element_type=F32)
            at = part * 2 * width + group * size
            out_ref[:, at : at + size] = value


def sum_blocks(parts, half, wrows):
    width = parts.shape[2]
    vmem = pl.BlockSpec(memory_space=pltpu.VMEM)
    padded = -(-2 * wrows // 16) * 16
    return pl.pallas_call(
        functools.partial(sum_kernel, half),
        out_shape=jax.ShapeDtypeStruct((wrows, 4 * width), F32),
        in_specs=[vmem],
        out_specs=vmem,
        scratch_shapes=[pltpu.VMEM((2, padded, width), F32)],
        compiler_params=pltpu.CompilerParams(vmem_limit_bytes=32 * 2**20),
        cost_estimate=pl.CostEstimate(
            flops=6 * wrows * 4 * width * 256, bytes_accessed=2**19, transcendentals=0
        ),
    )(parts)


def on_device(x, w, adjoint, mask):
    seqs = mask.shape[0]
    tokens, feats = x.shape
    span = tokens // seqs
    wrows, cols = w.shape
    n_z = lax.axis_size("z")
    n_mp = lax.axis_size("mp")
    half = cols // n_mp // 2
    side = lax.axis_index("pair")
    core = lax.axis_index("core")

    alive = mask != 0
    count = jnp.sum(mask)
    first_count = jnp.where(side == 0, count, 2 - count)
    skip_first = jnp.logical_not(alive[0])

    def survivor_first(value):
        return jnp.where(skip_first, value[::-1], value)

    def compact(own, other):
        a0 = jnp.where(side == 0, own[0], other[0])
        a1 = jnp.where(side == 0, own[1], other[1])
        b0 = jnp.where(side == 0, other[0], own[0])
        b1 = jnp.where(side == 0, other[1], own[1])
        slot0 = jnp.where(first_count >= 1, a0, b0)
        slot1 = jnp.where(first_count == 2, a1, jnp.where(first_count == 1, b0, b1))
        return jnp.stack([slot0, slot1])

    def unpack(value):
        lead = value.shape[:-2]
        value = value.reshape(*lead, 2, wrows, n_mp * half // 2)
        return jnp.swapaxes(value, -3, -2).reshape(*lead, wrows, n_mp * half)

    w_mine = lax.all_to_all(spread_weight(w, half, n_z), ("pair", "z"), 0, 0, tiled=True)

    g = survivor_first(adjoint.T.reshape(2, half, seqs, span).transpose(2, 0, 1, 3))
    g_mine = jnp.where(side == 0, g[:, 0], g[:, 1])
    g_theirs = jnp.where(side == 0, g[:, 1], g[:, 0])
    xs = survivor_first(x.reshape(seqs, span, feats))
    g_other = swap_pair(g_theirs)
    x_other = swap_pair(xs)
    g_pair = compact(g_mine, g_other)
    g_cols = g_pair.transpose(1, 0, 2).reshape(1, half, tokens)
    x_pair = compact(xs, x_other).reshape(tokens, feats)

    w_theirs = swap_core(w_mine)
    w_cores = jnp.where(core == 0, jnp.stack([w_mine, w_theirs], 1), jnp.stack([w_theirs, w_mine], 1))
    w_full = unpack(w_cores).reshape(4 * n_z * wrows, n_mp * half)[:feats]

    kv = lax.dot_general(w_full, x_pair, (((0,), (1,)), ((), ())), preferred_element_type=F32)
    kv = kv.astype(BF16).reshape(n_mp, half, tokens)
    both = jnp.concatenate([kv, jnp.broadcast_to(g_cols, (n_mp, half, tokens))], axis=1)
    both = lax.all_to_all(both, "mp", 0, 0, tiled=True)

    dw_mine, dw_theirs = weight_blocks(core, both, x_pair, 2 * n_z, wrows)
    dw_theirs, both = lax.optimization_barrier((dw_theirs, both))
    dw_sum = dw_mine + swap_core(dw_theirs).astype(F32)

    send, keep, kv = return_parts(both, w_full)
    received = swap_pair(send)
    dw_send, keep = lax.optimization_barrier((dw_sum.astype(BF16), keep))
    dw_parts = lax.all_to_all(dw_send, ("pair", "z"), 0, 0, tiled=True)
    weight_grad = sum_blocks(dw_parts, half, wrows)

    start = jnp.where(side == 0, 0, 2 - count)
    slots = jnp.minimum(jnp.stack([start, start + mask[0]]), 1)
    place = jnp.concatenate([mask, slots, side.reshape(1)])
    activation_grad, kv_home = bring_home(place, keep, received, kv, seqs)
    return kv_home.T, activation_grad, weight_grad


def solution(mesh):
    n_dp, n_mp = mesh.devices.shape
    names = ("pair", "z", "core", "mp")
    split = Mesh(mesh.devices.reshape(2, n_dp // 4, 2, n_mp), names)
    dp = ("pair", "z", "core")
    return jax.shard_map(
        on_device,
        mesh=split,
        in_specs=(P(dp, "mp"), P((*dp, "mp"), None), P(dp, "mp"), P(dp)),
        out_specs=(P(dp, "mp"), P(dp, "mp"), P((*dp, "mp"), None)),
        check_vma=False,
    )
```

```python
import functools

import jax
import jax.numpy as jnp
from jax import lax
from jax.experimental import pallas as pl
from jax.experimental.pallas import tpu as pltpu
from jax.sharding import Mesh, PartitionSpec as P

BF16 = jnp.bfloat16
F32 = jnp.float32
SWAP = [(0, 1), (1, 0)]
HALF = 32


def swap_pair(value):
    return lax.ppermute(value, "pair", SWAP)


def swap_core(value):
    return lax.ppermute(value, "core", SWAP)


def ordered(both_ref):
    n_x, rows, _ = both_ref.shape
    half = rows // 2
    n_y = half // HALF
    return jnp.concatenate(
        [
            both_ref[ix, half + iy * HALF : half + (iy + 1) * HALF]
            for iy in range(n_y)
            for ix in range(n_x)
        ],
        axis=0,
    )


def weight_kernel(blocks, wrows, core_ref, both_ref, x_ref, mine_ref, theirs_ref, acc_ref, stage_ref):
    tokens, feats = x_ref.shape
    width = acc_ref.shape[2]
    first_core = core_ref[0] == 0
    x_turned = x_ref[...].T
    g_all = ordered(both_ref)
    for part in range(2):
        g = g_all[part * width : (part + 1) * width]
        acc_ref[part, :feats] = lax.dot_general(
            x_turned, g, (((1,), (1,)), ((), ())), preferred_element_type=F32
        )
        acc_ref[part, feats:] = jnp.zeros_like(acc_ref[part, feats:])
    stage_ref[:, 2 * wrows :] = jnp.zeros_like(stage_ref[:, 2 * wrows :])
    for block in range(blocks):
        for part in range(2):
            top = acc_ref[part, pl.ds(2 * block * wrows, wrows)]
            bottom = acc_ref[part, pl.ds((2 * block + 1) * wrows, wrows)]
            mine_ref[block, pl.ds(part * wrows, wrows)] = jnp.where(first_core, top, bottom)
            stage_ref[block, pl.ds(part * wrows, wrows)] = jnp.where(first_core, bottom, top)
        theirs_ref[block] = stage_ref[block, : 2 * wrows].astype(BF16)


def weight_blocks(core, both, x_pair, blocks, wrows):
    tokens, feats = x_pair.shape
    width = both.shape[0] * both.shape[1] // 4
    vmem = pl.BlockSpec(memory_space=pltpu.VMEM)
    padded = -(-2 * wrows // 16) * 16
    shape = (blocks, 2 * wrows, width)
    return pl.pallas_call(
        functools.partial(weight_kernel, blocks, wrows),
        out_shape=(jax.ShapeDtypeStruct(shape, F32), jax.ShapeDtypeStruct(shape, BF16)),
        in_specs=[pl.BlockSpec(memory_space=pltpu.SMEM), vmem, vmem],
        out_specs=(vmem, vmem),
        scratch_shapes=[
            pltpu.VMEM((2, 2 * blocks * wrows, width), F32),
            pltpu.VMEM((blocks, padded, width), F32),
        ],
        compiler_params=pltpu.CompilerParams(vmem_limit_bytes=32 * 2**20),
        cost_estimate=pl.CostEstimate(
            flops=2 * feats * tokens * 2 * width, bytes_accessed=3 * 2**20, transcendentals=0
        ),
    )(core.reshape(1), both, x_pair)


def return_kernel(both_ref, w_ref, send_ref, keep_ref):
    g = ordered(both_ref)
    dx = lax.dot_general(g.T, w_ref[...], (((1,), (1,)), ((), ())), preferred_element_type=F32)
    keep_ref[...] = dx
    send_ref[...] = dx.astype(BF16)


def return_parts(both, w_full):
    tokens = both.shape[2]
    feats, width = w_full.shape
    vmem = pl.BlockSpec(memory_space=pltpu.VMEM)
    return pl.pallas_call(
        return_kernel,
        out_shape=(
            jax.ShapeDtypeStruct((tokens, feats), BF16),
            jax.ShapeDtypeStruct((tokens, feats), F32),
        ),
        in_specs=[vmem, vmem],
        out_specs=(vmem, vmem),
        compiler_params=pltpu.CompilerParams(vmem_limit_bytes=32 * 2**20),
        cost_estimate=pl.CostEstimate(
            flops=2 * feats * tokens * width, bytes_accessed=2 * 2**20, transcendentals=0
        ),
    )(both, w_full)


def home_kernel(seqs, place_ref, keep_ref, recv_ref, kv_ref, other_ref, dx_ref, out_ref):
    tokens, feats = keep_ref.shape
    half = kv_ref.shape[0]
    span = tokens // seqs
    left = place_ref[2 * seqs] == 0
    own = kv_ref[...].astype(F32)
    other = other_ref[...].astype(F32)
    low = jnp.where(left, own, other)
    high = jnp.where(left, other, own)
    for seq in range(seqs):
        alive = place_ref[seq] != 0
        slot = place_ref[seqs + seq]
        rows = pl.ds(pl.multiple_of(slot * span, span), span)
        total = keep_ref[rows] + recv_ref[rows].astype(F32)
        here = slice(seq * span, (seq + 1) * span)
        dx_ref[here] = jnp.where(alive, total, 0.0).astype(BF16)
        for at, value in ((0, low), (half, high)):
            picked = jnp.where(slot == 0, value[:, :span], value[:, span : 2 * span])
            out_ref[at : at + half, here] = jnp.where(alive, picked, 0.0).astype(BF16)


def bring_home(place, keep, received, kv, kv_other, seqs):
    tokens, feats = keep.shape
    half = kv.shape[0]
    vmem = pl.BlockSpec(memory_space=pltpu.VMEM)
    return pl.pallas_call(
        functools.partial(home_kernel, seqs),
        out_shape=(
            jax.ShapeDtypeStruct((tokens, feats), BF16),
            jax.ShapeDtypeStruct((2 * half, tokens), BF16),
        ),
        in_specs=[pl.BlockSpec(memory_space=pltpu.SMEM), vmem, vmem, vmem, vmem],
        out_specs=(vmem, vmem),
        compiler_params=pltpu.CompilerParams(vmem_limit_bytes=32 * 2**20),
        cost_estimate=pl.CostEstimate(flops=tokens * feats, bytes_accessed=2**20, transcendentals=0),
    )(place, keep, received, kv, kv_other)


def halves_matrix(size, half, transposed):
    here = lax.broadcasted_iota(jnp.int32, (size, size), 1 if transposed else 0)
    there = lax.broadcasted_iota(jnp.int32, (size, size), 0 if transposed else 1)
    rest = there % (size // 2)
    source = (rest // half) * (2 * half) + (there // (size // 2)) * half + rest % half
    return (here == source).astype(F32).astype(BF16)


def spread_kernel(half, n_z, w_ref, out_ref, stage_ref):
    wrows, cols = w_ref.shape
    width = cols // 4
    size = min(256, 2 * width)
    matrix = halves_matrix(size, half, False)
    stage_ref[:, 2 * wrows :] = jnp.zeros_like(stage_ref[:, 2 * wrows :])
    for part in range(2):
        for group in range(2 * width // size):
            at = part * 2 * width + group * size
            split = jnp.dot(w_ref[:, at : at + size], matrix, preferred_element_type=F32)
            lanes = slice(group * size // 2, (group + 1) * size // 2)
            for side in range(2):
                stage_ref[side, pl.ds(part * wrows, wrows), lanes] = split[
                    :, side * size // 2 : (side + 1) * size // 2
                ]
    for side in range(2):
        block = stage_ref[side, : 2 * wrows].astype(BF16)
        for z in range(n_z):
            out_ref[side * n_z + z] = block


def spread_weight(w, half, n_z):
    wrows, cols = w.shape
    vmem = pl.BlockSpec(memory_space=pltpu.VMEM)
    padded = -(-2 * wrows // 16) * 16
    return pl.pallas_call(
        functools.partial(spread_kernel, half, n_z),
        out_shape=jax.ShapeDtypeStruct((2 * n_z, 2 * wrows, cols // 4), BF16),
        in_specs=[vmem],
        out_specs=vmem,
        scratch_shapes=[pltpu.VMEM((2, padded, cols // 4), F32)],
        compiler_params=pltpu.CompilerParams(vmem_limit_bytes=32 * 2**20),
        cost_estimate=pl.CostEstimate(
            flops=2 * wrows * cols * 256, bytes_accessed=2**19, transcendentals=0
        ),
    )(w)


def sum_kernel(half, parts_ref, out_ref, stage_ref):
    blocks = parts_ref.shape[0]
    wrows, cols = out_ref.shape
    width = cols // 4
    size = min(256, 2 * width)
    matrix = halves_matrix(size, half, True)
    for side in range(2):
        first = side * blocks // 2
        total = parts_ref[first].astype(F32)
        for block in range(first + 1, first + blocks // 2):
            total = total + parts_ref[block].astype(F32)
        stage_ref[side, pl.ds(0, 2 * wrows)] = total
    for part in range(2):
        for group in range(2 * width // size):
            lanes = slice(group * size // 2, (group + 1) * size // 2)
            both = jnp.concatenate(
                [stage_ref[side, pl.ds(part * wrows, wrows), lanes] for side in range(2)], axis=1
            )
            top = both.astype(BF16)
            rest = both - top.astype(F32)
            middle = rest.astype(BF16)
            bottom = (rest - middle.astype(F32)).astype(BF16)
            value = jnp.dot(top, matrix, preferred_element_type=F32)
            value = value + jnp.dot(middle, matrix, preferred_element_type=F32)
            value = value + jnp.dot(bottom, matrix, preferred_element_type=F32)
            at = part * 2 * width + group * size
            out_ref[:, at : at + size] = value


def sum_blocks(parts, half, wrows):
    width = parts.shape[2]
    vmem = pl.BlockSpec(memory_space=pltpu.VMEM)
    padded = -(-2 * wrows // 16) * 16
    return pl.pallas_call(
        functools.partial(sum_kernel, half),
        out_shape=jax.ShapeDtypeStruct((wrows, 4 * width), F32),
        in_specs=[vmem],
        out_specs=vmem,
        scratch_shapes=[pltpu.VMEM((2, padded, width), F32)],
        compiler_params=pltpu.CompilerParams(vmem_limit_bytes=32 * 2**20),
        cost_estimate=pl.CostEstimate(
            flops=6 * wrows * 4 * width * 256, bytes_accessed=2**19, transcendentals=0
        ),
    )(parts)


def swap_kernel(mask_ref, x_ref, g_ref, send_ref):
    tokens, feats = x_ref.shape
    span = tokens // 2
    lanes = feats // tokens
    deep = HALF // lanes
    skip = mask_ref[0] == 0
    left = mask_ref[2] == 0
    for seq in range(2):
        source = jnp.where(skip, 1 - seq, seq)
        rows = pl.ds(pl.multiple_of(source * span, span), span)
        send_ref[seq * span : (seq + 1) * span] = x_ref[rows]
    g = jnp.where(left, g_ref[HALF:].astype(F32), g_ref[:HALF].astype(F32))
    g0 = jnp.where(skip, g[:, span:], g[:, :span])
    g1 = jnp.where(skip, g[:, :span], g[:, span:])
    g = jnp.concatenate([g0, g1], axis=1).astype(BF16)
    for part in range(lanes):
        send_ref[tokens:, part * tokens : (part + 1) * tokens] = g[part * deep : (part + 1) * deep]


def prepare_swap(state, x, g):
    tokens, feats = x.shape
    vmem = pl.BlockSpec(memory_space=pltpu.VMEM)
    return pl.pallas_call(
        swap_kernel,
        out_shape=jax.ShapeDtypeStruct((tokens + HALF * tokens // feats, feats), BF16),
        in_specs=[pl.BlockSpec(memory_space=pltpu.SMEM), vmem, vmem],
        out_specs=vmem,
        compiler_params=pltpu.CompilerParams(vmem_limit_bytes=32 * 2**20),
        cost_estimate=pl.CostEstimate(flops=2**18, bytes_accessed=2**19, transcendentals=0),
    )(state, x, g)


def compact_kernel(mask_ref, x_ref, g_ref, recv_ref, x_out, g_out):
    tokens, feats = x_ref.shape
    span = tokens // 2
    lanes = feats // tokens
    deep = HALF // lanes
    count = mask_ref[0] + mask_ref[1]
    skip = jnp.where(mask_ref[0] == 0, 1, 0)
    left = mask_ref[2] == 0
    two = count == 2
    some = count >= 1
    mine = (jnp.logical_or(jnp.logical_and(left, some), two), jnp.logical_or(jnp.logical_and(left, two), jnp.logical_and(jnp.logical_not(left), some)))
    own_at = (jnp.where(two, 0, skip), jnp.where(jnp.logical_or(left, two), 1, skip))
    other_at = (0, jnp.where(count == 1, 0, 1))
    own = jnp.where(left, g_ref[:HALF].astype(F32), g_ref[HALF:].astype(F32))
    other = jnp.concatenate(
        [
            recv_ref[tokens:, part * tokens : (part + 1) * tokens].astype(F32)
            for part in range(lanes)
        ],
        axis=0,
    )
    for slot in range(2):
        here = slice(slot * span, (slot + 1) * span)
        own_rows = pl.ds(pl.multiple_of(own_at[slot] * span, span), span)
        other_rows = pl.ds(pl.multiple_of(other_at[slot] * span, span), span)

        @pl.when(mine[slot])
        def _():
            x_out[here] = x_ref[own_rows]
            g_out[:, here] = jnp.where(own_at[slot] == 0, own[:, :span], own[:, span:]).astype(BF16)

        @pl.when(jnp.logical_not(mine[slot]))
        def _():
            x_out[here] = recv_ref[other_rows]
            g_out[:, here] = jnp.where(other_at[slot] == 0, other[:, :span], other[:, span:]).astype(BF16)


def compact_pair(state, x, g, received):
    tokens, feats = x.shape
    vmem = pl.BlockSpec(memory_space=pltpu.VMEM)
    return pl.pallas_call(
        compact_kernel,
        out_shape=(
            jax.ShapeDtypeStruct((tokens, feats), BF16),
            jax.ShapeDtypeStruct((HALF, tokens), BF16),
        ),
        in_specs=[pl.BlockSpec(memory_space=pltpu.SMEM), vmem, vmem, vmem],
        out_specs=(vmem, vmem),
        compiler_params=pltpu.CompilerParams(vmem_limit_bytes=32 * 2**20),
        cost_estimate=pl.CostEstimate(flops=2**18, bytes_accessed=2**19, transcendentals=0),
    )(state, x, g, received)


def gather_doubling(value, axis_name, n):
    index = lax.axis_index(axis_name)
    bits = n.bit_length() - 1
    value = value.reshape((1,) * bits + value.shape)
    for axis in range(bits):
        step = n >> (axis + 1)
        other = lax.ppermute(value, axis_name, [(i, i ^ step) for i in range(n)])
        upper = (index & step) != 0
        value = jnp.concatenate(
            [jnp.where(upper, other, value), jnp.where(upper, value, other)], axis=axis
        )
    return value


def on_device(x, w, adjoint, mask):
    seqs = mask.shape[0]
    tokens, feats = x.shape
    wrows, cols = w.shape
    n_z = lax.axis_size("z")
    n_y, n_x = lax.axis_size("y_hi"), lax.axis_size("x")
    n_mp = n_y * n_x
    half = cols // n_mp // 2
    side = lax.axis_index("pair")
    core = lax.axis_index("core")
    count = jnp.sum(mask)

    def unpack(value):
        lead = value.shape[:-2]
        value = value.reshape(*lead, 2, wrows, n_mp * half // 2)
        return jnp.swapaxes(value, -3, -2).reshape(*lead, wrows, n_mp * half)

    w_mine = lax.all_to_all(spread_weight(w, half, n_z), ("pair", "z"), 0, 0, tiled=True)

    state = jnp.concatenate([mask, side.reshape(1)])
    g = adjoint.T
    received = swap_pair(prepare_swap(state, x, g))
    x_pair, g_cols = compact_pair(state, x, g, received)
    g_rows = gather_doubling(g_cols, "y_hi", n_y).reshape(1, n_y * half, tokens)

    w_theirs = swap_core(w_mine)
    w_cores = jnp.where(core == 0, jnp.stack([w_mine, w_theirs], 1), jnp.stack([w_theirs, w_mine], 1))
    w_full = unpack(w_cores).reshape(4 * n_z * wrows, n_mp * half)[:feats]

    kv = lax.dot_general(w_full, x_pair, (((0,), (1,)), ((), ())), preferred_element_type=F32)
    kv = kv.astype(BF16).reshape(n_y, n_x, half, tokens).transpose(1, 0, 2, 3)
    kv = kv.reshape(n_x, n_y * half, tokens)
    both = jnp.concatenate([kv, jnp.broadcast_to(g_rows, kv.shape)], axis=1)
    both = lax.all_to_all(both, "x", 0, 0, tiled=True)
    kv = jnp.sum(both[:, : n_y * half].astype(F32), axis=0).astype(BF16)
    kv_parts = lax.all_to_all(kv.reshape(n_y, half, tokens), "y_hi", 0, 0, tiled=True)

    dw_mine, dw_theirs = weight_blocks(core, both, x_pair, 2 * n_z, wrows)
    dw_theirs, both = lax.optimization_barrier((dw_theirs, both))
    dw_sum = dw_mine + swap_core(dw_theirs).astype(F32)

    send, keep = return_parts(both, w_full)
    received = swap_pair(send)
    dw_send, kv_parts = lax.optimization_barrier((dw_sum.astype(BF16), kv_parts))
    dw_parts = lax.all_to_all(dw_send, ("pair", "z"), 0, 0, tiled=True)
    weight_grad = sum_blocks(dw_parts, half, wrows)

    start = jnp.where(side == 0, 0, 2 - count)
    slots = jnp.minimum(jnp.stack([start, start + mask[0]]), 1)
    place = jnp.concatenate([mask, slots, side.reshape(1)])
    kv = jnp.sum(kv_parts.astype(F32), axis=0).astype(BF16)
    activation_grad, kv_home = bring_home(place, keep, received, kv, swap_pair(kv), seqs)
    return kv_home.T, activation_grad, weight_grad


def solution(mesh):
    n_dp, n_mp = mesh.devices.shape
    n_y = 1 << ((n_mp.bit_length() - 1) // 2)
    names = ("pair", "z", "core", "y_hi", "x")
    split = Mesh(mesh.devices.reshape(2, n_dp // 4, 2, n_y, n_mp // n_y), names)
    dp, mp = names[:3], names[3:]
    return jax.shard_map(
        on_device,
        mesh=split,
        in_specs=(P(dp, mp), P((*dp, *mp), None), P(dp, mp), P(dp)),
        out_specs=(P(dp, mp), P(dp, mp), P((*dp, *mp), None)),
        check_vma=False,
    )
```

```python
import functools

import jax
import jax.numpy as jnp
from jax import lax
from jax.experimental import pallas as pl
from jax.experimental.pallas import tpu as pltpu
from jax.sharding import Mesh, PartitionSpec as P

BF16 = jnp.bfloat16
F32 = jnp.float32
SWAP = [(0, 1), (1, 0)]
HALF = 32


def swap_pair(value):
    return lax.ppermute(value, "pair", SWAP)


def swap_core(value):
    return lax.ppermute(value, "core", SWAP)


def ordered(both_ref):
    n_x, rows, _ = both_ref.shape
    half = rows // 2
    n_y = half // HALF
    return jnp.concatenate(
        [
            both_ref[ix, half + iy * HALF : half + (iy + 1) * HALF]
            for iy in range(n_y)
            for ix in range(n_x)
        ],
        axis=0,
    )


def weight_kernel(blocks, wrows, core_ref, both_ref, x_ref, mine_ref, theirs_ref, acc_ref, stage_ref):
    tokens, feats = x_ref.shape
    width = acc_ref.shape[2]
    first_core = core_ref[0] == 0
    x_turned = x_ref[...].T
    g_all = ordered(both_ref)
    for part in range(2):
        g = g_all[part * width : (part + 1) * width]
        acc_ref[part, :feats] = lax.dot_general(
            x_turned, g, (((1,), (1,)), ((), ())), preferred_element_type=F32
        )
        acc_ref[part, feats:] = jnp.zeros_like(acc_ref[part, feats:])
    stage_ref[:, 2 * wrows :] = jnp.zeros_like(stage_ref[:, 2 * wrows :])
    for block in range(blocks):
        for part in range(2):
            top = acc_ref[part, pl.ds(2 * block * wrows, wrows)]
            bottom = acc_ref[part, pl.ds((2 * block + 1) * wrows, wrows)]
            mine_ref[block, pl.ds(part * wrows, wrows)] = jnp.where(first_core, top, bottom)
            stage_ref[block, pl.ds(part * wrows, wrows)] = jnp.where(first_core, bottom, top)
        theirs_ref[block] = stage_ref[block, : 2 * wrows].astype(BF16)


def weight_blocks(core, both, x_pair, blocks, wrows):
    tokens, feats = x_pair.shape
    width = both.shape[0] * both.shape[1] // 4
    vmem = pl.BlockSpec(memory_space=pltpu.VMEM)
    padded = -(-2 * wrows // 16) * 16
    shape = (blocks, 2 * wrows, width)
    return pl.pallas_call(
        functools.partial(weight_kernel, blocks, wrows),
        out_shape=(jax.ShapeDtypeStruct(shape, F32), jax.ShapeDtypeStruct(shape, BF16)),
        in_specs=[pl.BlockSpec(memory_space=pltpu.SMEM), vmem, vmem],
        out_specs=(vmem, vmem),
        scratch_shapes=[
            pltpu.VMEM((2, 2 * blocks * wrows, width), F32),
            pltpu.VMEM((blocks, padded, width), F32),
        ],
        compiler_params=pltpu.CompilerParams(vmem_limit_bytes=32 * 2**20),
        cost_estimate=pl.CostEstimate(
            flops=2 * feats * tokens * 2 * width, bytes_accessed=3 * 2**20, transcendentals=0
        ),
    )(core.reshape(1), both, x_pair)


def return_kernel(both_ref, w_ref, send_ref, keep_ref):
    g = ordered(both_ref)
    dx = lax.dot_general(g.T, w_ref[...], (((1,), (1,)), ((), ())), preferred_element_type=F32)
    keep_ref[...] = dx
    send_ref[...] = dx.astype(BF16)


def return_parts(both, w_full):
    tokens = both.shape[2]
    feats, width = w_full.shape
    vmem = pl.BlockSpec(memory_space=pltpu.VMEM)
    return pl.pallas_call(
        return_kernel,
        out_shape=(
            jax.ShapeDtypeStruct((tokens, feats), BF16),
            jax.ShapeDtypeStruct((tokens, feats), F32),
        ),
        in_specs=[vmem, vmem],
        out_specs=(vmem, vmem),
        compiler_params=pltpu.CompilerParams(vmem_limit_bytes=32 * 2**20),
        cost_estimate=pl.CostEstimate(
            flops=2 * feats * tokens * width, bytes_accessed=2 * 2**20, transcendentals=0
        ),
    )(both, w_full)


def home_kernel(seqs, place_ref, keep_ref, recv_ref, kv_ref, other_ref, dx_ref, out_ref):
    tokens, feats = keep_ref.shape
    half = kv_ref.shape[0]
    span = tokens // seqs
    left = place_ref[2 * seqs] == 0
    own = kv_ref[...].astype(F32)
    other = other_ref[...].astype(F32)
    low = jnp.where(left, own, other)
    high = jnp.where(left, other, own)
    for seq in range(seqs):
        alive = place_ref[seq] != 0
        slot = place_ref[seqs + seq]
        rows = pl.ds(pl.multiple_of(slot * span, span), span)
        total = keep_ref[rows] + recv_ref[rows].astype(F32)
        here = slice(seq * span, (seq + 1) * span)
        dx_ref[here] = jnp.where(alive, total, 0.0).astype(BF16)
        for at, value in ((0, low), (half, high)):
            picked = jnp.where(slot == 0, value[:, :span], value[:, span : 2 * span])
            out_ref[at : at + half, here] = jnp.where(alive, picked, 0.0).astype(BF16)


def bring_home(place, keep, received, kv, kv_other, seqs):
    tokens, feats = keep.shape
    half = kv.shape[0]
    vmem = pl.BlockSpec(memory_space=pltpu.VMEM)
    return pl.pallas_call(
        functools.partial(home_kernel, seqs),
        out_shape=(
            jax.ShapeDtypeStruct((tokens, feats), BF16),
            jax.ShapeDtypeStruct((2 * half, tokens), BF16),
        ),
        in_specs=[pl.BlockSpec(memory_space=pltpu.SMEM), vmem, vmem, vmem, vmem],
        out_specs=(vmem, vmem),
        compiler_params=pltpu.CompilerParams(vmem_limit_bytes=32 * 2**20),
        cost_estimate=pl.CostEstimate(flops=tokens * feats, bytes_accessed=2**20, transcendentals=0),
    )(place, keep, received, kv, kv_other)


def halves_matrix(size, half, transposed):
    here = lax.broadcasted_iota(jnp.int32, (size, size), 1 if transposed else 0)
    there = lax.broadcasted_iota(jnp.int32, (size, size), 0 if transposed else 1)
    rest = there % (size // 2)
    source = (rest // half) * (2 * half) + (there // (size // 2)) * half + rest % half
    return (here == source).astype(F32).astype(BF16)


def spread_kernel(half, n_z, w_ref, out_ref, stage_ref):
    wrows, cols = w_ref.shape
    width = cols // 4
    size = min(256, 2 * width)
    matrix = halves_matrix(size, half, False)
    stage_ref[:, 2 * wrows :] = jnp.zeros_like(stage_ref[:, 2 * wrows :])
    for part in range(2):
        for group in range(2 * width // size):
            at = part * 2 * width + group * size
            split = jnp.dot(w_ref[:, at : at + size], matrix, preferred_element_type=F32)
            lanes = slice(group * size // 2, (group + 1) * size // 2)
            for side in range(2):
                stage_ref[side, pl.ds(part * wrows, wrows), lanes] = split[
                    :, side * size // 2 : (side + 1) * size // 2
                ]
    for side in range(2):
        block = stage_ref[side, : 2 * wrows].astype(BF16)
        for z in range(n_z):
            out_ref[side * n_z + z] = block


def spread_weight(w, half, n_z):
    wrows, cols = w.shape
    vmem = pl.BlockSpec(memory_space=pltpu.VMEM)
    padded = -(-2 * wrows // 16) * 16
    return pl.pallas_call(
        functools.partial(spread_kernel, half, n_z),
        out_shape=jax.ShapeDtypeStruct((2 * n_z, 2 * wrows, cols // 4), BF16),
        in_specs=[vmem],
        out_specs=vmem,
        scratch_shapes=[pltpu.VMEM((2, padded, cols // 4), F32)],
        compiler_params=pltpu.CompilerParams(vmem_limit_bytes=32 * 2**20),
        cost_estimate=pl.CostEstimate(
            flops=2 * wrows * cols * 256, bytes_accessed=2**19, transcendentals=0
        ),
    )(w)


def sum_kernel(half, parts_ref, out_ref, stage_ref):
    blocks = parts_ref.shape[0]
    wrows, cols = out_ref.shape
    width = cols // 4
    size = min(256, 2 * width)
    matrix = halves_matrix(size, half, True)
    for side in range(2):
        first = side * blocks // 2
        total = parts_ref[first].astype(F32)
        for block in range(first + 1, first + blocks // 2):
            total = total + parts_ref[block].astype(F32)
        stage_ref[side, pl.ds(0, 2 * wrows)] = total
    for part in range(2):
        for group in range(2 * width // size):
            lanes = slice(group * size // 2, (group + 1) * size // 2)
            both = jnp.concatenate(
                [stage_ref[side, pl.ds(part * wrows, wrows), lanes] for side in range(2)], axis=1
            )
            top = both.astype(BF16)
            rest = both - top.astype(F32)
            middle = rest.astype(BF16)
            bottom = (rest - middle.astype(F32)).astype(BF16)
            value = jnp.dot(top, matrix, preferred_element_type=F32)
            value = value + jnp.dot(middle, matrix, preferred_element_type=F32)
            value = value + jnp.dot(bottom, matrix, preferred_element_type=F32)
            at = part * 2 * width + group * size
            out_ref[:, at : at + size] = value


def sum_blocks(parts, half, wrows):
    width = parts.shape[2]
    vmem = pl.BlockSpec(memory_space=pltpu.VMEM)
    padded = -(-2 * wrows // 16) * 16
    return pl.pallas_call(
        functools.partial(sum_kernel, half),
        out_shape=jax.ShapeDtypeStruct((wrows, 4 * width), F32),
        in_specs=[vmem],
        out_specs=vmem,
        scratch_shapes=[pltpu.VMEM((2, padded, width), F32)],
        compiler_params=pltpu.CompilerParams(vmem_limit_bytes=32 * 2**20),
        cost_estimate=pl.CostEstimate(
            flops=6 * wrows * 4 * width * 256, bytes_accessed=2**19, transcendentals=0
        ),
    )(parts)


def first_kernel(mask_ref, x_ref, send_ref):
    span = x_ref.shape[0] // 2
    skip = mask_ref[0] == 0
    for seq in range(2):
        source = jnp.where(skip, 1 - seq, seq)
        rows = pl.ds(pl.multiple_of(source * span, span), span)
        send_ref[seq * span : (seq + 1) * span] = x_ref[rows]


def theirs_kernel(mask_ref, g_ref, send_ref):
    span = g_ref.shape[1] // 2
    skip = mask_ref[0] == 0
    left = mask_ref[2] == 0
    g = jnp.where(left, g_ref[HALF:].astype(F32), g_ref[:HALF].astype(F32))
    send_ref[:, :span] = jnp.where(skip, g[:, span:], g[:, :span]).astype(BF16)
    send_ref[:, span:] = jnp.where(skip, g[:, :span], g[:, span:]).astype(BF16)


def places(mask_ref):
    count = mask_ref[0] + mask_ref[1]
    skip = jnp.where(mask_ref[0] == 0, 1, 0)
    left = mask_ref[2] == 0
    two = count == 2
    some = count >= 1
    right_some = jnp.logical_and(jnp.logical_not(left), some)
    mine = (
        jnp.logical_or(jnp.logical_and(left, some), two),
        jnp.logical_or(two, right_some),
    )
    own_at = (jnp.where(two, 0, skip), jnp.where(jnp.logical_or(left, two), 1, skip))
    other_at = (0, jnp.where(count == 1, 0, 1))
    return mine, own_at, other_at


def rows_kernel(mask_ref, x_ref, recv_ref, out_ref):
    span = x_ref.shape[0] // 2
    mine, own_at, other_at = places(mask_ref)
    for slot in range(2):
        here = slice(slot * span, (slot + 1) * span)
        own_rows = pl.ds(pl.multiple_of(own_at[slot] * span, span), span)
        other_rows = pl.ds(pl.multiple_of(other_at[slot] * span, span), span)

        @pl.when(mine[slot])
        def _():
            out_ref[here] = x_ref[own_rows]

        @pl.when(jnp.logical_not(mine[slot]))
        def _():
            out_ref[here] = recv_ref[other_rows]


def columns_kernel(mask_ref, g_ref, recv_ref, out_ref):
    span = g_ref.shape[1] // 2
    left = mask_ref[2] == 0
    mine, own_at, other_at = places(mask_ref)
    own = jnp.where(left, g_ref[:HALF].astype(F32), g_ref[HALF:].astype(F32))
    other = recv_ref[...].astype(F32)
    for slot in range(2):
        here = slice(slot * span, (slot + 1) * span)
        a = jnp.where(own_at[slot] == 0, own[:, :span], own[:, span:])
        b = jnp.where(other_at[slot] == 0, other[:, :span], other[:, span:])
        out_ref[:, here] = jnp.where(mine[slot], a, b).astype(BF16)


def small_call(kernel, shape, state, *operands):
    vmem = pl.BlockSpec(memory_space=pltpu.VMEM)
    return pl.pallas_call(
        kernel,
        out_shape=jax.ShapeDtypeStruct(shape, BF16),
        in_specs=[pl.BlockSpec(memory_space=pltpu.SMEM)] + [vmem] * len(operands),
        out_specs=vmem,
        compiler_params=pltpu.CompilerParams(vmem_limit_bytes=32 * 2**20),
        cost_estimate=pl.CostEstimate(flops=2**18, bytes_accessed=2**18, transcendentals=0),
    )(state, *operands)


def gather_doubling(value, axis_name, n, early):
    index = lax.axis_index(axis_name)
    bits = n.bit_length() - 1
    value = value.reshape((1,) * bits + value.shape)
    for axis in range(bits):
        step = n >> (axis + 1)
        if axis == bits - 1:
            value, early = lax.optimization_barrier((value, early))
        other = lax.ppermute(value, axis_name, [(i, i ^ step) for i in range(n)])
        upper = (index & step) != 0
        value = jnp.concatenate(
            [jnp.where(upper, other, value), jnp.where(upper, value, other)], axis=axis
        )
    return value, early


def scatter_sum(value, axis_name, n):
    index = lax.axis_index(axis_name)
    total = lax.dynamic_index_in_dim(value, index, keepdims=False)
    narrow = value.astype(BF16)
    for step in range(1, n):
        block = lax.dynamic_index_in_dim(narrow, index ^ step, keepdims=False)
        total = total + lax.ppermute(block, axis_name, [(i, i ^ step) for i in range(n)]).astype(F32)
    return total


def on_device(x, w, adjoint, mask):
    seqs = mask.shape[0]
    tokens, feats = x.shape
    wrows, cols = w.shape
    n_z = lax.axis_size("z")
    n_y, n_x = lax.axis_size("y_hi"), lax.axis_size("x")
    n_mp = n_y * n_x
    half = cols // n_mp // 2
    side = lax.axis_index("pair")
    core = lax.axis_index("core")
    count = jnp.sum(mask)

    def unpack(value):
        lead = value.shape[:-2]
        value = value.reshape(*lead, 2, wrows, n_mp * half // 2)
        return jnp.swapaxes(value, -3, -2).reshape(*lead, wrows, n_mp * half)

    w_mine = lax.all_to_all(spread_weight(w, half, n_z), ("pair", "z"), 0, 0, tiled=True)

    state = jnp.concatenate([mask, side.reshape(1)])
    g = adjoint.T
    g_other = swap_pair(small_call(theirs_kernel, (half, tokens), state, g))
    g_cols = small_call(columns_kernel, (half, tokens), state, g, g_other)
    x_other = swap_pair(small_call(first_kernel, (tokens, feats), state, x))
    x_pair = small_call(rows_kernel, (tokens, feats), state, x, x_other)
    g_rows, x_pair = gather_doubling(g_cols, "y_hi", n_y, x_pair)
    g_rows = g_rows.reshape(1, n_y * half, tokens)

    w_theirs = swap_core(w_mine)
    w_cores = jnp.where(core == 0, jnp.stack([w_mine, w_theirs], 1), jnp.stack([w_theirs, w_mine], 1))
    w_full = unpack(w_cores).reshape(4 * n_z * wrows, n_mp * half)[:feats]

    kv = lax.dot_general(w_full, x_pair, (((0,), (1,)), ((), ())), preferred_element_type=F32)
    kv = kv.astype(BF16).reshape(n_y, n_x, half, tokens).transpose(1, 0, 2, 3)
    kv = kv.reshape(n_x, n_y * half, tokens)
    both = jnp.concatenate([kv, jnp.broadcast_to(g_rows, kv.shape)], axis=1)
    both = lax.all_to_all(both, "x", 0, 0, tiled=True)

    dw_mine, dw_theirs = weight_blocks(core, both, x_pair, 2 * n_z, wrows)
    dw_theirs, both = lax.optimization_barrier((dw_theirs, both))
    dw_sum = dw_mine + swap_core(dw_theirs).astype(F32)

    send, keep = return_parts(both, w_full)
    received = swap_pair(send)
    dw_send, both = lax.optimization_barrier((dw_sum.astype(BF16), both))
    dw_parts = lax.all_to_all(dw_send, ("pair", "z"), 0, 0, tiled=True)
    weight_grad = sum_blocks(dw_parts, half, wrows)

    start = jnp.where(side == 0, 0, 2 - count)
    slots = jnp.minimum(jnp.stack([start, start + mask[0]]), 1)
    place = jnp.concatenate([mask, slots, side.reshape(1)])
    kv = jnp.sum(both[:, : n_y * half].astype(F32), axis=0).reshape(n_y, half, tokens)
    kv = scatter_sum(kv, "y_hi", n_y).astype(BF16)
    activation_grad, kv_home = bring_home(place, keep, received, kv, swap_pair(kv), seqs)
    return kv_home.T, activation_grad, weight_grad


def solution(mesh):
    n_dp, n_mp = mesh.devices.shape
    n_y = 1 << ((n_mp.bit_length() - 1) // 2)
    names = ("pair", "z", "core", "y_hi", "x")
    split = Mesh(mesh.devices.reshape(2, n_dp // 4, 2, n_y, n_mp // n_y), names)
    dp, mp = names[:3], names[3:]
    return jax.shard_map(
        on_device,
        mesh=split,
        in_specs=(P(dp, mp), P((*dp, *mp), None), P(dp, mp), P(dp)),
        out_specs=(P(dp, mp), P(dp, mp), P((*dp, *mp), None)),
        check_vma=False,
    )
```

```python
import functools

import jax
import jax.numpy as jnp
from jax import lax
from jax.experimental import pallas as pl
from jax.experimental.pallas import tpu as pltpu
from jax.sharding import Mesh, PartitionSpec as P

BF16 = jnp.bfloat16
F32 = jnp.float32
SWAP = [(0, 1), (1, 0)]


def swap_pair(value):
    return lax.ppermute(value, "pair", SWAP)


def swap_core(value):
    return lax.ppermute(value, "core", SWAP)


def weight_kernel(blocks, wrows, core_ref, both_ref, x_ref, mine_ref, theirs_ref, acc_ref, stage_ref):
    tokens, feats = x_ref.shape
    n_mp, rows, _ = both_ref.shape
    half = rows // 2
    width = acc_ref.shape[2]
    groups = width // half
    first_core = core_ref[0] == 0
    x_turned = x_ref[...].T
    for part in range(2):
        g = both_ref[part * groups : (part + 1) * groups, half:, :].reshape(width, tokens)
        acc_ref[part, :feats] = lax.dot_general(
            x_turned, g, (((1,), (1,)), ((), ())), preferred_element_type=F32
        )
        acc_ref[part, feats:] = jnp.zeros_like(acc_ref[part, feats:])
    stage_ref[:, 2 * wrows :] = jnp.zeros_like(stage_ref[:, 2 * wrows :])
    for block in range(blocks):
        for part in range(2):
            top = acc_ref[part, pl.ds(2 * block * wrows, wrows)]
            bottom = acc_ref[part, pl.ds((2 * block + 1) * wrows, wrows)]
            mine_ref[block, pl.ds(part * wrows, wrows)] = jnp.where(first_core, top, bottom)
            stage_ref[block, pl.ds(part * wrows, wrows)] = jnp.where(first_core, bottom, top)
        theirs_ref[block] = stage_ref[block, : 2 * wrows].astype(BF16)


def weight_blocks(core, both, x_pair, blocks, wrows):
    tokens, feats = x_pair.shape
    n_mp, rows, _ = both.shape
    width = n_mp * rows // 4
    vmem = pl.BlockSpec(memory_space=pltpu.VMEM)
    padded = -(-2 * wrows // 16) * 16
    shape = (blocks, 2 * wrows, width)
    return pl.pallas_call(
        functools.partial(weight_kernel, blocks, wrows),
        out_shape=(jax.ShapeDtypeStruct(shape, F32), jax.ShapeDtypeStruct(shape, BF16)),
        in_specs=[pl.BlockSpec(memory_space=pltpu.SMEM), vmem, vmem],
        out_specs=(vmem, vmem),
        scratch_shapes=[
            pltpu.VMEM((2, 2 * blocks * wrows, width), F32),
            pltpu.VMEM((blocks, padded, width), F32),
        ],
        compiler_params=pltpu.CompilerParams(vmem_limit_bytes=32 * 2**20),
        cost_estimate=pl.CostEstimate(
            flops=2 * feats * tokens * 2 * width, bytes_accessed=3 * 2**20, transcendentals=0
        ),
    )(core.reshape(1), both, x_pair)


def return_kernel(both_ref, w_ref, send_ref, keep_ref, kv_ref):
    n_mp, rows, tokens = both_ref.shape
    feats = w_ref.shape[0]
    half = rows // 2
    g = both_ref[:, half:, :].reshape(n_mp * half, tokens)
    dx = lax.dot_general(g.T, w_ref[...], (((1,), (1,)), ((), ())), preferred_element_type=F32)
    keep_ref[...] = dx
    send_ref[:tokens] = dx.astype(BF16)
    kv = jnp.sum(both_ref[:, :half, :].astype(F32), axis=0).astype(BF16)
    kv_ref[...] = kv
    lanes = feats // tokens
    deep = half // lanes
    for part in range(lanes):
        send_ref[tokens:, part * tokens : (part + 1) * tokens] = kv[part * deep : (part + 1) * deep]


def return_parts(both, w_full):
    n_mp, rows, tokens = both.shape
    feats, width = w_full.shape
    half = rows // 2
    vmem = pl.BlockSpec(memory_space=pltpu.VMEM)
    return pl.pallas_call(
        return_kernel,
        out_shape=(
            jax.ShapeDtypeStruct((tokens + half * tokens // feats, feats), BF16),
            jax.ShapeDtypeStruct((tokens, feats), F32),
            jax.ShapeDtypeStruct((half, tokens), BF16),
        ),
        in_specs=[vmem, vmem],
        out_specs=(vmem, vmem, vmem),
        compiler_params=pltpu.CompilerParams(vmem_limit_bytes=32 * 2**20),
        cost_estimate=pl.CostEstimate(
            flops=2 * feats * tokens * width, bytes_accessed=2 * 2**20, transcendentals=0
        ),
    )(both, w_full)


def home_kernel(seqs, place_ref, keep_ref, recv_ref, kv_ref, dx_ref, out_ref):
    tokens, feats = keep_ref.shape
    half = kv_ref.shape[0]
    span = tokens // seqs
    lanes = feats // tokens
    deep = half // lanes
    left = place_ref[2 * seqs] == 0
    own = kv_ref[...].astype(F32)
    other = jnp.concatenate(
        [
            recv_ref[tokens:, part * tokens : (part + 1) * tokens].astype(F32)
            for part in range(lanes)
        ],
        axis=0,
    )
    low = jnp.where(left, own, other)
    high = jnp.where(left, other, own)
    for seq in range(seqs):
        alive = place_ref[seq] != 0
        slot = place_ref[seqs + seq]
        rows = pl.ds(pl.multiple_of(slot * span, span), span)
        total = keep_ref[rows] + recv_ref[rows].astype(F32)
        here = slice(seq * span, (seq + 1) * span)
        dx_ref[here] = jnp.where(alive, total, 0.0).astype(BF16)
        for at, value in ((0, low), (half, high)):
            picked = jnp.where(slot == 0, value[:, :span], value[:, span : 2 * span])
            out_ref[at : at + half, here] = jnp.where(alive, picked, 0.0).astype(BF16)


def bring_home(place, keep, received, kv, seqs):
    tokens, feats = keep.shape
    half = kv.shape[0]
    vmem = pl.BlockSpec(memory_space=pltpu.VMEM)
    return pl.pallas_call(
        functools.partial(home_kernel, seqs),
        out_shape=(
            jax.ShapeDtypeStruct((tokens, feats), BF16),
            jax.ShapeDtypeStruct((2 * half, tokens), BF16),
        ),
        in_specs=[pl.BlockSpec(memory_space=pltpu.SMEM), vmem, vmem, vmem],
        out_specs=(vmem, vmem),
        compiler_params=pltpu.CompilerParams(vmem_limit_bytes=32 * 2**20),
        cost_estimate=pl.CostEstimate(flops=tokens * feats, bytes_accessed=2**20, transcendentals=0),
    )(place, keep, received, kv)


def halves_matrix(size, half, transposed):
    here = lax.broadcasted_iota(jnp.int32, (size, size), 1 if transposed else 0)
    there = lax.broadcasted_iota(jnp.int32, (size, size), 0 if transposed else 1)
    rest = there % (size // 2)
    source = (rest // half) * (2 * half) + (there // (size // 2)) * half + rest % half
    return (here == source).astype(F32).astype(BF16)


def spread_kernel(half, n_z, turn_ref, w_ref, out_ref, stage_ref):
    wrows, cols = w_ref.shape
    width = cols // 4
    size = min(256, 2 * width)
    matrix = halves_matrix(size, half, False)
    stage_ref[:, 2 * wrows :] = jnp.zeros_like(stage_ref[:, 2 * wrows :])
    for part in range(2):
        for group in range(2 * width // size):
            at = part * 2 * width + group * size
            split = jnp.dot(w_ref[:, at : at + size], matrix, preferred_element_type=F32)
            lanes = slice(group * size // 2, (group + 1) * size // 2)
            for side in range(2):
                stage_ref[side, pl.ds(part * wrows, wrows), lanes] = split[
                    :, side * size // 2 : (side + 1) * size // 2
                ]
    turned = turn_ref[0] != 0
    low, high = stage_ref[0, : 2 * wrows], stage_ref[1, : 2 * wrows]
    for side, block in enumerate((jnp.where(turned, high, low), jnp.where(turned, low, high))):
        block = block.astype(BF16)
        for z in range(n_z):
            out_ref[side * n_z + z] = block


def spread_weight(turn, w, half, n_z):
    wrows, cols = w.shape
    vmem = pl.BlockSpec(memory_space=pltpu.VMEM)
    padded = -(-2 * wrows // 16) * 16
    return pl.pallas_call(
        functools.partial(spread_kernel, half, n_z),
        out_shape=jax.ShapeDtypeStruct((2 * n_z, 2 * wrows, cols // 4), BF16),
        in_specs=[pl.BlockSpec(memory_space=pltpu.SMEM), vmem],
        out_specs=vmem,
        scratch_shapes=[pltpu.VMEM((2, padded, cols // 4), F32)],
        compiler_params=pltpu.CompilerParams(vmem_limit_bytes=32 * 2**20),
        cost_estimate=pl.CostEstimate(
            flops=2 * wrows * cols * 256, bytes_accessed=2**19, transcendentals=0
        ),
    )(turn.reshape(1), w)


def sum_kernel(half, turn_ref, parts_ref, out_ref, stage_ref):
    blocks = parts_ref.shape[0]
    wrows, cols = out_ref.shape
    width = cols // 4
    size = min(256, 2 * width)
    matrix = halves_matrix(size, half, True)
    sums = []
    for side in range(2):
        first = side * blocks // 2
        total = parts_ref[first].astype(F32)
        for block in range(first + 1, first + blocks // 2):
            total = total + parts_ref[block].astype(F32)
        sums.append(total)
    turned = turn_ref[0] != 0
    stage_ref[0, pl.ds(0, 2 * wrows)] = jnp.where(turned, sums[1], sums[0])
    stage_ref[1, pl.ds(0, 2 * wrows)] = jnp.where(turned, sums[0], sums[1])
    for part in range(2):
        for group in range(2 * width // size):
            lanes = slice(group * size // 2, (group + 1) * size // 2)
            both = jnp.concatenate(
                [stage_ref[side, pl.ds(part * wrows, wrows), lanes] for side in range(2)], axis=1
            )
            top = both.astype(BF16)
            rest = both - top.astype(F32)
            middle = rest.astype(BF16)
            bottom = (rest - middle.astype(F32)).astype(BF16)
            value = jnp.dot(top, matrix, preferred_element_type=F32)
            value = value + jnp.dot(middle, matrix, preferred_element_type=F32)
            value = value + jnp.dot(bottom, matrix, preferred_element_type=F32)
            at = part * 2 * width + group * size
            out_ref[:, at : at + size] = value


def sum_blocks(turn, parts, half, wrows):
    width = parts.shape[2]
    vmem = pl.BlockSpec(memory_space=pltpu.VMEM)
    padded = -(-2 * wrows // 16) * 16
    return pl.pallas_call(
        functools.partial(sum_kernel, half),
        out_shape=jax.ShapeDtypeStruct((wrows, 4 * width), F32),
        in_specs=[pl.BlockSpec(memory_space=pltpu.SMEM), vmem],
        out_specs=vmem,
        scratch_shapes=[pltpu.VMEM((2, padded, width), F32)],
        compiler_params=pltpu.CompilerParams(vmem_limit_bytes=32 * 2**20),
        cost_estimate=pl.CostEstimate(
            flops=6 * wrows * 4 * width * 256, bytes_accessed=2**19, transcendentals=0
        ),
    )(turn.reshape(1), parts)


def on_device(x, w, adjoint, mask):
    seqs = mask.shape[0]
    tokens, feats = x.shape
    span = tokens // seqs
    wrows, cols = w.shape
    n_z = lax.axis_size("z")
    n_mp = lax.axis_size("mp")
    half = cols // n_mp // 2
    side = lax.axis_index("pair")
    core = lax.axis_index("core")
    turn = lax.axis_index("mp") // (n_mp // 2)
    hand = jnp.bitwise_xor(side, turn)
    groups = [
        [(s ^ (g // (n_mp // 2))) * n_mp + g for g in range(n_mp)] for s in range(2)
    ]

    alive = mask != 0
    count = jnp.sum(mask)
    first_count = jnp.where(side == 0, count, 2 - count)
    skip_first = jnp.logical_not(alive[0])

    def survivor_first(value):
        return jnp.where(skip_first, value[::-1], value)

    def compact(own, other):
        a0 = jnp.where(side == 0, own[0], other[0])
        a1 = jnp.where(side == 0, own[1], other[1])
        b0 = jnp.where(side == 0, other[0], own[0])
        b1 = jnp.where(side == 0, other[1], own[1])
        slot0 = jnp.where(first_count >= 1, a0, b0)
        slot1 = jnp.where(first_count == 2, a1, jnp.where(first_count == 1, b0, b1))
        return jnp.stack([slot0, slot1])

    def unpack(value):
        lead = value.shape[:-2]
        value = value.reshape(*lead, 2, wrows, n_mp * half // 2)
        return jnp.swapaxes(value, -3, -2).reshape(*lead, wrows, n_mp * half)

    w_mine = lax.all_to_all(spread_weight(turn, w, half, n_z), ("pair", "z"), 0, 0, tiled=True)

    g = survivor_first(adjoint.T.reshape(2, half, seqs, span).transpose(2, 0, 1, 3))
    g_mine = jnp.where(hand == 0, g[:, 0], g[:, 1])
    g_theirs = jnp.where(hand == 0, g[:, 1], g[:, 0])
    xs = survivor_first(x.reshape(seqs, span, feats))
    g_other = swap_pair(g_theirs)
    x_other = swap_pair(xs)
    g_pair = compact(g_mine, g_other)
    g_cols = g_pair.transpose(1, 0, 2).reshape(1, half, tokens)
    x_pair = compact(xs, x_other).reshape(tokens, feats)

    w_theirs = swap_core(w_mine)
    w_cores = jnp.where(core == 0, jnp.stack([w_mine, w_theirs], 1), jnp.stack([w_theirs, w_mine], 1))
    w_full = unpack(w_cores).reshape(4 * n_z * wrows, n_mp * half)[:feats]

    kv = lax.dot_general(w_full, x_pair, (((0,), (1,)), ((), ())), preferred_element_type=F32)
    kv = kv.astype(BF16).reshape(n_mp, half, tokens)
    both = jnp.concatenate([kv, jnp.broadcast_to(g_cols, (n_mp, half, tokens))], axis=1)
    both = lax.all_to_all(both, ("pair", "mp"), 0, 0, axis_index_groups=groups, tiled=True)

    dw_mine, dw_theirs = weight_blocks(core, both, x_pair, 2 * n_z, wrows)
    dw_theirs, both = lax.optimization_barrier((dw_theirs, both))
    dw_sum = dw_mine + swap_core(dw_theirs).astype(F32)

    send, keep, kv = return_parts(both, w_full)
    received = swap_pair(send)
    dw_send, keep = lax.optimization_barrier((dw_sum.astype(BF16), keep))
    dw_parts = lax.all_to_all(dw_send, ("pair", "z"), 0, 0, tiled=True)
    weight_grad = sum_blocks(turn, dw_parts, half, wrows)

    start = jnp.where(side == 0, 0, 2 - count)
    slots = jnp.minimum(jnp.stack([start, start + mask[0]]), 1)
    place = jnp.concatenate([mask, slots, hand.reshape(1)])
    activation_grad, kv_home = bring_home(place, keep, received, kv, seqs)
    return kv_home.T, activation_grad, weight_grad


def solution(mesh):
    n_dp, n_mp = mesh.devices.shape
    names = ("pair", "z", "core", "mp")
    split = Mesh(mesh.devices.reshape(2, n_dp // 4, 2, n_mp), names)
    dp = ("pair", "z", "core")
    return jax.shard_map(
        on_device,
        mesh=split,
        in_specs=(P(dp, "mp"), P((*dp, "mp"), None), P(dp, "mp"), P(dp)),
        out_specs=(P(dp, "mp"), P(dp, "mp"), P((*dp, "mp"), None)),
        check_vma=False,
    )
```

```python
import functools

import jax
import jax.numpy as jnp
from jax import lax
from jax.experimental import pallas as pl
from jax.experimental.pallas import tpu as pltpu
from jax.sharding import Mesh, PartitionSpec as P

BF16 = jnp.bfloat16
F32 = jnp.float32
SWAP = [(0, 1), (1, 0)]
HALF = 32


def swap_pair(value):
    return lax.ppermute(value, "pair", SWAP)


def swap_core(value):
    return lax.ppermute(value, "core", SWAP)


def weight_kernel(blocks, wrows, core_ref, both_ref, x_ref, mine_ref, theirs_ref, acc_ref, stage_ref):
    tokens, feats = x_ref.shape
    n_mp, rows, _ = both_ref.shape
    half = rows // 2
    width = acc_ref.shape[2]
    groups = width // half
    first_core = core_ref[0] == 0
    x_turned = x_ref[...].T
    for part in range(2):
        g = both_ref[part * groups : (part + 1) * groups, half:, :].reshape(width, tokens)
        acc_ref[part, :feats] = lax.dot_general(
            x_turned, g, (((1,), (1,)), ((), ())), preferred_element_type=F32
        )
        acc_ref[part, feats:] = jnp.zeros_like(acc_ref[part, feats:])
    stage_ref[:, 2 * wrows :] = jnp.zeros_like(stage_ref[:, 2 * wrows :])
    for block in range(blocks):
        for part in range(2):
            top = acc_ref[part, pl.ds(2 * block * wrows, wrows)]
            bottom = acc_ref[part, pl.ds((2 * block + 1) * wrows, wrows)]
            mine_ref[block, pl.ds(part * wrows, wrows)] = jnp.where(first_core, top, bottom)
            stage_ref[block, pl.ds(part * wrows, wrows)] = jnp.where(first_core, bottom, top)
        theirs_ref[block] = stage_ref[block, : 2 * wrows].astype(BF16)


def weight_blocks(core, both, x_pair, blocks, wrows):
    tokens, feats = x_pair.shape
    n_mp, rows, _ = both.shape
    width = n_mp * rows // 4
    vmem = pl.BlockSpec(memory_space=pltpu.VMEM)
    padded = -(-2 * wrows // 16) * 16
    shape = (blocks, 2 * wrows, width)
    return pl.pallas_call(
        functools.partial(weight_kernel, blocks, wrows),
        out_shape=(jax.ShapeDtypeStruct(shape, F32), jax.ShapeDtypeStruct(shape, BF16)),
        in_specs=[pl.BlockSpec(memory_space=pltpu.SMEM), vmem, vmem],
        out_specs=(vmem, vmem),
        scratch_shapes=[
            pltpu.VMEM((2, 2 * blocks * wrows, width), F32),
            pltpu.VMEM((blocks, padded, width), F32),
        ],
        compiler_params=pltpu.CompilerParams(vmem_limit_bytes=32 * 2**20),
        cost_estimate=pl.CostEstimate(
            flops=2 * feats * tokens * 2 * width, bytes_accessed=3 * 2**20, transcendentals=0
        ),
    )(core.reshape(1), both, x_pair)


def return_kernel(both_ref, w_ref, send_ref, keep_ref, kv_ref):
    n_mp, rows, tokens = both_ref.shape
    feats = w_ref.shape[0]
    half = rows // 2
    g = both_ref[:, half:, :].reshape(n_mp * half, tokens)
    dx = lax.dot_general(g.T, w_ref[...], (((1,), (1,)), ((), ())), preferred_element_type=F32)
    keep_ref[...] = dx
    send_ref[:tokens] = dx.astype(BF16)
    kv = jnp.sum(both_ref[:, :half, :].astype(F32), axis=0).astype(BF16)
    kv_ref[...] = kv
    lanes = feats // tokens
    deep = half // lanes
    for part in range(lanes):
        send_ref[tokens:, part * tokens : (part + 1) * tokens] = kv[part * deep : (part + 1) * deep]


def return_parts(both, w_full):
    n_mp, rows, tokens = both.shape
    feats, width = w_full.shape
    half = rows // 2
    vmem = pl.BlockSpec(memory_space=pltpu.VMEM)
    return pl.pallas_call(
        return_kernel,
        out_shape=(
            jax.ShapeDtypeStruct((tokens + half * tokens // feats, feats), BF16),
            jax.ShapeDtypeStruct((tokens, feats), F32),
            jax.ShapeDtypeStruct((half, tokens), BF16),
        ),
        in_specs=[vmem, vmem],
        out_specs=(vmem, vmem, vmem),
        compiler_params=pltpu.CompilerParams(vmem_limit_bytes=32 * 2**20),
        cost_estimate=pl.CostEstimate(
            flops=2 * feats * tokens * width, bytes_accessed=2 * 2**20, transcendentals=0
        ),
    )(both, w_full)


def home_kernel(seqs, place_ref, keep_ref, recv_ref, kv_ref, dx_ref, out_ref):
    tokens, feats = keep_ref.shape
    half = kv_ref.shape[0]
    span = tokens // seqs
    lanes = feats // tokens
    deep = half // lanes
    left = place_ref[2 * seqs] == 0
    own = kv_ref[...].astype(F32)
    other = jnp.concatenate(
        [
            recv_ref[tokens:, part * tokens : (part + 1) * tokens].astype(F32)
            for part in range(lanes)
        ],
        axis=0,
    )
    low = jnp.where(left, own, other)
    high = jnp.where(left, other, own)
    for seq in range(seqs):
        alive = place_ref[seq] != 0
        slot = place_ref[seqs + seq]
        rows = pl.ds(pl.multiple_of(slot * span, span), span)
        total = keep_ref[rows] + recv_ref[rows].astype(F32)
        here = slice(seq * span, (seq + 1) * span)
        dx_ref[here] = jnp.where(alive, total, 0.0).astype(BF16)
        for at, value in ((0, low), (half, high)):
            picked = jnp.where(slot == 0, value[:, :span], value[:, span : 2 * span])
            out_ref[at : at + half, here] = jnp.where(alive, picked, 0.0).astype(BF16)


def bring_home(place, keep, received, kv, seqs):
    tokens, feats = keep.shape
    half = kv.shape[0]
    vmem = pl.BlockSpec(memory_space=pltpu.VMEM)
    return pl.pallas_call(
        functools.partial(home_kernel, seqs),
        out_shape=(
            jax.ShapeDtypeStruct((tokens, feats), BF16),
            jax.ShapeDtypeStruct((2 * half, tokens), BF16),
        ),
        in_specs=[pl.BlockSpec(memory_space=pltpu.SMEM), vmem, vmem, vmem],
        out_specs=(vmem, vmem),
        compiler_params=pltpu.CompilerParams(vmem_limit_bytes=32 * 2**20),
        cost_estimate=pl.CostEstimate(flops=tokens * feats, bytes_accessed=2**20, transcendentals=0),
    )(place, keep, received, kv)


def halves_matrix(size, half, transposed):
    here = lax.broadcasted_iota(jnp.int32, (size, size), 1 if transposed else 0)
    there = lax.broadcasted_iota(jnp.int32, (size, size), 0 if transposed else 1)
    rest = there % (size // 2)
    source = (rest // half) * (2 * half) + (there // (size // 2)) * half + rest % half
    return (here == source).astype(F32).astype(BF16)


def spread_kernel(half, n_z, turn_ref, w_ref, out_ref, stage_ref):
    wrows, cols = w_ref.shape
    width = cols // 4
    size = min(256, 2 * width)
    matrix = halves_matrix(size, half, False)
    stage_ref[:, 2 * wrows :] = jnp.zeros_like(stage_ref[:, 2 * wrows :])
    for part in range(2):
        for group in range(2 * width // size):
            at = part * 2 * width + group * size
            split = jnp.dot(w_ref[:, at : at + size], matrix, preferred_element_type=F32)
            lanes = slice(group * size // 2, (group + 1) * size // 2)
            for side in range(2):
                stage_ref[side, pl.ds(part * wrows, wrows), lanes] = split[
                    :, side * size // 2 : (side + 1) * size // 2
                ]
    turned = turn_ref[0] != 0
    low, high = stage_ref[0, : 2 * wrows], stage_ref[1, : 2 * wrows]
    for side, block in enumerate((jnp.where(turned, high, low), jnp.where(turned, low, high))):
        block = block.astype(BF16)
        for z in range(n_z):
            out_ref[side * n_z + z] = block


def spread_weight(turn, w, half, n_z):
    wrows, cols = w.shape
    vmem = pl.BlockSpec(memory_space=pltpu.VMEM)
    padded = -(-2 * wrows // 16) * 16
    return pl.pallas_call(
        functools.partial(spread_kernel, half, n_z),
        out_shape=jax.ShapeDtypeStruct((2 * n_z, 2 * wrows, cols // 4), BF16),
        in_specs=[pl.BlockSpec(memory_space=pltpu.SMEM), vmem],
        out_specs=vmem,
        scratch_shapes=[pltpu.VMEM((2, padded, cols // 4), F32)],
        compiler_params=pltpu.CompilerParams(vmem_limit_bytes=32 * 2**20),
        cost_estimate=pl.CostEstimate(
            flops=2 * wrows * cols * 256, bytes_accessed=2**19, transcendentals=0
        ),
    )(turn.reshape(1), w)


def sum_kernel(half, turn_ref, parts_ref, out_ref, stage_ref):
    blocks = parts_ref.shape[0]
    wrows, cols = out_ref.shape
    width = cols // 4
    size = min(256, 2 * width)
    matrix = halves_matrix(size, half, True)
    sums = []
    for side in range(2):
        first = side * blocks // 2
        total = parts_ref[first].astype(F32)
        for block in range(first + 1, first + blocks // 2):
            total = total + parts_ref[block].astype(F32)
        sums.append(total)
    turned = turn_ref[0] != 0
    stage_ref[0, pl.ds(0, 2 * wrows)] = jnp.where(turned, sums[1], sums[0])
    stage_ref[1, pl.ds(0, 2 * wrows)] = jnp.where(turned, sums[0], sums[1])
    for part in range(2):
        for group in range(2 * width // size):
            lanes = slice(group * size // 2, (group + 1) * size // 2)
            both = jnp.concatenate(
                [stage_ref[side, pl.ds(part * wrows, wrows), lanes] for side in range(2)], axis=1
            )
            top = both.astype(BF16)
            rest = both - top.astype(F32)
            middle = rest.astype(BF16)
            bottom = (rest - middle.astype(F32)).astype(BF16)
            value = jnp.dot(top, matrix, preferred_element_type=F32)
            value = value + jnp.dot(middle, matrix, preferred_element_type=F32)
            value = value + jnp.dot(bottom, matrix, preferred_element_type=F32)
            at = part * 2 * width + group * size
            out_ref[:, at : at + size] = value


def sum_blocks(turn, parts, half, wrows):
    width = parts.shape[2]
    vmem = pl.BlockSpec(memory_space=pltpu.VMEM)
    padded = -(-2 * wrows // 16) * 16
    return pl.pallas_call(
        functools.partial(sum_kernel, half),
        out_shape=jax.ShapeDtypeStruct((wrows, 4 * width), F32),
        in_specs=[pl.BlockSpec(memory_space=pltpu.SMEM), vmem],
        out_specs=vmem,
        scratch_shapes=[pltpu.VMEM((2, padded, width), F32)],
        compiler_params=pltpu.CompilerParams(vmem_limit_bytes=32 * 2**20),
        cost_estimate=pl.CostEstimate(
            flops=6 * wrows * 4 * width * 256, bytes_accessed=2**19, transcendentals=0
        ),
    )(turn.reshape(1), parts)


def swap_kernel(mask_ref, x_ref, g_ref, send_ref):
    tokens, feats = x_ref.shape
    span = tokens // 2
    lanes = feats // tokens
    deep = HALF // lanes
    skip = mask_ref[0] == 0
    low_half = mask_ref[3] == 0
    for seq in range(2):
        source = jnp.where(skip, 1 - seq, seq)
        rows = pl.ds(pl.multiple_of(source * span, span), span)
        send_ref[seq * span : (seq + 1) * span] = x_ref[rows]
    g = jnp.where(low_half, g_ref[HALF:].astype(F32), g_ref[:HALF].astype(F32))
    g0 = jnp.where(skip, g[:, span:], g[:, :span])
    g1 = jnp.where(skip, g[:, :span], g[:, span:])
    g = jnp.concatenate([g0, g1], axis=1).astype(BF16)
    for part in range(lanes):
        send_ref[tokens:, part * tokens : (part + 1) * tokens] = g[part * deep : (part + 1) * deep]


def prepare_swap(state, x, g):
    tokens, feats = x.shape
    vmem = pl.BlockSpec(memory_space=pltpu.VMEM)
    return pl.pallas_call(
        swap_kernel,
        out_shape=jax.ShapeDtypeStruct((tokens + HALF * tokens // feats, feats), BF16),
        in_specs=[pl.BlockSpec(memory_space=pltpu.SMEM), vmem, vmem],
        out_specs=vmem,
        compiler_params=pltpu.CompilerParams(vmem_limit_bytes=32 * 2**20),
        cost_estimate=pl.CostEstimate(flops=2**18, bytes_accessed=2**19, transcendentals=0),
    )(state, x, g)


def compact_kernel(mask_ref, x_ref, g_ref, recv_ref, x_out, g_out):
    tokens, feats = x_ref.shape
    span = tokens // 2
    lanes = feats // tokens
    deep = HALF // lanes
    count = mask_ref[0] + mask_ref[1]
    skip = jnp.where(mask_ref[0] == 0, 1, 0)
    left = mask_ref[2] == 0
    two = count == 2
    some = count >= 1
    right_some = jnp.logical_and(jnp.logical_not(left), some)
    mine = (jnp.logical_or(jnp.logical_and(left, some), two), jnp.logical_or(two, right_some))
    own_at = (jnp.where(two, 0, skip), jnp.where(jnp.logical_or(left, two), 1, skip))
    other_at = (0, jnp.where(count == 1, 0, 1))
    low_half = mask_ref[3] == 0
    own = jnp.where(low_half, g_ref[:HALF].astype(F32), g_ref[HALF:].astype(F32))
    other = jnp.concatenate(
        [
            recv_ref[tokens:, part * tokens : (part + 1) * tokens].astype(F32)
            for part in range(lanes)
        ],
        axis=0,
    )
    for slot in range(2):
        here = slice(slot * span, (slot + 1) * span)
        own_rows = pl.ds(pl.multiple_of(own_at[slot] * span, span), span)
        other_rows = pl.ds(pl.multiple_of(other_at[slot] * span, span), span)

        @pl.when(mine[slot])
        def _():
            x_out[here] = x_ref[own_rows]
            g_out[:, here] = jnp.where(own_at[slot] == 0, own[:, :span], own[:, span:]).astype(BF16)

        @pl.when(jnp.logical_not(mine[slot]))
        def _():
            x_out[here] = recv_ref[other_rows]
            g_out[:, here] = jnp.where(other_at[slot] == 0, other[:, :span], other[:, span:]).astype(BF16)


def compact_pair(state, x, g, received):
    tokens, feats = x.shape
    vmem = pl.BlockSpec(memory_space=pltpu.VMEM)
    return pl.pallas_call(
        compact_kernel,
        out_shape=(
            jax.ShapeDtypeStruct((tokens, feats), BF16),
            jax.ShapeDtypeStruct((HALF, tokens), BF16),
        ),
        in_specs=[pl.BlockSpec(memory_space=pltpu.SMEM), vmem, vmem, vmem],
        out_specs=(vmem, vmem),
        compiler_params=pltpu.CompilerParams(vmem_limit_bytes=32 * 2**20),
        cost_estimate=pl.CostEstimate(flops=2**18, bytes_accessed=2**19, transcendentals=0),
    )(state, x, g, received)


def on_device(x, w, adjoint, mask):
    seqs = mask.shape[0]
    tokens, feats = x.shape
    wrows, cols = w.shape
    n_z = lax.axis_size("z")
    n_mp = lax.axis_size("mp")
    half = cols // n_mp // 2
    side = lax.axis_index("pair")
    core = lax.axis_index("core")
    turn = lax.axis_index("mp") // (n_mp // 2)
    hand = jnp.bitwise_xor(side, turn)
    groups = [
        [(s ^ (g // (n_mp // 2))) * n_mp + g for g in range(n_mp)] for s in range(2)
    ]

    count = jnp.sum(mask)

    def unpack(value):
        lead = value.shape[:-2]
        value = value.reshape(*lead, 2, wrows, n_mp * half // 2)
        return jnp.swapaxes(value, -3, -2).reshape(*lead, wrows, n_mp * half)

    w_mine = lax.all_to_all(spread_weight(turn, w, half, n_z), ("pair", "z"), 0, 0, tiled=True)

    state = jnp.concatenate([mask, jnp.stack([side, hand])])
    g = adjoint.T
    received = swap_pair(prepare_swap(state, x, g))
    x_pair, g_cols = compact_pair(state, x, g, received)

    w_theirs = swap_core(w_mine)
    w_cores = jnp.where(core == 0, jnp.stack([w_mine, w_theirs], 1), jnp.stack([w_theirs, w_mine], 1))
    w_full = unpack(w_cores).reshape(4 * n_z * wrows, n_mp * half)[:feats]

    kv = lax.dot_general(w_full, x_pair, (((0,), (1,)), ((), ())), preferred_element_type=F32)
    kv = kv.astype(BF16).reshape(n_mp, half, tokens)
    both = jnp.concatenate([kv, jnp.broadcast_to(g_cols, (n_mp, half, tokens))], axis=1)
    both = lax.all_to_all(both, ("pair", "mp"), 0, 0, axis_index_groups=groups, tiled=True)

    dw_mine, dw_theirs = weight_blocks(core, both, x_pair, 2 * n_z, wrows)
    dw_theirs, both = lax.optimization_barrier((dw_theirs, both))
    dw_sum = dw_mine + swap_core(dw_theirs).astype(F32)

    send, keep, kv = return_parts(both, w_full)
    received = swap_pair(send)
    dw_send, keep = lax.optimization_barrier((dw_sum.astype(BF16), keep))
    dw_parts = lax.all_to_all(dw_send, ("pair", "z"), 0, 0, tiled=True)
    weight_grad = sum_blocks(turn, dw_parts, half, wrows)

    start = jnp.where(side == 0, 0, 2 - count)
    slots = jnp.minimum(jnp.stack([start, start + mask[0]]), 1)
    place = jnp.concatenate([mask, slots, hand.reshape(1)])
    activation_grad, kv_home = bring_home(place, keep, received, kv, seqs)
    return kv_home.T, activation_grad, weight_grad


def solution(mesh):
    n_dp, n_mp = mesh.devices.shape
    names = ("pair", "z", "core", "mp")
    split = Mesh(mesh.devices.reshape(2, n_dp // 4, 2, n_mp), names)
    dp = ("pair", "z", "core")
    return jax.shard_map(
        on_device,
        mesh=split,
        in_specs=(P(dp, "mp"), P((*dp, "mp"), None), P(dp, "mp"), P(dp)),
        out_specs=(P(dp, "mp"), P(dp, "mp"), P((*dp, "mp"), None)),
        check_vma=False,
    )
```

```python
import functools

import jax
import jax.numpy as jnp
from jax import lax
from jax.experimental import pallas as pl
from jax.experimental.pallas import tpu as pltpu
from jax.sharding import Mesh, PartitionSpec as P

BF16 = jnp.bfloat16
F32 = jnp.float32
SWAP = [(0, 1), (1, 0)]
HALF = 32


def swap_pair(value):
    return lax.ppermute(value, "pair", SWAP)


def swap_core(value):
    return lax.ppermute(value, "core", SWAP)


def weight_kernel(blocks, wrows, core_ref, both_ref, x_ref, mine_ref, theirs_ref, acc_ref, own_ref, stage_ref):
    tokens, feats = x_ref.shape
    n_mp, rows, _ = both_ref.shape
    half = rows // 2
    width = acc_ref.shape[2]
    groups = width // half
    first_core = core_ref[0] == 0
    x_turned = x_ref[...].T
    for part in range(2):
        g = both_ref[part * groups : (part + 1) * groups, half:, :].reshape(width, tokens)
        acc_ref[part, :feats] = lax.dot_general(
            x_turned, g, (((1,), (1,)), ((), ())), preferred_element_type=F32
        )
        acc_ref[part, feats:] = jnp.zeros_like(acc_ref[part, feats:])
    stage_ref[:, 2 * wrows :] = jnp.zeros_like(stage_ref[:, 2 * wrows :])
    for block in range(blocks):
        for part in range(2):
            top = acc_ref[part, pl.ds(2 * block * wrows, wrows)]
            bottom = acc_ref[part, pl.ds((2 * block + 1) * wrows, wrows)]
            own_ref[block, pl.ds(part * wrows, wrows)] = jnp.where(first_core, top, bottom)
            stage_ref[block, pl.ds(part * wrows, wrows)] = jnp.where(first_core, bottom, top)
        mine_ref[block] = own_ref[block, : 2 * wrows].astype(BF16)
        theirs_ref[block] = stage_ref[block, : 2 * wrows].astype(BF16)


def weight_blocks(core, both, x_pair, blocks, wrows):
    tokens, feats = x_pair.shape
    n_mp, rows, _ = both.shape
    width = n_mp * rows // 4
    vmem = pl.BlockSpec(memory_space=pltpu.VMEM)
    padded = -(-2 * wrows // 16) * 16
    shape = (blocks, 2 * wrows, width)
    return pl.pallas_call(
        functools.partial(weight_kernel, blocks, wrows),
        out_shape=(jax.ShapeDtypeStruct(shape, BF16), jax.ShapeDtypeStruct(shape, BF16)),
        in_specs=[pl.BlockSpec(memory_space=pltpu.SMEM), vmem, vmem],
        out_specs=(vmem, vmem),
        scratch_shapes=[
            pltpu.VMEM((2, 2 * blocks * wrows, width), F32),
            pltpu.VMEM((blocks, padded, width), F32),
            pltpu.VMEM((blocks, padded, width), F32),
        ],
        compiler_params=pltpu.CompilerParams(vmem_limit_bytes=32 * 2**20),
        cost_estimate=pl.CostEstimate(
            flops=2 * feats * tokens * 2 * width, bytes_accessed=3 * 2**20, transcendentals=0
        ),
    )(core.reshape(1), both, x_pair)


def return_kernel(both_ref, w_ref, send_ref, keep_ref, kv_ref):
    n_mp, rows, tokens = both_ref.shape
    feats = w_ref.shape[0]
    half = rows // 2
    g = both_ref[:, half:, :].reshape(n_mp * half, tokens)
    dx = lax.dot_general(g.T, w_ref[...], (((1,), (1,)), ((), ())), preferred_element_type=F32)
    dx = dx.astype(BF16)
    keep_ref[...] = dx
    send_ref[:tokens] = dx
    kv = jnp.sum(both_ref[:, :half, :].astype(F32), axis=0).astype(BF16)
    kv_ref[...] = kv
    lanes = feats // tokens
    deep = half // lanes
    for part in range(lanes):
        send_ref[tokens:, part * tokens : (part + 1) * tokens] = kv[part * deep : (part + 1) * deep]


def return_parts(both, w_full):
    n_mp, rows, tokens = both.shape
    feats, width = w_full.shape
    half = rows // 2
    vmem = pl.BlockSpec(memory_space=pltpu.VMEM)
    return pl.pallas_call(
        return_kernel,
        out_shape=(
            jax.ShapeDtypeStruct((tokens + half * tokens // feats, feats), BF16),
            jax.ShapeDtypeStruct((tokens, feats), BF16),
            jax.ShapeDtypeStruct((half, tokens), BF16),
        ),
        in_specs=[vmem, vmem],
        out_specs=(vmem, vmem, vmem),
        compiler_params=pltpu.CompilerParams(vmem_limit_bytes=32 * 2**20),
        cost_estimate=pl.CostEstimate(
            flops=2 * feats * tokens * width, bytes_accessed=2 * 2**20, transcendentals=0
        ),
    )(both, w_full)


def home_kernel(seqs, place_ref, keep_ref, recv_ref, kv_ref, dx_ref, out_ref):
    tokens, feats = keep_ref.shape
    half = kv_ref.shape[0]
    span = tokens // seqs
    lanes = feats // tokens
    deep = half // lanes
    left = place_ref[2 * seqs] == 0
    own = kv_ref[...].astype(F32)
    other = jnp.concatenate(
        [
            recv_ref[tokens:, part * tokens : (part + 1) * tokens].astype(F32)
            for part in range(lanes)
        ],
        axis=0,
    )
    low = jnp.where(left, own, other)
    high = jnp.where(left, other, own)
    for seq in range(seqs):
        alive = place_ref[seq] != 0
        slot = place_ref[seqs + seq]
        rows = pl.ds(pl.multiple_of(slot * span, span), span)
        total = keep_ref[rows].astype(F32) + recv_ref[rows].astype(F32)
        here = slice(seq * span, (seq + 1) * span)
        dx_ref[here] = jnp.where(alive, total, 0.0).astype(BF16)
        for at, value in ((0, low), (half, high)):
            picked = jnp.where(slot == 0, value[:, :span], value[:, span : 2 * span])
            out_ref[at : at + half, here] = jnp.where(alive, picked, 0.0).astype(BF16)


def bring_home(place, keep, received, kv, seqs):
    tokens, feats = keep.shape
    half = kv.shape[0]
    vmem = pl.BlockSpec(memory_space=pltpu.VMEM)
    return pl.pallas_call(
        functools.partial(home_kernel, seqs),
        out_shape=(
            jax.ShapeDtypeStruct((tokens, feats), BF16),
            jax.ShapeDtypeStruct((2 * half, tokens), BF16),
        ),
        in_specs=[pl.BlockSpec(memory_space=pltpu.SMEM), vmem, vmem, vmem],
        out_specs=(vmem, vmem),
        compiler_params=pltpu.CompilerParams(vmem_limit_bytes=32 * 2**20),
        cost_estimate=pl.CostEstimate(flops=tokens * feats, bytes_accessed=2**20, transcendentals=0),
    )(place, keep, received, kv)


def halves_matrix(size, half, transposed):
    here = lax.broadcasted_iota(jnp.int32, (size, size), 1 if transposed else 0)
    there = lax.broadcasted_iota(jnp.int32, (size, size), 0 if transposed else 1)
    rest = there % (size // 2)
    source = (rest // half) * (2 * half) + (there // (size // 2)) * half + rest % half
    return (here == source).astype(F32).astype(BF16)


def spread_kernel(half, n_z, turn_ref, w_ref, out_ref, stage_ref):
    wrows, cols = w_ref.shape
    width = cols // 4
    size = min(256, 2 * width)
    matrix = halves_matrix(size, half, False)
    stage_ref[:, 2 * wrows :] = jnp.zeros_like(stage_ref[:, 2 * wrows :])
    for part in range(2):
        for group in range(2 * width // size):
            at = part * 2 * width + group * size
            split = jnp.dot(w_ref[:, at : at + size], matrix, preferred_element_type=F32)
            lanes = slice(group * size // 2, (group + 1) * size // 2)
            for side in range(2):
                stage_ref[side, pl.ds(part * wrows, wrows), lanes] = split[
                    :, side * size // 2 : (side + 1) * size // 2
                ]
    turned = turn_ref[0] != 0
    low, high = stage_ref[0, : 2 * wrows], stage_ref[1, : 2 * wrows]
    for side, block in enumerate((jnp.where(turned, high, low), jnp.where(turned, low, high))):
        block = block.astype(BF16)
        for z in range(n_z):
            out_ref[side * n_z + z] = block


def spread_weight(turn, w, half, n_z):
    wrows, cols = w.shape
    vmem = pl.BlockSpec(memory_space=pltpu.VMEM)
    padded = -(-2 * wrows // 16) * 16
    return pl.pallas_call(
        functools.partial(spread_kernel, half, n_z),
        out_shape=jax.ShapeDtypeStruct((2 * n_z, 2 * wrows, cols // 4), BF16),
        in_specs=[pl.BlockSpec(memory_space=pltpu.SMEM), vmem],
        out_specs=vmem,
        scratch_shapes=[pltpu.VMEM((2, padded, cols // 4), F32)],
        compiler_params=pltpu.CompilerParams(vmem_limit_bytes=32 * 2**20),
        cost_estimate=pl.CostEstimate(
            flops=2 * wrows * cols * 256, bytes_accessed=2**19, transcendentals=0
        ),
    )(turn.reshape(1), w)


def sum_kernel(half, turn_ref, parts_ref, out_ref, stage_ref):
    blocks = parts_ref.shape[0]
    wrows, cols = out_ref.shape
    width = cols // 4
    size = min(256, 2 * width)
    matrix = halves_matrix(size, half, True)
    sums = []
    for side in range(2):
        first = side * blocks // 2
        total = parts_ref[first].astype(F32)
        for block in range(first + 1, first + blocks // 2):
            total = total + parts_ref[block].astype(F32)
        sums.append(total)
    turned = turn_ref[0] != 0
    stage_ref[0, pl.ds(0, 2 * wrows)] = jnp.where(turned, sums[1], sums[0])
    stage_ref[1, pl.ds(0, 2 * wrows)] = jnp.where(turned, sums[0], sums[1])
    for part in range(2):
        for group in range(2 * width // size):
            lanes = slice(group * size // 2, (group + 1) * size // 2)
            both = jnp.concatenate(
                [stage_ref[side, pl.ds(part * wrows, wrows), lanes] for side in range(2)], axis=1
            )
            top = both.astype(BF16)
            rest = both - top.astype(F32)
            middle = rest.astype(BF16)
            bottom = (rest - middle.astype(F32)).astype(BF16)
            value = jnp.dot(top, matrix, preferred_element_type=F32)
            value = value + jnp.dot(middle, matrix, preferred_element_type=F32)
            value = value + jnp.dot(bottom, matrix, preferred_element_type=F32)
            at = part * 2 * width + group * size
            out_ref[:, at : at + size] = value


def sum_blocks(turn, parts, half, wrows):
    width = parts.shape[2]
    vmem = pl.BlockSpec(memory_space=pltpu.VMEM)
    padded = -(-2 * wrows // 16) * 16
    return pl.pallas_call(
        functools.partial(sum_kernel, half),
        out_shape=jax.ShapeDtypeStruct((wrows, 4 * width), F32),
        in_specs=[pl.BlockSpec(memory_space=pltpu.SMEM), vmem],
        out_specs=vmem,
        scratch_shapes=[pltpu.VMEM((2, padded, width), F32)],
        compiler_params=pltpu.CompilerParams(vmem_limit_bytes=32 * 2**20),
        cost_estimate=pl.CostEstimate(
            flops=6 * wrows * 4 * width * 256, bytes_accessed=2**19, transcendentals=0
        ),
    )(turn.reshape(1), parts)


def swap_kernel(mask_ref, x_ref, g_ref, send_ref):
    tokens, feats = x_ref.shape
    span = tokens // 2
    lanes = feats // tokens
    deep = HALF // lanes
    skip = mask_ref[0] == 0
    low_half = mask_ref[3] == 0
    for seq in range(2):
        source = jnp.where(skip, 1 - seq, seq)
        rows = pl.ds(pl.multiple_of(source * span, span), span)
        send_ref[seq * span : (seq + 1) * span] = x_ref[rows]
    g = jnp.where(low_half, g_ref[HALF:].astype(F32), g_ref[:HALF].astype(F32))
    g0 = jnp.where(skip, g[:, span:], g[:, :span])
    g1 = jnp.where(skip, g[:, :span], g[:, span:])
    g = jnp.concatenate([g0, g1], axis=1).astype(BF16)
    for part in range(lanes):
        send_ref[tokens:, part * tokens : (part + 1) * tokens] = g[part * deep : (part + 1) * deep]


def prepare_swap(state, x, g):
    tokens, feats = x.shape
    vmem = pl.BlockSpec(memory_space=pltpu.VMEM)
    return pl.pallas_call(
        swap_kernel,
        out_shape=jax.ShapeDtypeStruct((tokens + HALF * tokens // feats, feats), BF16),
        in_specs=[pl.BlockSpec(memory_space=pltpu.SMEM), vmem, vmem],
        out_specs=vmem,
        compiler_params=pltpu.CompilerParams(vmem_limit_bytes=32 * 2**20),
        cost_estimate=pl.CostEstimate(flops=2**18, bytes_accessed=2**19, transcendentals=0),
    )(state, x, g)


def compact_kernel(mask_ref, x_ref, g_ref, recv_ref, x_out, g_out):
    tokens, feats = x_ref.shape
    span = tokens // 2
    lanes = feats // tokens
    deep = HALF // lanes
    count = mask_ref[0] + mask_ref[1]
    skip = jnp.where(mask_ref[0] == 0, 1, 0)
    left = mask_ref[2] == 0
    two = count == 2
    some = count >= 1
    right_some = jnp.logical_and(jnp.logical_not(left), some)
    mine = (jnp.logical_or(jnp.logical_and(left, some), two), jnp.logical_or(two, right_some))
    own_at = (jnp.where(two, 0, skip), jnp.where(jnp.logical_or(left, two), 1, skip))
    other_at = (0, jnp.where(count == 1, 0, 1))
    low_half = mask_ref[3] == 0
    own = jnp.where(low_half, g_ref[:HALF].astype(F32), g_ref[HALF:].astype(F32))
    other = jnp.concatenate(
        [
            recv_ref[tokens:, part * tokens : (part + 1) * tokens].astype(F32)
            for part in range(lanes)
        ],
        axis=0,
    )
    for slot in range(2):
        here = slice(slot * span, (slot + 1) * span)
        own_rows = pl.ds(pl.multiple_of(own_at[slot] * span, span), span)
        other_rows = pl.ds(pl.multiple_of(other_at[slot] * span, span), span)

        @pl.when(mine[slot])
        def _():
            x_out[here] = x_ref[own_rows]
            g_out[:, here] = jnp.where(own_at[slot] == 0, own[:, :span], own[:, span:]).astype(BF16)

        @pl.when(jnp.logical_not(mine[slot]))
        def _():
            x_out[here] = recv_ref[other_rows]
            g_out[:, here] = jnp.where(other_at[slot] == 0, other[:, :span], other[:, span:]).astype(BF16)


def compact_pair(state, x, g, received):
    tokens, feats = x.shape
    vmem = pl.BlockSpec(memory_space=pltpu.VMEM)
    return pl.pallas_call(
        compact_kernel,
        out_shape=(
            jax.ShapeDtypeStruct((tokens, feats), BF16),
            jax.ShapeDtypeStruct((HALF, tokens), BF16),
        ),
        in_specs=[pl.BlockSpec(memory_space=pltpu.SMEM), vmem, vmem, vmem],
        out_specs=(vmem, vmem),
        compiler_params=pltpu.CompilerParams(vmem_limit_bytes=32 * 2**20),
        cost_estimate=pl.CostEstimate(flops=2**18, bytes_accessed=2**19, transcendentals=0),
    )(state, x, g, received)


def on_device(x, w, adjoint, mask):
    seqs = mask.shape[0]
    tokens, feats = x.shape
    wrows, cols = w.shape
    n_z = lax.axis_size("z")
    n_mp = lax.axis_size("mp")
    half = cols // n_mp // 2
    side = lax.axis_index("pair")
    core = lax.axis_index("core")
    turn = lax.axis_index("mp") // (n_mp // 2)
    hand = jnp.bitwise_xor(side, turn)
    groups = [
        [(s ^ (g // (n_mp // 2))) * n_mp + g for g in range(n_mp)] for s in range(2)
    ]

    count = jnp.sum(mask)

    def unpack(value):
        lead = value.shape[:-2]
        value = value.reshape(*lead, 2, wrows, n_mp * half // 2)
        return jnp.swapaxes(value, -3, -2).reshape(*lead, wrows, n_mp * half)

    w_mine = lax.all_to_all(spread_weight(turn, w, half, n_z), ("pair", "z"), 0, 0, tiled=True)

    state = jnp.concatenate([mask, jnp.stack([side, hand])])
    g = adjoint.T
    received = swap_pair(prepare_swap(state, x, g))
    x_pair, g_cols = compact_pair(state, x, g, received)

    w_theirs = swap_core(w_mine)
    w_cores = jnp.where(core == 0, jnp.stack([w_mine, w_theirs], 1), jnp.stack([w_theirs, w_mine], 1))
    w_full = unpack(w_cores).reshape(4 * n_z * wrows, n_mp * half)[:feats]

    kv = lax.dot_general(w_full, x_pair, (((0,), (1,)), ((), ())), preferred_element_type=F32)
    kv = kv.astype(BF16).reshape(n_mp, half, tokens)
    both = jnp.concatenate([kv, jnp.broadcast_to(g_cols, (n_mp, half, tokens))], axis=1)
    both = lax.all_to_all(both, ("pair", "mp"), 0, 0, axis_index_groups=groups, tiled=True)

    dw_mine, dw_theirs = weight_blocks(core, both, x_pair, 2 * n_z, wrows)
    dw_theirs, both = lax.optimization_barrier((dw_theirs, both))
    dw_sum = dw_mine.astype(F32) + swap_core(dw_theirs).astype(F32)

    send, keep, kv = return_parts(both, w_full)
    received = swap_pair(send)
    dw_send, keep = lax.optimization_barrier((dw_sum.astype(BF16), keep))
    dw_parts = lax.all_to_all(dw_send, ("pair", "z"), 0, 0, tiled=True)
    weight_grad = sum_blocks(turn, dw_parts, half, wrows)

    start = jnp.where(side == 0, 0, 2 - count)
    slots = jnp.minimum(jnp.stack([start, start + mask[0]]), 1)
    place = jnp.concatenate([mask, slots, hand.reshape(1)])
    activation_grad, kv_home = bring_home(place, keep, received, kv, seqs)
    return kv_home.T, activation_grad, weight_grad


def solution(mesh):
    n_dp, n_mp = mesh.devices.shape
    names = ("pair", "z", "core", "mp")
    split = Mesh(mesh.devices.reshape(2, n_dp // 4, 2, n_mp), names)
    dp = ("pair", "z", "core")
    return jax.shard_map(
        on_device,
        mesh=split,
        in_specs=(P(dp, "mp"), P((*dp, "mp"), None), P(dp, "mp"), P(dp)),
        out_specs=(P(dp, "mp"), P(dp, "mp"), P((*dp, "mp"), None)),
        check_vma=False,
    )
```

```python
import functools

import jax
import jax.numpy as jnp
from jax import lax
from jax.experimental import pallas as pl
from jax.experimental.pallas import tpu as pltpu
from jax.sharding import Mesh, PartitionSpec as P

BF16 = jnp.bfloat16
F32 = jnp.float32
SWAP = [(0, 1), (1, 0)]
HALF = 32


def swap_pair(value):
    return lax.ppermute(value, "pair", SWAP)


def swap_core(value):
    return lax.ppermute(value, "core", SWAP)


def weight_kernel(blocks, wrows, core_ref, both_ref, x_ref, mine_ref, theirs_ref, acc_ref, stage_ref):
    tokens, feats = x_ref.shape
    n_mp, rows, _ = both_ref.shape
    half = rows // 2
    width = acc_ref.shape[2]
    groups = width // half
    first_core = core_ref[0] == 0
    x_turned = x_ref[...].T
    for part in range(2):
        g = both_ref[part * groups : (part + 1) * groups, half:, :].reshape(width, tokens)
        acc_ref[part, :feats] = lax.dot_general(
            x_turned, g, (((1,), (1,)), ((), ())), preferred_element_type=F32
        )
        acc_ref[part, feats:] = jnp.zeros_like(acc_ref[part, feats:])
    stage_ref[:, 2 * wrows :] = jnp.zeros_like(stage_ref[:, 2 * wrows :])
    for block in range(blocks):
        ahead, back = block, blocks - 1 - block
        mine = jnp.where(first_core, ahead, back)
        theirs = jnp.where(first_core, back, ahead)
        for part in range(2):
            top = acc_ref[part, pl.ds(2 * block * wrows, wrows)]
            bottom = acc_ref[part, pl.ds((2 * block + 1) * wrows, wrows)]
            mine_ref[mine, pl.ds(part * wrows, wrows)] = jnp.where(first_core, top, bottom)
            stage_ref[block, pl.ds(part * wrows, wrows)] = jnp.where(first_core, bottom, top)
        theirs_ref[theirs] = stage_ref[block, : 2 * wrows].astype(BF16)


def weight_blocks(core, both, x_pair, blocks, wrows):
    tokens, feats = x_pair.shape
    n_mp, rows, _ = both.shape
    width = n_mp * rows // 4
    vmem = pl.BlockSpec(memory_space=pltpu.VMEM)
    padded = -(-2 * wrows // 16) * 16
    shape = (blocks, 2 * wrows, width)
    return pl.pallas_call(
        functools.partial(weight_kernel, blocks, wrows),
        out_shape=(jax.ShapeDtypeStruct(shape, F32), jax.ShapeDtypeStruct(shape, BF16)),
        in_specs=[pl.BlockSpec(memory_space=pltpu.SMEM), vmem, vmem],
        out_specs=(vmem, vmem),
        scratch_shapes=[
            pltpu.VMEM((2, 2 * blocks * wrows, width), F32),
            pltpu.VMEM((blocks, padded, width), F32),
        ],
        compiler_params=pltpu.CompilerParams(vmem_limit_bytes=32 * 2**20),
        cost_estimate=pl.CostEstimate(
            flops=2 * feats * tokens * 2 * width, bytes_accessed=3 * 2**20, transcendentals=0
        ),
    )(core.reshape(1), both, x_pair)


def return_kernel(both_ref, w_ref, send_ref, keep_ref, kv_ref):
    n_mp, rows, tokens = both_ref.shape
    feats = w_ref.shape[0]
    half = rows // 2
    g = both_ref[:, half:, :].reshape(n_mp * half, tokens)
    dx = lax.dot_general(g.T, w_ref[...], (((1,), (1,)), ((), ())), preferred_element_type=F32)
    keep_ref[...] = dx
    send_ref[:tokens] = dx.astype(BF16)
    kv = jnp.sum(both_ref[:, :half, :].astype(F32), axis=0).astype(BF16)
    kv_ref[...] = kv
    lanes = feats // tokens
    deep = half // lanes
    for part in range(lanes):
        send_ref[tokens:, part * tokens : (part + 1) * tokens] = kv[part * deep : (part + 1) * deep]


def return_parts(both, w_full):
    n_mp, rows, tokens = both.shape
    feats, width = w_full.shape
    half = rows // 2
    vmem = pl.BlockSpec(memory_space=pltpu.VMEM)
    return pl.pallas_call(
        return_kernel,
        out_shape=(
            jax.ShapeDtypeStruct((tokens + half * tokens // feats, feats), BF16),
            jax.ShapeDtypeStruct((tokens, feats), F32),
            jax.ShapeDtypeStruct((half, tokens), BF16),
        ),
        in_specs=[vmem, vmem],
        out_specs=(vmem, vmem, vmem),
        compiler_params=pltpu.CompilerParams(vmem_limit_bytes=32 * 2**20),
        cost_estimate=pl.CostEstimate(
            flops=2 * feats * tokens * width, bytes_accessed=2 * 2**20, transcendentals=0
        ),
    )(both, w_full)


def home_kernel(seqs, place_ref, keep_ref, recv_ref, kv_ref, dx_ref, out_ref):
    tokens, feats = keep_ref.shape
    half = kv_ref.shape[0]
    span = tokens // seqs
    lanes = feats // tokens
    deep = half // lanes
    left = place_ref[2 * seqs] == 0
    own = kv_ref[...].astype(F32)
    other = jnp.concatenate(
        [
            recv_ref[tokens:, part * tokens : (part + 1) * tokens].astype(F32)
            for part in range(lanes)
        ],
        axis=0,
    )
    low = jnp.where(left, own, other)
    high = jnp.where(left, other, own)
    for seq in range(seqs):
        alive = place_ref[seq] != 0
        slot = place_ref[seqs + seq]
        rows = pl.ds(pl.multiple_of(slot * span, span), span)
        total = keep_ref[rows] + recv_ref[rows].astype(F32)
        here = slice(seq * span, (seq + 1) * span)
        dx_ref[here] = jnp.where(alive, total, 0.0).astype(BF16)
        for at, value in ((0, low), (half, high)):
            picked = jnp.where(slot == 0, value[:, :span], value[:, span : 2 * span])
            out_ref[at : at + half, here] = jnp.where(alive, picked, 0.0).astype(BF16)


def bring_home(place, keep, received, kv, seqs):
    tokens, feats = keep.shape
    half = kv.shape[0]
    vmem = pl.BlockSpec(memory_space=pltpu.VMEM)
    return pl.pallas_call(
        functools.partial(home_kernel, seqs),
        out_shape=(
            jax.ShapeDtypeStruct((tokens, feats), BF16),
            jax.ShapeDtypeStruct((2 * half, tokens), BF16),
        ),
        in_specs=[pl.BlockSpec(memory_space=pltpu.SMEM), vmem, vmem, vmem],
        out_specs=(vmem, vmem),
        compiler_params=pltpu.CompilerParams(vmem_limit_bytes=32 * 2**20),
        cost_estimate=pl.CostEstimate(flops=tokens * feats, bytes_accessed=2**20, transcendentals=0),
    )(place, keep, received, kv)


def halves_matrix(size, half, transposed):
    here = lax.broadcasted_iota(jnp.int32, (size, size), 1 if transposed else 0)
    there = lax.broadcasted_iota(jnp.int32, (size, size), 0 if transposed else 1)
    rest = there % (size // 2)
    source = (rest // half) * (2 * half) + (there // (size // 2)) * half + rest % half
    return (here == source).astype(F32).astype(BF16)


def spread_kernel(half, n_z, turn_ref, w_ref, out_ref, stage_ref):
    wrows, cols = w_ref.shape
    width = cols // 4
    size = min(256, 2 * width)
    matrix = halves_matrix(size, half, False)
    stage_ref[:, 2 * wrows :] = jnp.zeros_like(stage_ref[:, 2 * wrows :])
    for part in range(2):
        for group in range(2 * width // size):
            at = part * 2 * width + group * size
            split = jnp.dot(w_ref[:, at : at + size], matrix, preferred_element_type=F32)
            lanes = slice(group * size // 2, (group + 1) * size // 2)
            for side in range(2):
                stage_ref[side, pl.ds(part * wrows, wrows), lanes] = split[
                    :, side * size // 2 : (side + 1) * size // 2
                ]
    turned = turn_ref[0] != 0
    low, high = stage_ref[0, : 2 * wrows], stage_ref[1, : 2 * wrows]
    for side, block in enumerate((jnp.where(turned, high, low), jnp.where(turned, low, high))):
        block = block.astype(BF16)
        for z in range(n_z):
            out_ref[side * n_z + z] = block


def spread_weight(turn, w, half, n_z):
    wrows, cols = w.shape
    vmem = pl.BlockSpec(memory_space=pltpu.VMEM)
    padded = -(-2 * wrows // 16) * 16
    return pl.pallas_call(
        functools.partial(spread_kernel, half, n_z),
        out_shape=jax.ShapeDtypeStruct((2 * n_z, 2 * wrows, cols // 4), BF16),
        in_specs=[pl.BlockSpec(memory_space=pltpu.SMEM), vmem],
        out_specs=vmem,
        scratch_shapes=[pltpu.VMEM((2, padded, cols // 4), F32)],
        compiler_params=pltpu.CompilerParams(vmem_limit_bytes=32 * 2**20),
        cost_estimate=pl.CostEstimate(
            flops=2 * wrows * cols * 256, bytes_accessed=2**19, transcendentals=0
        ),
    )(turn.reshape(1), w)


def sum_kernel(half, turn_ref, parts_ref, out_ref, stage_ref):
    blocks = parts_ref.shape[0]
    wrows, cols = out_ref.shape
    width = cols // 4
    size = min(256, 2 * width)
    matrix = halves_matrix(size, half, True)
    sums = []
    for side in range(2):
        first = side * blocks // 2
        total = parts_ref[first].astype(F32)
        for block in range(first + 1, first + blocks // 2):
            total = total + parts_ref[block].astype(F32)
        sums.append(total)
    turned = turn_ref[0] != 0
    stage_ref[0, pl.ds(0, 2 * wrows)] = jnp.where(turned, sums[1], sums[0])
    stage_ref[1, pl.ds(0, 2 * wrows)] = jnp.where(turned, sums[0], sums[1])
    for part in range(2):
        for group in range(2 * width // size):
            lanes = slice(group * size // 2, (group + 1) * size // 2)
            both = jnp.concatenate(
                [stage_ref[side, pl.ds(part * wrows, wrows), lanes] for side in range(2)], axis=1
            )
            top = both.astype(BF16)
            rest = both - top.astype(F32)
            middle = rest.astype(BF16)
            bottom = (rest - middle.astype(F32)).astype(BF16)
            value = jnp.dot(top, matrix, preferred_element_type=F32)
            value = value + jnp.dot(middle, matrix, preferred_element_type=F32)
            value = value + jnp.dot(bottom, matrix, preferred_element_type=F32)
            at = part * 2 * width + group * size
            out_ref[:, at : at + size] = value


def sum_blocks(turn, parts, half, wrows):
    width = parts.shape[2]
    vmem = pl.BlockSpec(memory_space=pltpu.VMEM)
    padded = -(-2 * wrows // 16) * 16
    return pl.pallas_call(
        functools.partial(sum_kernel, half),
        out_shape=jax.ShapeDtypeStruct((wrows, 4 * width), F32),
        in_specs=[pl.BlockSpec(memory_space=pltpu.SMEM), vmem],
        out_specs=vmem,
        scratch_shapes=[pltpu.VMEM((2, padded, width), F32)],
        compiler_params=pltpu.CompilerParams(vmem_limit_bytes=32 * 2**20),
        cost_estimate=pl.CostEstimate(
            flops=6 * wrows * 4 * width * 256, bytes_accessed=2**19, transcendentals=0
        ),
    )(turn.reshape(1), parts)


def swap_kernel(mask_ref, x_ref, g_ref, send_ref):
    tokens, feats = x_ref.shape
    span = tokens // 2
    lanes = feats // tokens
    deep = HALF // lanes
    skip = mask_ref[0] == 0
    low_half = mask_ref[3] == 0
    for seq in range(2):
        source = jnp.where(skip, 1 - seq, seq)
        rows = pl.ds(pl.multiple_of(source * span, span), span)
        send_ref[seq * span : (seq + 1) * span] = x_ref[rows]
    g = jnp.where(low_half, g_ref[HALF:].astype(F32), g_ref[:HALF].astype(F32))
    g0 = jnp.where(skip, g[:, span:], g[:, :span])
    g1 = jnp.where(skip, g[:, :span], g[:, span:])
    g = jnp.concatenate([g0, g1], axis=1).astype(BF16)
    for part in range(lanes):
        send_ref[tokens:, part * tokens : (part + 1) * tokens] = g[part * deep : (part + 1) * deep]


def prepare_swap(state, x, g):
    tokens, feats = x.shape
    vmem = pl.BlockSpec(memory_space=pltpu.VMEM)
    return pl.pallas_call(
        swap_kernel,
        out_shape=jax.ShapeDtypeStruct((tokens + HALF * tokens // feats, feats), BF16),
        in_specs=[pl.BlockSpec(memory_space=pltpu.SMEM), vmem, vmem],
        out_specs=vmem,
        compiler_params=pltpu.CompilerParams(vmem_limit_bytes=32 * 2**20),
        cost_estimate=pl.CostEstimate(flops=2**18, bytes_accessed=2**19, transcendentals=0),
    )(state, x, g)


def compact_kernel(mask_ref, x_ref, g_ref, recv_ref, x_out, g_out):
    tokens, feats = x_ref.shape
    span = tokens // 2
    lanes = feats // tokens
    deep = HALF // lanes
    count = mask_ref[0] + mask_ref[1]
    skip = jnp.where(mask_ref[0] == 0, 1, 0)
    left = mask_ref[2] == 0
    two = count == 2
    some = count >= 1
    right_some = jnp.logical_and(jnp.logical_not(left), some)
    mine = (jnp.logical_or(jnp.logical_and(left, some), two), jnp.logical_or(two, right_some))
    own_at = (jnp.where(two, 0, skip), jnp.where(jnp.logical_or(left, two), 1, skip))
    other_at = (0, jnp.where(count == 1, 0, 1))
    low_half = mask_ref[3] == 0
    own = jnp.where(low_half, g_ref[:HALF].astype(F32), g_ref[HALF:].astype(F32))
    other = jnp.concatenate(
        [
            recv_ref[tokens:, part * tokens : (part + 1) * tokens].astype(F32)
            for part in range(lanes)
        ],
        axis=0,
    )
    for slot in range(2):
        here = slice(slot * span, (slot + 1) * span)
        own_rows = pl.ds(pl.multiple_of(own_at[slot] * span, span), span)
        other_rows = pl.ds(pl.multiple_of(other_at[slot] * span, span), span)

        @pl.when(mine[slot])
        def _():
            x_out[here] = x_ref[own_rows]
            g_out[:, here] = jnp.where(own_at[slot] == 0, own[:, :span], own[:, span:]).astype(BF16)

        @pl.when(jnp.logical_not(mine[slot]))
        def _():
            x_out[here] = recv_ref[other_rows]
            g_out[:, here] = jnp.where(other_at[slot] == 0, other[:, :span], other[:, span:]).astype(BF16)


def compact_pair(state, x, g, received):
    tokens, feats = x.shape
    vmem = pl.BlockSpec(memory_space=pltpu.VMEM)
    return pl.pallas_call(
        compact_kernel,
        out_shape=(
            jax.ShapeDtypeStruct((tokens, feats), BF16),
            jax.ShapeDtypeStruct((HALF, tokens), BF16),
        ),
        in_specs=[pl.BlockSpec(memory_space=pltpu.SMEM), vmem, vmem, vmem],
        out_specs=(vmem, vmem),
        compiler_params=pltpu.CompilerParams(vmem_limit_bytes=32 * 2**20),
        cost_estimate=pl.CostEstimate(flops=2**18, bytes_accessed=2**19, transcendentals=0),
    )(state, x, g, received)


def on_device(x, w, adjoint, mask):
    seqs = mask.shape[0]
    tokens, feats = x.shape
    wrows, cols = w.shape
    n_z = lax.axis_size("z")
    n_mp = lax.axis_size("mp")
    half = cols // n_mp // 2
    side = lax.axis_index("pair")
    core = lax.axis_index("core")
    turn = lax.axis_index("mp") // (n_mp // 2)
    hand = jnp.bitwise_xor(side, turn)
    groups = [
        [(s ^ (g // (n_mp // 2))) * n_mp + g for g in range(n_mp)] for s in range(2)
    ]

    count = jnp.sum(mask)

    def unpack(value):
        lead = value.shape[:-2]
        value = value.reshape(*lead, 2, wrows, n_mp * half // 2)
        return jnp.swapaxes(value, -3, -2).reshape(*lead, wrows, n_mp * half)

    w_mine = lax.all_to_all(spread_weight(turn, w, half, n_z), ("pair", "z"), 0, 0, tiled=True)

    state = jnp.concatenate([mask, jnp.stack([side, hand])])
    g = adjoint.T
    received = swap_pair(prepare_swap(state, x, g))
    x_pair, g_cols = compact_pair(state, x, g, received)

    w_theirs = swap_core(w_mine)
    w_cores = jnp.where(core == 0, jnp.stack([w_mine, w_theirs], 1), jnp.stack([w_theirs, w_mine], 1))
    w_full = unpack(w_cores).reshape(4 * n_z * wrows, n_mp * half)[:feats]

    kv = lax.dot_general(w_full, x_pair, (((0,), (1,)), ((), ())), preferred_element_type=F32)
    kv = kv.astype(BF16).reshape(n_mp, half, tokens)
    both = jnp.concatenate([kv, jnp.broadcast_to(g_cols, (n_mp, half, tokens))], axis=1)
    both = lax.all_to_all(both, ("pair", "mp"), 0, 0, axis_index_groups=groups, tiled=True)

    dw_mine, dw_theirs = weight_blocks(core, both, x_pair, 2 * n_z, wrows)
    dw_theirs, both = lax.optimization_barrier((dw_theirs, both))
    dw_sum = dw_mine + swap_core(dw_theirs).astype(F32)

    send, keep, kv = return_parts(both, w_full)
    received = swap_pair(send)
    dw_send, keep = lax.optimization_barrier((dw_sum.astype(BF16), keep))
    ahead = [2 * k for k in range(2 * n_z)]
    back = [2 * k + 1 for k in reversed(range(2 * n_z))]
    dw_parts = lax.all_to_all(
        dw_send, ("pair", "z", "core"), 0, 0, axis_index_groups=[ahead, back], tiled=True
    )
    weight_grad = sum_blocks(jnp.bitwise_xor(turn, core), dw_parts, half, wrows)

    start = jnp.where(side == 0, 0, 2 - count)
    slots = jnp.minimum(jnp.stack([start, start + mask[0]]), 1)
    place = jnp.concatenate([mask, slots, hand.reshape(1)])
    activation_grad, kv_home = bring_home(place, keep, received, kv, seqs)
    return kv_home.T, activation_grad, weight_grad


def solution(mesh):
    n_dp, n_mp = mesh.devices.shape
    names = ("pair", "z", "core", "mp")
    split = Mesh(mesh.devices.reshape(2, n_dp // 4, 2, n_mp), names)
    dp = ("pair", "z", "core")
    return jax.shard_map(
        on_device,
        mesh=split,
        in_specs=(P(dp, "mp"), P((*dp, "mp"), None), P(dp, "mp"), P(dp)),
        out_specs=(P(dp, "mp"), P(dp, "mp"), P((*dp, "mp"), None)),
        check_vma=False,
    )
```

```python
import functools

import jax
import jax.numpy as jnp
from jax import lax
from jax.experimental import pallas as pl
from jax.experimental.pallas import tpu as pltpu
from jax.sharding import Mesh, PartitionSpec as P

BF16 = jnp.bfloat16
F32 = jnp.float32
SWAP = [(0, 1), (1, 0)]
HALF = 32


def swap_pair(value):
    return lax.ppermute(value, "pair", SWAP)


def swap_core(value):
    return lax.ppermute(value, "core", SWAP)


def weight_kernel(blocks, wrows, core_ref, both_ref, x_ref, mine_ref, theirs_ref, acc_ref, own_ref, stage_ref):
    tokens, feats = x_ref.shape
    n_mp, rows, _ = both_ref.shape
    half = rows // 2
    width = acc_ref.shape[2]
    groups = width // half
    first_core = core_ref[0] == 0
    x_turned = x_ref[...].T
    for part in range(2):
        g = both_ref[part * groups : (part + 1) * groups, half:, :].reshape(width, tokens)
        acc_ref[part, :feats] = lax.dot_general(
            x_turned, g, (((1,), (1,)), ((), ())), preferred_element_type=F32
        )
        acc_ref[part, feats:] = jnp.zeros_like(acc_ref[part, feats:])
    stage_ref[:, 2 * wrows :] = jnp.zeros_like(stage_ref[:, 2 * wrows :])
    for block in range(blocks):
        for part in range(2):
            top = acc_ref[part, pl.ds(2 * block * wrows, wrows)]
            bottom = acc_ref[part, pl.ds((2 * block + 1) * wrows, wrows)]
            own_ref[block, pl.ds(part * wrows, wrows)] = jnp.where(first_core, top, bottom)
            stage_ref[block, pl.ds(part * wrows, wrows)] = jnp.where(first_core, bottom, top)
        mine_ref[block] = own_ref[block, : 2 * wrows].astype(BF16)
        theirs_ref[block] = stage_ref[block, : 2 * wrows].astype(BF16)


def weight_blocks(core, both, x_pair, blocks, wrows):
    tokens, feats = x_pair.shape
    n_mp, rows, _ = both.shape
    width = n_mp * rows // 4
    vmem = pl.BlockSpec(memory_space=pltpu.VMEM)
    padded = -(-2 * wrows // 16) * 16
    shape = (blocks, 2 * wrows, width)
    return pl.pallas_call(
        functools.partial(weight_kernel, blocks, wrows),
        out_shape=(jax.ShapeDtypeStruct(shape, BF16), jax.ShapeDtypeStruct(shape, BF16)),
        in_specs=[pl.BlockSpec(memory_space=pltpu.SMEM), vmem, vmem],
        out_specs=(vmem, vmem),
        scratch_shapes=[
            pltpu.VMEM((2, 2 * blocks * wrows, width), F32),
            pltpu.VMEM((blocks, padded, width), F32),
            pltpu.VMEM((blocks, padded, width), F32),
        ],
        compiler_params=pltpu.CompilerParams(vmem_limit_bytes=32 * 2**20),
        cost_estimate=pl.CostEstimate(
            flops=2 * feats * tokens * 2 * width, bytes_accessed=3 * 2**20, transcendentals=0
        ),
    )(core.reshape(1), both, x_pair)


def return_kernel(both_ref, w_ref, send_ref, keep_ref, kv_ref):
    n_mp, rows, tokens = both_ref.shape
    feats = w_ref.shape[0]
    half = rows // 2
    g = both_ref[:, half:, :].reshape(n_mp * half, tokens)
    dx = lax.dot_general(g.T, w_ref[...], (((1,), (1,)), ((), ())), preferred_element_type=F32)
    dx = dx.astype(BF16)
    keep_ref[...] = dx
    send_ref[:tokens] = dx
    kv = jnp.sum(both_ref[:, :half, :].astype(F32), axis=0).astype(BF16)
    kv_ref[...] = kv
    lanes = feats // tokens
    deep = half // lanes
    for part in range(lanes):
        send_ref[tokens:, part * tokens : (part + 1) * tokens] = kv[part * deep : (part + 1) * deep]


def return_parts(both, w_full):
    n_mp, rows, tokens = both.shape
    feats, width = w_full.shape
    half = rows // 2
    vmem = pl.BlockSpec(memory_space=pltpu.VMEM)
    return pl.pallas_call(
        return_kernel,
        out_shape=(
            jax.ShapeDtypeStruct((tokens + half * tokens // feats, feats), BF16),
            jax.ShapeDtypeStruct((tokens, feats), BF16),
            jax.ShapeDtypeStruct((half, tokens), BF16),
        ),
        in_specs=[vmem, vmem],
        out_specs=(vmem, vmem, vmem),
        compiler_params=pltpu.CompilerParams(vmem_limit_bytes=32 * 2**20),
        cost_estimate=pl.CostEstimate(
            flops=2 * feats * tokens * width, bytes_accessed=2 * 2**20, transcendentals=0
        ),
    )(both, w_full)


def home_kernel(seqs, place_ref, keep_ref, recv_ref, kv_ref, dx_ref, out_ref):
    tokens, feats = keep_ref.shape
    half = kv_ref.shape[0]
    span = tokens // seqs
    lanes = feats // tokens
    deep = half // lanes
    left = place_ref[2 * seqs] == 0
    own = kv_ref[...].astype(F32)
    other = jnp.concatenate(
        [
            recv_ref[tokens:, part * tokens : (part + 1) * tokens].astype(F32)
            for part in range(lanes)
        ],
        axis=0,
    )
    low = jnp.where(left, own, other)
    high = jnp.where(left, other, own)
    for seq in range(seqs):
        alive = place_ref[seq] != 0
        slot = place_ref[seqs + seq]
        rows = pl.ds(pl.multiple_of(slot * span, span), span)
        total = keep_ref[rows].astype(F32) + recv_ref[rows].astype(F32)
        here = slice(seq * span, (seq + 1) * span)
        dx_ref[here] = jnp.where(alive, total, 0.0).astype(BF16)
        for at, value in ((0, low), (half, high)):
            picked = jnp.where(slot == 0, value[:, :span], value[:, span : 2 * span])
            out_ref[at : at + half, here] = jnp.where(alive, picked, 0.0).astype(BF16)


def bring_home(place, keep, received, kv, seqs):
    tokens, feats = keep.shape
    half = kv.shape[0]
    vmem = pl.BlockSpec(memory_space=pltpu.VMEM)
    return pl.pallas_call(
        functools.partial(home_kernel, seqs),
        out_shape=(
            jax.ShapeDtypeStruct((tokens, feats), BF16),
            jax.ShapeDtypeStruct((2 * half, tokens), BF16),
        ),
        in_specs=[pl.BlockSpec(memory_space=pltpu.SMEM), vmem, vmem, vmem],
        out_specs=(vmem, vmem),
        compiler_params=pltpu.CompilerParams(vmem_limit_bytes=32 * 2**20),
        cost_estimate=pl.CostEstimate(flops=tokens * feats, bytes_accessed=2**20, transcendentals=0),
    )(place, keep, received, kv)


def halves_matrix(size, half, transposed):
    here = lax.broadcasted_iota(jnp.int32, (size, size), 1 if transposed else 0)
    there = lax.broadcasted_iota(jnp.int32, (size, size), 0 if transposed else 1)
    rest = there % (size // 2)
    source = (rest // half) * (2 * half) + (there // (size // 2)) * half + rest % half
    return (here == source).astype(F32).astype(BF16)


def spread_kernel(half, n_z, turn_ref, w_ref, out_ref, stage_ref):
    wrows, cols = w_ref.shape
    width = cols // 4
    size = min(256, 2 * width)
    matrix = halves_matrix(size, half, False)
    stage_ref[:, 2 * wrows :] = jnp.zeros_like(stage_ref[:, 2 * wrows :])
    for part in range(2):
        for group in range(2 * width // size):
            at = part * 2 * width + group * size
            split = jnp.dot(w_ref[:, at : at + size], matrix, preferred_element_type=F32)
            lanes = slice(group * size // 2, (group + 1) * size // 2)
            for side in range(2):
                stage_ref[side, pl.ds(part * wrows, wrows), lanes] = split[
                    :, side * size // 2 : (side + 1) * size // 2
                ]
    turned = turn_ref[0] != 0
    low, high = stage_ref[0, : 2 * wrows], stage_ref[1, : 2 * wrows]
    for side, block in enumerate((jnp.where(turned, high, low), jnp.where(turned, low, high))):
        block = block.astype(BF16)
        for z in range(n_z):
            out_ref[side * n_z + z] = block


def spread_weight(turn, w, half, n_z):
    wrows, cols = w.shape
    vmem = pl.BlockSpec(memory_space=pltpu.VMEM)
    padded = -(-2 * wrows // 16) * 16
    return pl.pallas_call(
        functools.partial(spread_kernel, half, n_z),
        out_shape=jax.ShapeDtypeStruct((2 * n_z, 2 * wrows, cols // 4), BF16),
        in_specs=[pl.BlockSpec(memory_space=pltpu.SMEM), vmem],
        out_specs=vmem,
        scratch_shapes=[pltpu.VMEM((2, padded, cols // 4), F32)],
        compiler_params=pltpu.CompilerParams(vmem_limit_bytes=32 * 2**20),
        cost_estimate=pl.CostEstimate(
            flops=2 * wrows * cols * 256, bytes_accessed=2**19, transcendentals=0
        ),
    )(turn.reshape(1), w)


def sum_kernel(half, turn_ref, parts_ref, out_ref, stage_ref):
    blocks = parts_ref.shape[0]
    wrows, cols = out_ref.shape
    width = cols // 4
    size = min(256, 2 * width)
    matrix = halves_matrix(size, half, True)
    sums = []
    for side in range(2):
        first = side * blocks // 2
        total = parts_ref[first].astype(F32)
        for block in range(first + 1, first + blocks // 2):
            total = total + parts_ref[block].astype(F32)
        sums.append(total)
    turned = turn_ref[0] != 0
    stage_ref[0, pl.ds(0, 2 * wrows)] = jnp.where(turned, sums[1], sums[0])
    stage_ref[1, pl.ds(0, 2 * wrows)] = jnp.where(turned, sums[0], sums[1])
    for part in range(2):
        for group in range(2 * width // size):
            lanes = slice(group * size // 2, (group + 1) * size // 2)
            both = jnp.concatenate(
                [stage_ref[side, pl.ds(part * wrows, wrows), lanes] for side in range(2)], axis=1
            )
            top = both.astype(BF16)
            rest = both - top.astype(F32)
            middle = rest.astype(BF16)
            bottom = (rest - middle.astype(F32)).astype(BF16)
            value = jnp.dot(top, matrix, preferred_element_type=F32)
            value = value + jnp.dot(middle, matrix, preferred_element_type=F32)
            value = value + jnp.dot(bottom, matrix, preferred_element_type=F32)
            at = part * 2 * width + group * size
            out_ref[:, at : at + size] = value


def sum_blocks(turn, parts, half, wrows):
    width = parts.shape[2]
    vmem = pl.BlockSpec(memory_space=pltpu.VMEM)
    padded = -(-2 * wrows // 16) * 16
    return pl.pallas_call(
        functools.partial(sum_kernel, half),
        out_shape=jax.ShapeDtypeStruct((wrows, 4 * width), F32),
        in_specs=[pl.BlockSpec(memory_space=pltpu.SMEM), vmem],
        out_specs=vmem,
        scratch_shapes=[pltpu.VMEM((2, padded, width), F32)],
        compiler_params=pltpu.CompilerParams(vmem_limit_bytes=32 * 2**20),
        cost_estimate=pl.CostEstimate(
            flops=6 * wrows * 4 * width * 256, bytes_accessed=2**19, transcendentals=0
        ),
    )(turn.reshape(1), parts)


def swap_kernel(mask_ref, x_ref, g_ref, send_ref):
    tokens, feats = x_ref.shape
    span = tokens // 2
    lanes = feats // tokens
    deep = HALF // lanes
    skip = mask_ref[0] == 0
    low_half = mask_ref[3] == 0
    for seq in range(2):
        source = jnp.where(skip, 1 - seq, seq)
        rows = pl.ds(pl.multiple_of(source * span, span), span)
        send_ref[seq * span : (seq + 1) * span] = x_ref[rows]
    g = jnp.where(low_half, g_ref[HALF:].astype(F32), g_ref[:HALF].astype(F32))
    g0 = jnp.where(skip, g[:, span:], g[:, :span])
    g1 = jnp.where(skip, g[:, :span], g[:, span:])
    g = jnp.concatenate([g0, g1], axis=1).astype(BF16)
    for part in range(lanes):
        send_ref[tokens:, part * tokens : (part + 1) * tokens] = g[part * deep : (part + 1) * deep]


def prepare_swap(state, x, g):
    tokens, feats = x.shape
    vmem = pl.BlockSpec(memory_space=pltpu.VMEM)
    return pl.pallas_call(
        swap_kernel,
        out_shape=jax.ShapeDtypeStruct((tokens + HALF * tokens // feats, feats), BF16),
        in_specs=[pl.BlockSpec(memory_space=pltpu.SMEM), vmem, vmem],
        out_specs=vmem,
        compiler_params=pltpu.CompilerParams(vmem_limit_bytes=32 * 2**20),
        cost_estimate=pl.CostEstimate(flops=2**18, bytes_accessed=2**19, transcendentals=0),
    )(state, x, g)


def compact_kernel(mask_ref, x_ref, g_ref, recv_ref, x_out, g_out):
    tokens, feats = x_ref.shape
    span = tokens // 2
    lanes = feats // tokens
    deep = HALF // lanes
    count = mask_ref[0] + mask_ref[1]
    skip = jnp.where(mask_ref[0] == 0, 1, 0)
    left = mask_ref[2] == 0
    two = count == 2
    some = count >= 1
    right_some = jnp.logical_and(jnp.logical_not(left), some)
    mine = (jnp.logical_or(jnp.logical_and(left, some), two), jnp.logical_or(two, right_some))
    own_at = (jnp.where(two, 0, skip), jnp.where(jnp.logical_or(left, two), 1, skip))
    other_at = (0, jnp.where(count == 1, 0, 1))
    low_half = mask_ref[3] == 0
    own = jnp.where(low_half, g_ref[:HALF].astype(F32), g_ref[HALF:].astype(F32))
    other = jnp.concatenate(
        [
            recv_ref[tokens:, part * tokens : (part + 1) * tokens].astype(F32)
            for part in range(lanes)
        ],
        axis=0,
    )
    for slot in range(2):
        here = slice(slot * span, (slot + 1) * span)
        own_rows = pl.ds(pl.multiple_of(own_at[slot] * span, span), span)
        other_rows = pl.ds(pl.multiple_of(other_at[slot] * span, span), span)

        @pl.when(mine[slot])
        def _():
            x_out[here] = x_ref[own_rows]
            g_out[:, here] = jnp.where(own_at[slot] == 0, own[:, :span], own[:, span:]).astype(BF16)

        @pl.when(jnp.logical_not(mine[slot]))
        def _():
            x_out[here] = recv_ref[other_rows]
            g_out[:, here] = jnp.where(other_at[slot] == 0, other[:, :span], other[:, span:]).astype(BF16)


def compact_pair(state, x, g, received):
    tokens, feats = x.shape
    vmem = pl.BlockSpec(memory_space=pltpu.VMEM)
    return pl.pallas_call(
        compact_kernel,
        out_shape=(
            jax.ShapeDtypeStruct((tokens, feats), BF16),
            jax.ShapeDtypeStruct((HALF, tokens), BF16),
        ),
        in_specs=[pl.BlockSpec(memory_space=pltpu.SMEM), vmem, vmem, vmem],
        out_specs=(vmem, vmem),
        compiler_params=pltpu.CompilerParams(vmem_limit_bytes=32 * 2**20),
        cost_estimate=pl.CostEstimate(flops=2**18, bytes_accessed=2**19, transcendentals=0),
    )(state, x, g, received)


def keys_kernel(blocks, wrows, core_ref, mine_ref, theirs_ref, x_ref, g_ref, both_ref, w_ref, acc_ref, stage_ref):
    feats, cols = w_ref.shape
    width = cols // 2
    n_mp, _, tokens = both_ref.shape
    groups = n_mp // 2
    first_core = core_ref[0] == 0
    for block in range(blocks):
        mine = mine_ref[block].astype(F32)
        theirs = theirs_ref[block].astype(F32)
        stage_ref[2 * block, : 2 * wrows] = jnp.where(first_core, mine, theirs)
        stage_ref[2 * block + 1, : 2 * wrows] = jnp.where(first_core, theirs, mine)
    for block in range(2 * blocks):
        for part in range(2):
            rows = pl.ds(block * wrows, wrows)
            acc_ref[part, rows] = stage_ref[block, pl.ds(part * wrows, wrows)]
    x = x_ref[...]
    for part in range(2):
        w = acc_ref[part, :feats].astype(BF16)
        w_ref[:, part * width : (part + 1) * width] = w
        kv = lax.dot_general(w.T, x, (((1,), (1,)), ((), ())), preferred_element_type=F32)
        both_ref[part * groups : (part + 1) * groups, :HALF, :] = kv.astype(BF16).reshape(
            groups, HALF, tokens
        )
    both_ref[:, HALF:, :] = jnp.broadcast_to(g_ref[...][None], (n_mp, HALF, tokens))


def make_keys(core, w_mine, w_theirs, x_pair, g_cols, wrows, n_mp):
    blocks, _, width = w_mine.shape
    tokens, feats = x_pair.shape
    vmem = pl.BlockSpec(memory_space=pltpu.VMEM)
    padded = -(-2 * wrows // 16) * 16
    return pl.pallas_call(
        functools.partial(keys_kernel, blocks, wrows),
        out_shape=(
            jax.ShapeDtypeStruct((n_mp, 2 * HALF, tokens), BF16),
            jax.ShapeDtypeStruct((feats, 2 * width), BF16),
        ),
        in_specs=[pl.BlockSpec(memory_space=pltpu.SMEM), vmem, vmem, vmem, vmem],
        out_specs=(vmem, vmem),
        scratch_shapes=[
            pltpu.VMEM((2, 2 * blocks * wrows, width), F32),
            pltpu.VMEM((2 * blocks, padded, width), F32),
        ],
        compiler_params=pltpu.CompilerParams(vmem_limit_bytes=32 * 2**20),
        cost_estimate=pl.CostEstimate(
            flops=4 * feats * tokens * width, bytes_accessed=2 * 2**20, transcendentals=0
        ),
    )(core.reshape(1), w_mine, w_theirs, x_pair, g_cols)


def add_kernel(mine_ref, theirs_ref, out_ref):
    out_ref[...] = (mine_ref[...].astype(F32) + theirs_ref[...].astype(F32)).astype(BF16)


def add_blocks(mine, theirs):
    vmem = pl.BlockSpec(memory_space=pltpu.VMEM)
    return pl.pallas_call(
        add_kernel,
        out_shape=jax.ShapeDtypeStruct(mine.shape, BF16),
        in_specs=[vmem, vmem],
        out_specs=vmem,
        compiler_params=pltpu.CompilerParams(vmem_limit_bytes=32 * 2**20),
        cost_estimate=pl.CostEstimate(flops=2**18, bytes_accessed=2**20, transcendentals=0),
    )(mine, theirs)


def on_device(x, w, adjoint, mask):
    seqs = mask.shape[0]
    tokens, feats = x.shape
    wrows, cols = w.shape
    n_z = lax.axis_size("z")
    n_mp = lax.axis_size("mp")
    half = cols // n_mp // 2
    side = lax.axis_index("pair")
    core = lax.axis_index("core")
    turn = lax.axis_index("mp") // (n_mp // 2)
    hand = jnp.bitwise_xor(side, turn)
    groups = [
        [(s ^ (g // (n_mp // 2))) * n_mp + g for g in range(n_mp)] for s in range(2)
    ]

    count = jnp.sum(mask)

    w_mine = lax.all_to_all(spread_weight(turn, w, half, n_z), ("pair", "z"), 0, 0, tiled=True)

    state = jnp.concatenate([mask, jnp.stack([side, hand])])
    g = adjoint.T
    received = swap_pair(prepare_swap(state, x, g))
    x_pair, g_cols = compact_pair(state, x, g, received)

    both, w_full = make_keys(core, w_mine, swap_core(w_mine), x_pair, g_cols, wrows, n_mp)
    both = lax.all_to_all(both, ("pair", "mp"), 0, 0, axis_index_groups=groups, tiled=True)

    dw_mine, dw_theirs = weight_blocks(core, both, x_pair, 2 * n_z, wrows)
    dw_theirs, both = lax.optimization_barrier((dw_theirs, both))
    dw_sum = add_blocks(dw_mine, swap_core(dw_theirs))

    send, keep, kv = return_parts(both, w_full)
    received = swap_pair(send)
    dw_send, keep = lax.optimization_barrier((dw_sum, keep))
    dw_parts = lax.all_to_all(dw_send, ("pair", "z"), 0, 0, tiled=True)
    weight_grad = sum_blocks(turn, dw_parts, half, wrows)

    start = jnp.where(side == 0, 0, 2 - count)
    slots = jnp.minimum(jnp.stack([start, start + mask[0]]), 1)
    place = jnp.concatenate([mask, slots, hand.reshape(1)])
    activation_grad, kv_home = bring_home(place, keep, received, kv, seqs)
    return kv_home.T, activation_grad, weight_grad


def solution(mesh):
    n_dp, n_mp = mesh.devices.shape
    names = ("pair", "z", "core", "mp")
    split = Mesh(mesh.devices.reshape(2, n_dp // 4, 2, n_mp), names)
    dp = ("pair", "z", "core")
    return jax.shard_map(
        on_device,
        mesh=split,
        in_specs=(P(dp, "mp"), P((*dp, "mp"), None), P(dp, "mp"), P(dp)),
        out_specs=(P(dp, "mp"), P(dp, "mp"), P((*dp, "mp"), None)),
        check_vma=False,
    )
```

```python
import functools

import jax
import jax.numpy as jnp
from jax import lax
from jax.experimental import pallas as pl
from jax.experimental.pallas import tpu as pltpu
from jax.sharding import Mesh, PartitionSpec as P

BF16 = jnp.bfloat16
F32 = jnp.float32
SWAP = [(0, 1), (1, 0)]
HALF = 32


def swap_pair(value):
    return lax.ppermute(value, "pair", SWAP)


def swap_core(value):
    return lax.ppermute(value, "core", SWAP)


def weight_kernel(blocks, wrows, core_ref, both_ref, x_ref, mine_ref, theirs_ref, acc_ref, own_ref, stage_ref):
    tokens, feats = x_ref.shape
    n_mp, rows, _ = both_ref.shape
    half = rows // 2
    width = acc_ref.shape[2]
    groups = width // half
    first_core = core_ref[0] == 0
    x_turned = x_ref[...].T
    for part in range(2):
        g = both_ref[part * groups : (part + 1) * groups, half:, :].reshape(width, tokens)
        acc_ref[part, :feats] = lax.dot_general(
            x_turned, g, (((1,), (1,)), ((), ())), preferred_element_type=F32
        )
        acc_ref[part, feats:] = jnp.zeros_like(acc_ref[part, feats:])
    stage_ref[:, 2 * wrows :] = jnp.zeros_like(stage_ref[:, 2 * wrows :])
    for block in range(blocks):
        for part in range(2):
            top = acc_ref[part, pl.ds(2 * block * wrows, wrows)]
            bottom = acc_ref[part, pl.ds((2 * block + 1) * wrows, wrows)]
            own_ref[block, pl.ds(part * wrows, wrows)] = jnp.where(first_core, top, bottom)
            stage_ref[block, pl.ds(part * wrows, wrows)] = jnp.where(first_core, bottom, top)
        mine_ref[block] = own_ref[block, : 2 * wrows].astype(BF16)
        theirs_ref[block] = stage_ref[block, : 2 * wrows].astype(BF16)


def weight_blocks(core, both, x_pair, blocks, wrows):
    tokens, feats = x_pair.shape
    n_mp, rows, _ = both.shape
    width = n_mp * rows // 4
    vmem = pl.BlockSpec(memory_space=pltpu.VMEM)
    padded = -(-2 * wrows // 16) * 16
    shape = (blocks, 2 * wrows, width)
    return pl.pallas_call(
        functools.partial(weight_kernel, blocks, wrows),
        out_shape=(jax.ShapeDtypeStruct(shape, BF16), jax.ShapeDtypeStruct(shape, BF16)),
        in_specs=[pl.BlockSpec(memory_space=pltpu.SMEM), vmem, vmem],
        out_specs=(vmem, vmem),
        scratch_shapes=[
            pltpu.VMEM((2, 2 * blocks * wrows, width), F32),
            pltpu.VMEM((blocks, padded, width), F32),
            pltpu.VMEM((blocks, padded, width), F32),
        ],
        compiler_params=pltpu.CompilerParams(vmem_limit_bytes=32 * 2**20),
        cost_estimate=pl.CostEstimate(
            flops=2 * feats * tokens * 2 * width, bytes_accessed=3 * 2**20, transcendentals=0
        ),
    )(core.reshape(1), both, x_pair)


def return_kernel(both_ref, w_ref, send_ref, keep_ref, kv_ref):
    n_mp, rows, tokens = both_ref.shape
    feats = w_ref.shape[0]
    half = rows // 2
    g = both_ref[:, half:, :].reshape(n_mp * half, tokens)
    dx = lax.dot_general(g.T, w_ref[...], (((1,), (1,)), ((), ())), preferred_element_type=F32)
    dx = dx.astype(BF16)
    keep_ref[...] = dx
    send_ref[:tokens] = dx
    kv = jnp.sum(both_ref[:, :half, :].astype(F32), axis=0).astype(BF16)
    kv_ref[...] = kv
    lanes = feats // tokens
    deep = half // lanes
    for part in range(lanes):
        send_ref[tokens:, part * tokens : (part + 1) * tokens] = kv[part * deep : (part + 1) * deep]


def return_parts(both, w_full):
    n_mp, rows, tokens = both.shape
    feats, width = w_full.shape
    half = rows // 2
    vmem = pl.BlockSpec(memory_space=pltpu.VMEM)
    return pl.pallas_call(
        return_kernel,
        out_shape=(
            jax.ShapeDtypeStruct((tokens + half * tokens // feats, feats), BF16),
            jax.ShapeDtypeStruct((tokens, feats), BF16),
            jax.ShapeDtypeStruct((half, tokens), BF16),
        ),
        in_specs=[vmem, vmem],
        out_specs=(vmem, vmem, vmem),
        compiler_params=pltpu.CompilerParams(vmem_limit_bytes=32 * 2**20),
        cost_estimate=pl.CostEstimate(
            flops=2 * feats * tokens * width, bytes_accessed=2 * 2**20, transcendentals=0
        ),
    )(both, w_full)


def home_kernel(seqs, place_ref, keep_ref, recv_ref, kv_ref, dx_ref, out_ref, held_ref, sems):
    tokens, feats = keep_ref.shape
    half = kv_ref.shape[0]
    span = tokens // seqs
    lanes = feats // tokens
    deep = half // lanes
    left = place_ref[2 * seqs] == 0
    own = kv_ref[...].astype(F32)
    other = jnp.concatenate(
        [
            recv_ref[tokens:, part * tokens : (part + 1) * tokens].astype(F32)
            for part in range(lanes)
        ],
        axis=0,
    )
    low = jnp.where(left, own, other)
    high = jnp.where(left, other, own)
    copies = []
    for seq in range(seqs):
        alive = place_ref[seq] != 0
        slot = place_ref[seqs + seq]
        rows = pl.ds(pl.multiple_of(slot * span, span), span)
        total = keep_ref[rows].astype(F32) + recv_ref[rows].astype(F32)
        here = slice(seq * span, (seq + 1) * span)
        held_ref[here] = jnp.where(alive, total, 0.0).astype(BF16)
        rows = pl.ds(seq * span, span)
        copies.append(pltpu.make_async_copy(held_ref.at[rows], dx_ref.at[rows], sems.at[seq]))
        copies[-1].start()
        for at, value in ((0, low), (half, high)):
            picked = jnp.where(slot == 0, value[:, :span], value[:, span : 2 * span])
            out_ref[at : at + half, here] = jnp.where(alive, picked, 0.0).astype(BF16)
    for copy in copies:
        copy.wait()


def bring_home(place, keep, received, kv, seqs):
    tokens, feats = keep.shape
    half = kv.shape[0]
    vmem = pl.BlockSpec(memory_space=pltpu.VMEM)
    return pl.pallas_call(
        functools.partial(home_kernel, seqs),
        out_shape=(
            jax.ShapeDtypeStruct((tokens, feats), BF16),
            jax.ShapeDtypeStruct((2 * half, tokens), BF16),
        ),
        in_specs=[pl.BlockSpec(memory_space=pltpu.SMEM), vmem, vmem, vmem],
        out_specs=(pl.BlockSpec(memory_space=pl.ANY), vmem),
        scratch_shapes=[pltpu.VMEM((tokens, feats), BF16), pltpu.SemaphoreType.DMA((seqs,))],
        compiler_params=pltpu.CompilerParams(vmem_limit_bytes=32 * 2**20),
        cost_estimate=pl.CostEstimate(flops=tokens * feats, bytes_accessed=2**20, transcendentals=0),
    )(place, keep, received, kv)


def halves_matrix(size, half, transposed):
    here = lax.broadcasted_iota(jnp.int32, (size, size), 1 if transposed else 0)
    there = lax.broadcasted_iota(jnp.int32, (size, size), 0 if transposed else 1)
    rest = there % (size // 2)
    source = (rest // half) * (2 * half) + (there // (size // 2)) * half + rest % half
    return (here == source).astype(F32).astype(BF16)


def spread_kernel(half, n_z, turn_ref, w_ref, out_ref, stage_ref):
    wrows, cols = w_ref.shape
    width = cols // 4
    size = min(256, 2 * width)
    matrix = halves_matrix(size, half, False)
    stage_ref[:, 2 * wrows :] = jnp.zeros_like(stage_ref[:, 2 * wrows :])
    for part in range(2):
        for group in range(2 * width // size):
            at = part * 2 * width + group * size
            split = jnp.dot(w_ref[:, at : at + size], matrix, preferred_element_type=F32)
            lanes = slice(group * size // 2, (group + 1) * size // 2)
            for side in range(2):
                stage_ref[side, pl.ds(part * wrows, wrows), lanes] = split[
                    :, side * size // 2 : (side + 1) * size // 2
                ]
    turned = turn_ref[0] != 0
    low, high = stage_ref[0, : 2 * wrows], stage_ref[1, : 2 * wrows]
    for side, block in enumerate((jnp.where(turned, high, low), jnp.where(turned, low, high))):
        block = block.astype(BF16)
        for z in range(n_z):
            out_ref[side * n_z + z] = block


def spread_weight(turn, w, half, n_z):
    wrows, cols = w.shape
    vmem = pl.BlockSpec(memory_space=pltpu.VMEM)
    padded = -(-2 * wrows // 16) * 16
    return pl.pallas_call(
        functools.partial(spread_kernel, half, n_z),
        out_shape=jax.ShapeDtypeStruct((2 * n_z, 2 * wrows, cols // 4), BF16),
        in_specs=[pl.BlockSpec(memory_space=pltpu.SMEM), vmem],
        out_specs=vmem,
        scratch_shapes=[pltpu.VMEM((2, padded, cols // 4), F32)],
        compiler_params=pltpu.CompilerParams(vmem_limit_bytes=32 * 2**20),
        cost_estimate=pl.CostEstimate(
            flops=2 * wrows * cols * 256, bytes_accessed=2**19, transcendentals=0
        ),
    )(turn.reshape(1), w)


def sum_kernel(half, turn_ref, parts_ref, out_ref, stage_ref):
    blocks = parts_ref.shape[0]
    wrows, cols = out_ref.shape
    width = cols // 4
    size = min(256, 2 * width)
    matrix = halves_matrix(size, half, True)
    sums = []
    for side in range(2):
        first = side * blocks // 2
        total = parts_ref[first].astype(F32)
        for block in range(first + 1, first + blocks // 2):
            total = total + parts_ref[block].astype(F32)
        sums.append(total)
    turned = turn_ref[0] != 0
    stage_ref[0, pl.ds(0, 2 * wrows)] = jnp.where(turned, sums[1], sums[0])
    stage_ref[1, pl.ds(0, 2 * wrows)] = jnp.where(turned, sums[0], sums[1])
    for part in range(2):
        for group in range(2 * width // size):
            lanes = slice(group * size // 2, (group + 1) * size // 2)
            both = jnp.concatenate(
                [stage_ref[side, pl.ds(part * wrows, wrows), lanes] for side in range(2)], axis=1
            )
            top = both.astype(BF16)
            rest = both - top.astype(F32)
            middle = rest.astype(BF16)
            bottom = (rest - middle.astype(F32)).astype(BF16)
            value = jnp.dot(top, matrix, preferred_element_type=F32)
            value = value + jnp.dot(middle, matrix, preferred_element_type=F32)
            value = value + jnp.dot(bottom, matrix, preferred_element_type=F32)
            at = part * 2 * width + group * size
            out_ref[:, at : at + size] = value


def sum_blocks(turn, parts, half, wrows):
    width = parts.shape[2]
    vmem = pl.BlockSpec(memory_space=pltpu.VMEM)
    padded = -(-2 * wrows // 16) * 16
    return pl.pallas_call(
        functools.partial(sum_kernel, half),
        out_shape=jax.ShapeDtypeStruct((wrows, 4 * width), F32),
        in_specs=[pl.BlockSpec(memory_space=pltpu.SMEM), vmem],
        out_specs=vmem,
        scratch_shapes=[pltpu.VMEM((2, padded, width), F32)],
        compiler_params=pltpu.CompilerParams(vmem_limit_bytes=32 * 2**20),
        cost_estimate=pl.CostEstimate(
            flops=6 * wrows * 4 * width * 256, bytes_accessed=2**19, transcendentals=0
        ),
    )(turn.reshape(1), parts)


def swap_kernel(mask_ref, x_ref, g_ref, send_ref):
    tokens, feats = x_ref.shape
    span = tokens // 2
    lanes = feats // tokens
    deep = HALF // lanes
    skip = mask_ref[0] == 0
    low_half = mask_ref[3] == 0
    for seq in range(2):
        source = jnp.where(skip, 1 - seq, seq)
        rows = pl.ds(pl.multiple_of(source * span, span), span)
        send_ref[seq * span : (seq + 1) * span] = x_ref[rows]
    g = jnp.where(low_half, g_ref[HALF:].astype(F32), g_ref[:HALF].astype(F32))
    g0 = jnp.where(skip, g[:, span:], g[:, :span])
    g1 = jnp.where(skip, g[:, :span], g[:, span:])
    g = jnp.concatenate([g0, g1], axis=1).astype(BF16)
    for part in range(lanes):
        send_ref[tokens:, part * tokens : (part + 1) * tokens] = g[part * deep : (part + 1) * deep]


def prepare_swap(state, x, g):
    tokens, feats = x.shape
    vmem = pl.BlockSpec(memory_space=pltpu.VMEM)
    return pl.pallas_call(
        swap_kernel,
        out_shape=jax.ShapeDtypeStruct((tokens + HALF * tokens // feats, feats), BF16),
        in_specs=[pl.BlockSpec(memory_space=pltpu.SMEM), vmem, vmem],
        out_specs=vmem,
        compiler_params=pltpu.CompilerParams(vmem_limit_bytes=32 * 2**20),
        cost_estimate=pl.CostEstimate(flops=2**18, bytes_accessed=2**19, transcendentals=0),
    )(state, x, g)


def compact_kernel(mask_ref, x_ref, g_ref, recv_ref, x_out, g_out):
    tokens, feats = x_ref.shape
    span = tokens // 2
    lanes = feats // tokens
    deep = HALF // lanes
    count = mask_ref[0] + mask_ref[1]
    skip = jnp.where(mask_ref[0] == 0, 1, 0)
    left = mask_ref[2] == 0
    two = count == 2
    some = count >= 1
    right_some = jnp.logical_and(jnp.logical_not(left), some)
    mine = (jnp.logical_or(jnp.logical_and(left, some), two), jnp.logical_or(two, right_some))
    own_at = (jnp.where(two, 0, skip), jnp.where(jnp.logical_or(left, two), 1, skip))
    other_at = (0, jnp.where(count == 1, 0, 1))
    low_half = mask_ref[3] == 0
    own = jnp.where(low_half, g_ref[:HALF].astype(F32), g_ref[HALF:].astype(F32))
    other = jnp.concatenate(
        [
            recv_ref[tokens:, part * tokens : (part + 1) * tokens].astype(F32)
            for part in range(lanes)
        ],
        axis=0,
    )
    for slot in range(2):
        here = slice(slot * span, (slot + 1) * span)
        own_rows = pl.ds(pl.multiple_of(own_at[slot] * span, span), span)
        other_rows = pl.ds(pl.multiple_of(other_at[slot] * span, span), span)

        @pl.when(mine[slot])
        def _():
            x_out[here] = x_ref[own_rows]
            g_out[:, here] = jnp.where(own_at[slot] == 0, own[:, :span], own[:, span:]).astype(BF16)

        @pl.when(jnp.logical_not(mine[slot]))
        def _():
            x_out[here] = recv_ref[other_rows]
            g_out[:, here] = jnp.where(other_at[slot] == 0, other[:, :span], other[:, span:]).astype(BF16)


def compact_pair(state, x, g, received):
    tokens, feats = x.shape
    vmem = pl.BlockSpec(memory_space=pltpu.VMEM)
    return pl.pallas_call(
        compact_kernel,
        out_shape=(
            jax.ShapeDtypeStruct((tokens, feats), BF16),
            jax.ShapeDtypeStruct((HALF, tokens), BF16),
        ),
        in_specs=[pl.BlockSpec(memory_space=pltpu.SMEM), vmem, vmem, vmem],
        out_specs=(vmem, vmem),
        compiler_params=pltpu.CompilerParams(vmem_limit_bytes=32 * 2**20),
        cost_estimate=pl.CostEstimate(flops=2**18, bytes_accessed=2**19, transcendentals=0),
    )(state, x, g, received)


def keys_kernel(blocks, wrows, core_ref, mine_ref, theirs_ref, x_ref, g_ref, both_ref, w_ref, acc_ref, stage_ref):
    feats, cols = w_ref.shape
    width = cols // 2
    n_mp, _, tokens = both_ref.shape
    groups = n_mp // 2
    first_core = core_ref[0] == 0
    for block in range(blocks):
        mine = mine_ref[block].astype(F32)
        theirs = theirs_ref[block].astype(F32)
        stage_ref[2 * block, : 2 * wrows] = jnp.where(first_core, mine, theirs)
        stage_ref[2 * block + 1, : 2 * wrows] = jnp.where(first_core, theirs, mine)
    for block in range(2 * blocks):
        for part in range(2):
            rows = pl.ds(block * wrows, wrows)
            acc_ref[part, rows] = stage_ref[block, pl.ds(part * wrows, wrows)]
    x = x_ref[...]
    for part in range(2):
        w = acc_ref[part, :feats].astype(BF16)
        w_ref[:, part * width : (part + 1) * width] = w
        kv = lax.dot_general(w.T, x, (((1,), (1,)), ((), ())), preferred_element_type=F32)
        both_ref[part * groups : (part + 1) * groups, :HALF, :] = kv.astype(BF16).reshape(
            groups, HALF, tokens
        )
    both_ref[:, HALF:, :] = jnp.broadcast_to(g_ref[...][None], (n_mp, HALF, tokens))


def make_keys(core, w_mine, w_theirs, x_pair, g_cols, wrows, n_mp):
    blocks, _, width = w_mine.shape
    tokens, feats = x_pair.shape
    vmem = pl.BlockSpec(memory_space=pltpu.VMEM)
    padded = -(-2 * wrows // 16) * 16
    return pl.pallas_call(
        functools.partial(keys_kernel, blocks, wrows),
        out_shape=(
            jax.ShapeDtypeStruct((n_mp, 2 * HALF, tokens), BF16),
            jax.ShapeDtypeStruct((feats, 2 * width), BF16),
        ),
        in_specs=[pl.BlockSpec(memory_space=pltpu.SMEM), vmem, vmem, vmem, vmem],
        out_specs=(vmem, vmem),
        scratch_shapes=[
            pltpu.VMEM((2, 2 * blocks * wrows, width), F32),
            pltpu.VMEM((2 * blocks, padded, width), F32),
        ],
        compiler_params=pltpu.CompilerParams(vmem_limit_bytes=32 * 2**20),
        cost_estimate=pl.CostEstimate(
            flops=4 * feats * tokens * width, bytes_accessed=2 * 2**20, transcendentals=0
        ),
    )(core.reshape(1), w_mine, w_theirs, x_pair, g_cols)


def add_kernel(steps, mine_ref, theirs_ref, out_ref, held_ref, sems):
    size = mine_ref.shape[0] // steps
    copies = []
    for step in range(steps):
        part = slice(step * size, (step + 1) * size)
        held_ref[part] = (mine_ref[part].astype(F32) + theirs_ref[part].astype(F32)).astype(BF16)
        rows = pl.ds(step * size, size)
        copies.append(pltpu.make_async_copy(held_ref.at[rows], out_ref.at[rows], sems.at[step]))
        copies[-1].start()
    for copy in copies:
        copy.wait()


def add_blocks(mine, theirs):
    vmem = pl.BlockSpec(memory_space=pltpu.VMEM)
    return pl.pallas_call(
        functools.partial(add_kernel, 3),
        out_shape=jax.ShapeDtypeStruct(mine.shape, BF16),
        in_specs=[vmem, vmem],
        out_specs=pl.BlockSpec(memory_space=pl.ANY),
        scratch_shapes=[pltpu.VMEM(mine.shape, BF16), pltpu.SemaphoreType.DMA((3,))],
        compiler_params=pltpu.CompilerParams(vmem_limit_bytes=32 * 2**20),
        cost_estimate=pl.CostEstimate(flops=2**18, bytes_accessed=2**20, transcendentals=0),
    )(mine, theirs)


def on_device(x, w, adjoint, mask):
    seqs = mask.shape[0]
    tokens, feats = x.shape
    wrows, cols = w.shape
    n_z = lax.axis_size("z")
    n_mp = lax.axis_size("mp")
    half = cols // n_mp // 2
    side = lax.axis_index("pair")
    core = lax.axis_index("core")
    turn = lax.axis_index("mp") // (n_mp // 2)
    hand = jnp.bitwise_xor(side, turn)
    groups = [
        [(s ^ (g // (n_mp // 2))) * n_mp + g for g in range(n_mp)] for s in range(2)
    ]

    count = jnp.sum(mask)

    w_mine = lax.all_to_all(spread_weight(turn, w, half, n_z), ("pair", "z"), 0, 0, tiled=True)

    state = jnp.concatenate([mask, jnp.stack([side, hand])])
    g = adjoint.T
    received = swap_pair(prepare_swap(state, x, g))
    x_pair, g_cols = compact_pair(state, x, g, received)

    both, w_full = make_keys(core, w_mine, swap_core(w_mine), x_pair, g_cols, wrows, n_mp)
    both = lax.all_to_all(both, ("pair", "mp"), 0, 0, axis_index_groups=groups, tiled=True)

    dw_mine, dw_theirs = weight_blocks(core, both, x_pair, 2 * n_z, wrows)
    dw_theirs, both = lax.optimization_barrier((dw_theirs, both))
    dw_sum = add_blocks(dw_mine, swap_core(dw_theirs))

    send, keep, kv = return_parts(both, w_full)
    received = swap_pair(send)
    dw_send, keep = lax.optimization_barrier((dw_sum, keep))
    dw_parts = lax.all_to_all(dw_send, ("pair", "z"), 0, 0, tiled=True)
    weight_grad = sum_blocks(turn, dw_parts, half, wrows)

    start = jnp.where(side == 0, 0, 2 - count)
    slots = jnp.minimum(jnp.stack([start, start + mask[0]]), 1)
    place = jnp.concatenate([mask, slots, hand.reshape(1)])
    activation_grad, kv_home = bring_home(place, keep, received, kv, seqs)
    return kv_home.T, activation_grad, weight_grad


def solution(mesh):
    n_dp, n_mp = mesh.devices.shape
    names = ("pair", "z", "core", "mp")
    split = Mesh(mesh.devices.reshape(2, n_dp // 4, 2, n_mp), names)
    dp = ("pair", "z", "core")
    return jax.shard_map(
        on_device,
        mesh=split,
        in_specs=(P(dp, "mp"), P((*dp, "mp"), None), P(dp, "mp"), P(dp)),
        out_specs=(P(dp, "mp"), P(dp, "mp"), P((*dp, "mp"), None)),
        check_vma=False,
    )
```

```python
import functools

import jax
import jax.numpy as jnp
from jax import lax
from jax.experimental import pallas as pl
from jax.experimental.pallas import tpu as pltpu
from jax.sharding import Mesh, PartitionSpec as P

BF16 = jnp.bfloat16
F32 = jnp.float32
SWAP = [(0, 1), (1, 0)]
HALF = 32


def swap_pair(value):
    return lax.ppermute(value, "pair", SWAP)


def swap_core(value):
    return lax.ppermute(value, "core", SWAP)


def weight_kernel(blocks, wrows, core_ref, both_ref, x_ref, mine_ref, theirs_ref, acc_ref, own_ref, stage_ref):
    tokens, feats = x_ref.shape
    n_mp, rows, _ = both_ref.shape
    half = rows // 2
    width = acc_ref.shape[2]
    groups = width // half
    first_core = core_ref[0] == 0
    x_turned = x_ref[...].T
    for part in range(2):
        g = both_ref[part * groups : (part + 1) * groups, half:, :].reshape(width, tokens)
        acc_ref[part, :feats] = lax.dot_general(
            x_turned, g, (((1,), (1,)), ((), ())), preferred_element_type=F32
        )
        acc_ref[part, feats:] = jnp.zeros_like(acc_ref[part, feats:])
    stage_ref[:, 2 * wrows :] = jnp.zeros_like(stage_ref[:, 2 * wrows :])
    for block in range(blocks):
        for part in range(2):
            top = acc_ref[part, pl.ds(2 * block * wrows, wrows)]
            bottom = acc_ref[part, pl.ds((2 * block + 1) * wrows, wrows)]
            own_ref[block, pl.ds(part * wrows, wrows)] = jnp.where(first_core, top, bottom)
            stage_ref[block, pl.ds(part * wrows, wrows)] = jnp.where(first_core, bottom, top)
        mine_ref[block] = own_ref[block, : 2 * wrows].astype(BF16)
        theirs_ref[block] = stage_ref[block, : 2 * wrows].astype(BF16)


def weight_blocks(core, both, x_pair, blocks, wrows):
    tokens, feats = x_pair.shape
    n_mp, rows, _ = both.shape
    width = n_mp * rows // 4
    vmem = pl.BlockSpec(memory_space=pltpu.VMEM)
    padded = -(-2 * wrows // 16) * 16
    shape = (blocks, 2 * wrows, width)
    return pl.pallas_call(
        functools.partial(weight_kernel, blocks, wrows),
        out_shape=(jax.ShapeDtypeStruct(shape, BF16), jax.ShapeDtypeStruct(shape, BF16)),
        in_specs=[pl.BlockSpec(memory_space=pltpu.SMEM), vmem, vmem],
        out_specs=(vmem, vmem),
        scratch_shapes=[
            pltpu.VMEM((2, 2 * blocks * wrows, width), F32),
            pltpu.VMEM((blocks, padded, width), F32),
            pltpu.VMEM((blocks, padded, width), F32),
        ],
        compiler_params=pltpu.CompilerParams(vmem_limit_bytes=32 * 2**20),
        cost_estimate=pl.CostEstimate(
            flops=2 * feats * tokens * 2 * width, bytes_accessed=3 * 2**20, transcendentals=0
        ),
    )(core.reshape(1), both, x_pair)


def return_kernel(both_ref, w_ref, send_ref, keep_ref, kv_ref):
    n_mp, rows, tokens = both_ref.shape
    feats = w_ref.shape[0]
    half = rows // 2
    g = both_ref[:, half:, :].reshape(n_mp * half, tokens)
    dx = lax.dot_general(g.T, w_ref[...], (((1,), (1,)), ((), ())), preferred_element_type=F32)
    dx = dx.astype(BF16)
    keep_ref[...] = dx
    send_ref[:tokens] = dx
    kv = jnp.sum(both_ref[:, :half, :].astype(F32), axis=0).astype(BF16)
    kv_ref[...] = kv
    lanes = feats // tokens
    deep = half // lanes
    for part in range(lanes):
        send_ref[tokens:, part * tokens : (part + 1) * tokens] = kv[part * deep : (part + 1) * deep]


def return_parts(both, w_full):
    n_mp, rows, tokens = both.shape
    feats, width = w_full.shape
    half = rows // 2
    vmem = pl.BlockSpec(memory_space=pltpu.VMEM)
    return pl.pallas_call(
        return_kernel,
        out_shape=(
            jax.ShapeDtypeStruct((tokens + half * tokens // feats, feats), BF16),
            jax.ShapeDtypeStruct((tokens, feats), BF16),
            jax.ShapeDtypeStruct((half, tokens), BF16),
        ),
        in_specs=[vmem, vmem],
        out_specs=(vmem, vmem, vmem),
        compiler_params=pltpu.CompilerParams(vmem_limit_bytes=32 * 2**20),
        cost_estimate=pl.CostEstimate(
            flops=2 * feats * tokens * width, bytes_accessed=2 * 2**20, transcendentals=0
        ),
    )(both, w_full)


def home_kernel(seqs, place_ref, keep_ref, recv_ref, kv_ref, dx_ref, out_ref):
    tokens, feats = keep_ref.shape
    half = kv_ref.shape[0]
    span = tokens // seqs
    lanes = feats // tokens
    deep = half // lanes
    left = place_ref[2 * seqs] == 0
    own = kv_ref[...].astype(F32)
    other = jnp.concatenate(
        [
            recv_ref[tokens:, part * tokens : (part + 1) * tokens].astype(F32)
            for part in range(lanes)
        ],
        axis=0,
    )
    low = jnp.where(left, own, other)
    high = jnp.where(left, other, own)
    totals = [
        keep_ref[at : at + span].astype(F32) + recv_ref[at : at + span].astype(F32)
        for at in (0, span)
    ]
    for seq in range(seqs):
        alive = place_ref[seq] != 0
        slot = place_ref[seqs + seq]
        total = jnp.where(slot == 0, totals[0], totals[1])
        here = slice(seq * span, (seq + 1) * span)
        dx_ref[here] = jnp.where(alive, total, 0.0).astype(BF16)
        for at, value in ((0, low), (half, high)):
            picked = jnp.where(slot == 0, value[:, :span], value[:, span : 2 * span])
            out_ref[at : at + half, here] = jnp.where(alive, picked, 0.0).astype(BF16)


def bring_home(place, keep, received, kv, seqs):
    tokens, feats = keep.shape
    half = kv.shape[0]
    vmem = pl.BlockSpec(memory_space=pltpu.VMEM)
    return pl.pallas_call(
        functools.partial(home_kernel, seqs),
        out_shape=(
            jax.ShapeDtypeStruct((tokens, feats), BF16),
            jax.ShapeDtypeStruct((2 * half, tokens), BF16),
        ),
        in_specs=[pl.BlockSpec(memory_space=pltpu.SMEM), vmem, vmem, vmem],
        out_specs=(vmem, vmem),
        compiler_params=pltpu.CompilerParams(vmem_limit_bytes=32 * 2**20),
        cost_estimate=pl.CostEstimate(flops=tokens * feats, bytes_accessed=2**20, transcendentals=0),
    )(place, keep, received, kv)


def halves_matrix(size, half, transposed):
    here = lax.broadcasted_iota(jnp.int32, (size, size), 1 if transposed else 0)
    there = lax.broadcasted_iota(jnp.int32, (size, size), 0 if transposed else 1)
    rest = there % (size // 2)
    source = (rest // half) * (2 * half) + (there // (size // 2)) * half + rest % half
    return (here == source).astype(F32).astype(BF16)


def spread_kernel(half, n_z, turn_ref, w_ref, out_ref, stage_ref):
    wrows, cols = w_ref.shape
    width = cols // 4
    size = min(256, 2 * width)
    matrix = halves_matrix(size, half, False)
    stage_ref[:, 2 * wrows :] = jnp.zeros_like(stage_ref[:, 2 * wrows :])
    for part in range(2):
        for group in range(2 * width // size):
            at = part * 2 * width + group * size
            split = jnp.dot(w_ref[:, at : at + size], matrix, preferred_element_type=F32)
            lanes = slice(group * size // 2, (group + 1) * size // 2)
            for side in range(2):
                stage_ref[side, pl.ds(part * wrows, wrows), lanes] = split[
                    :, side * size // 2 : (side + 1) * size // 2
                ]
    turned = turn_ref[0] != 0
    low, high = stage_ref[0, : 2 * wrows], stage_ref[1, : 2 * wrows]
    for side, block in enumerate((jnp.where(turned, high, low), jnp.where(turned, low, high))):
        block = block.astype(BF16)
        for z in range(n_z):
            out_ref[side * n_z + z] = block


def spread_weight(turn, w, half, n_z):
    wrows, cols = w.shape
    vmem = pl.BlockSpec(memory_space=pltpu.VMEM)
    padded = -(-2 * wrows // 16) * 16
    return pl.pallas_call(
        functools.partial(spread_kernel, half, n_z),
        out_shape=jax.ShapeDtypeStruct((2 * n_z, 2 * wrows, cols // 4), BF16),
        in_specs=[pl.BlockSpec(memory_space=pltpu.SMEM), vmem],
        out_specs=vmem,
        scratch_shapes=[pltpu.VMEM((2, padded, cols // 4), F32)],
        compiler_params=pltpu.CompilerParams(vmem_limit_bytes=32 * 2**20),
        cost_estimate=pl.CostEstimate(
            flops=2 * wrows * cols * 256, bytes_accessed=2**19, transcendentals=0
        ),
    )(turn.reshape(1), w)


def sum_kernel(half, turn_ref, parts_ref, out_ref, stage_ref):
    blocks = parts_ref.shape[0]
    wrows, cols = out_ref.shape
    width = cols // 4
    size = min(256, 2 * width)
    matrix = halves_matrix(size, half, True)
    sums = []
    for side in range(2):
        first = side * blocks // 2
        total = parts_ref[first].astype(F32)
        for block in range(first + 1, first + blocks // 2):
            total = total + parts_ref[block].astype(F32)
        sums.append(total)
    turned = turn_ref[0] != 0
    stage_ref[0, pl.ds(0, 2 * wrows)] = jnp.where(turned, sums[1], sums[0])
    stage_ref[1, pl.ds(0, 2 * wrows)] = jnp.where(turned, sums[0], sums[1])
    for part in range(2):
        for group in range(2 * width // size):
            lanes = slice(group * size // 2, (group + 1) * size // 2)
            both = jnp.concatenate(
                [stage_ref[side, pl.ds(part * wrows, wrows), lanes] for side in range(2)], axis=1
            )
            top = both.astype(BF16)
            rest = both - top.astype(F32)
            middle = rest.astype(BF16)
            bottom = (rest - middle.astype(F32)).astype(BF16)
            value = jnp.dot(top, matrix, preferred_element_type=F32)
            value = value + jnp.dot(middle, matrix, preferred_element_type=F32)
            value = value + jnp.dot(bottom, matrix, preferred_element_type=F32)
            at = part * 2 * width + group * size
            out_ref[:, at : at + size] = value


def sum_blocks(turn, parts, half, wrows):
    width = parts.shape[2]
    vmem = pl.BlockSpec(memory_space=pltpu.VMEM)
    padded = -(-2 * wrows // 16) * 16
    return pl.pallas_call(
        functools.partial(sum_kernel, half),
        out_shape=jax.ShapeDtypeStruct((wrows, 4 * width), F32),
        in_specs=[pl.BlockSpec(memory_space=pltpu.SMEM), vmem],
        out_specs=vmem,
        scratch_shapes=[pltpu.VMEM((2, padded, width), F32)],
        compiler_params=pltpu.CompilerParams(vmem_limit_bytes=32 * 2**20),
        cost_estimate=pl.CostEstimate(
            flops=6 * wrows * 4 * width * 256, bytes_accessed=2**19, transcendentals=0
        ),
    )(turn.reshape(1), parts)


def swap_kernel(mask_ref, x_ref, g_ref, send_ref):
    tokens, feats = x_ref.shape
    span = tokens // 2
    lanes = feats // tokens
    deep = HALF // lanes
    skip = mask_ref[0] == 0
    low_half = mask_ref[3] == 0
    for seq in range(2):
        source = jnp.where(skip, 1 - seq, seq)
        rows = pl.ds(pl.multiple_of(source * span, span), span)
        send_ref[seq * span : (seq + 1) * span] = x_ref[rows]
    g = jnp.where(low_half, g_ref[HALF:].astype(F32), g_ref[:HALF].astype(F32))
    g0 = jnp.where(skip, g[:, span:], g[:, :span])
    g1 = jnp.where(skip, g[:, :span], g[:, span:])
    g = jnp.concatenate([g0, g1], axis=1).astype(BF16)
    for part in range(lanes):
        send_ref[tokens:, part * tokens : (part + 1) * tokens] = g[part * deep : (part + 1) * deep]


def prepare_swap(state, x, g):
    tokens, feats = x.shape
    vmem = pl.BlockSpec(memory_space=pltpu.VMEM)
    return pl.pallas_call(
        swap_kernel,
        out_shape=jax.ShapeDtypeStruct((tokens + HALF * tokens // feats, feats), BF16),
        in_specs=[pl.BlockSpec(memory_space=pltpu.SMEM), vmem, vmem],
        out_specs=vmem,
        compiler_params=pltpu.CompilerParams(vmem_limit_bytes=32 * 2**20),
        cost_estimate=pl.CostEstimate(flops=2**18, bytes_accessed=2**19, transcendentals=0),
    )(state, x, g)


def compact_kernel(mask_ref, x_ref, g_ref, recv_ref, x_out, g_out):
    tokens, feats = x_ref.shape
    span = tokens // 2
    lanes = feats // tokens
    deep = HALF // lanes
    count = mask_ref[0] + mask_ref[1]
    skip = jnp.where(mask_ref[0] == 0, 1, 0)
    left = mask_ref[2] == 0
    two = count == 2
    some = count >= 1
    right_some = jnp.logical_and(jnp.logical_not(left), some)
    mine = (jnp.logical_or(jnp.logical_and(left, some), two), jnp.logical_or(two, right_some))
    own_at = (jnp.where(two, 0, skip), jnp.where(jnp.logical_or(left, two), 1, skip))
    other_at = (0, jnp.where(count == 1, 0, 1))
    low_half = mask_ref[3] == 0
    own = jnp.where(low_half, g_ref[:HALF].astype(F32), g_ref[HALF:].astype(F32))
    other = jnp.concatenate(
        [
            recv_ref[tokens:, part * tokens : (part + 1) * tokens].astype(F32)
            for part in range(lanes)
        ],
        axis=0,
    )
    for slot in range(2):
        here = slice(slot * span, (slot + 1) * span)
        own_rows = pl.ds(pl.multiple_of(own_at[slot] * span, span), span)
        other_rows = pl.ds(pl.multiple_of(other_at[slot] * span, span), span)

        @pl.when(mine[slot])
        def _():
            x_out[here] = x_ref[own_rows]
            g_out[:, here] = jnp.where(own_at[slot] == 0, own[:, :span], own[:, span:]).astype(BF16)

        @pl.when(jnp.logical_not(mine[slot]))
        def _():
            x_out[here] = recv_ref[other_rows]
            g_out[:, here] = jnp.where(other_at[slot] == 0, other[:, :span], other[:, span:]).astype(BF16)


def compact_pair(state, x, g, received):
    tokens, feats = x.shape
    vmem = pl.BlockSpec(memory_space=pltpu.VMEM)
    return pl.pallas_call(
        compact_kernel,
        out_shape=(
            jax.ShapeDtypeStruct((tokens, feats), BF16),
            jax.ShapeDtypeStruct((HALF, tokens), BF16),
        ),
        in_specs=[pl.BlockSpec(memory_space=pltpu.SMEM), vmem, vmem, vmem],
        out_specs=(vmem, vmem),
        compiler_params=pltpu.CompilerParams(vmem_limit_bytes=32 * 2**20),
        cost_estimate=pl.CostEstimate(flops=2**18, bytes_accessed=2**19, transcendentals=0),
    )(state, x, g, received)


def keys_kernel(blocks, wrows, core_ref, mine_ref, theirs_ref, x_ref, g_ref, both_ref, w_ref, acc_ref, stage_ref):
    feats, cols = w_ref.shape
    width = cols // 2
    n_mp, _, tokens = both_ref.shape
    groups = n_mp // 2
    first_core = core_ref[0] == 0
    for block in range(blocks):
        mine = mine_ref[block].astype(F32)
        theirs = theirs_ref[block].astype(F32)
        stage_ref[2 * block, : 2 * wrows] = jnp.where(first_core, mine, theirs)
        stage_ref[2 * block + 1, : 2 * wrows] = jnp.where(first_core, theirs, mine)
    for block in range(2 * blocks):
        for part in range(2):
            rows = pl.ds(block * wrows, wrows)
            acc_ref[part, rows] = stage_ref[block, pl.ds(part * wrows, wrows)]
    x = x_ref[...]
    for part in range(2):
        w = acc_ref[part, :feats].astype(BF16)
        w_ref[:, part * width : (part + 1) * width] = w
        kv = lax.dot_general(w.T, x, (((1,), (1,)), ((), ())), preferred_element_type=F32)
        both_ref[part * groups : (part + 1) * groups, :HALF, :] = kv.astype(BF16).reshape(
            groups, HALF, tokens
        )
    both_ref[:, HALF:, :] = jnp.broadcast_to(g_ref[...][None], (n_mp, HALF, tokens))


def make_keys(core, w_mine, w_theirs, x_pair, g_cols, wrows, n_mp):
    blocks, _, width = w_mine.shape
    tokens, feats = x_pair.shape
    vmem = pl.BlockSpec(memory_space=pltpu.VMEM)
    padded = -(-2 * wrows // 16) * 16
    return pl.pallas_call(
        functools.partial(keys_kernel, blocks, wrows),
        out_shape=(
            jax.ShapeDtypeStruct((n_mp, 2 * HALF, tokens), BF16),
            jax.ShapeDtypeStruct((feats, 2 * width), BF16),
        ),
        in_specs=[pl.BlockSpec(memory_space=pltpu.SMEM), vmem, vmem, vmem, vmem],
        out_specs=(vmem, vmem),
        scratch_shapes=[
            pltpu.VMEM((2, 2 * blocks * wrows, width), F32),
            pltpu.VMEM((2 * blocks, padded, width), F32),
        ],
        compiler_params=pltpu.CompilerParams(vmem_limit_bytes=32 * 2**20),
        cost_estimate=pl.CostEstimate(
            flops=4 * feats * tokens * width, bytes_accessed=2 * 2**20, transcendentals=0
        ),
    )(core.reshape(1), w_mine, w_theirs, x_pair, g_cols)


def add_kernel(mine_ref, theirs_ref, out_ref):
    out_ref[...] = (mine_ref[...].astype(F32) + theirs_ref[...].astype(F32)).astype(BF16)


def add_blocks(mine, theirs):
    vmem = pl.BlockSpec(memory_space=pltpu.VMEM)
    return pl.pallas_call(
        add_kernel,
        out_shape=jax.ShapeDtypeStruct(mine.shape, BF16),
        in_specs=[vmem, vmem],
        out_specs=vmem,
        compiler_params=pltpu.CompilerParams(vmem_limit_bytes=32 * 2**20),
        cost_estimate=pl.CostEstimate(flops=2**18, bytes_accessed=2**20, transcendentals=0),
    )(mine, theirs)


def on_device(x, w, adjoint, mask):
    seqs = mask.shape[0]
    tokens, feats = x.shape
    wrows, cols = w.shape
    n_z = lax.axis_size("z")
    n_mp = lax.axis_size("mp")
    half = cols // n_mp // 2
    side = lax.axis_index("pair")
    core = lax.axis_index("core")
    turn = lax.axis_index("mp") // (n_mp // 2)
    hand = jnp.bitwise_xor(side, turn)
    groups = [
        [(s ^ (g // (n_mp // 2))) * n_mp + g for g in range(n_mp)] for s in range(2)
    ]

    count = jnp.sum(mask)

    w_mine = lax.all_to_all(spread_weight(turn, w, half, n_z), ("pair", "z"), 0, 0, tiled=True)

    state = jnp.concatenate([mask, jnp.stack([side, hand])])
    g = adjoint.T
    received = swap_pair(prepare_swap(state, x, g))
    x_pair, g_cols = compact_pair(state, x, g, received)

    both, w_full = make_keys(core, w_mine, swap_core(w_mine), x_pair, g_cols, wrows, n_mp)
    both = lax.all_to_all(both, ("pair", "mp"), 0, 0, axis_index_groups=groups, tiled=True)

    dw_mine, dw_theirs = weight_blocks(core, both, x_pair, 2 * n_z, wrows)
    dw_theirs, both = lax.optimization_barrier((dw_theirs, both))
    dw_sum = add_blocks(dw_mine, swap_core(dw_theirs))

    send, keep, kv = return_parts(both, w_full)
    received = swap_pair(send)
    dw_send, keep = lax.optimization_barrier((dw_sum, keep))
    dw_parts = lax.all_to_all(dw_send, ("pair", "z"), 0, 0, tiled=True)
    weight_grad = sum_blocks(turn, dw_parts, half, wrows)

    start = jnp.where(side == 0, 0, 2 - count)
    slots = jnp.minimum(jnp.stack([start, start + mask[0]]), 1)
    place = jnp.concatenate([mask, slots, hand.reshape(1)])
    activation_grad, kv_home = bring_home(place, keep, received, kv, seqs)
    return kv_home.T, activation_grad, weight_grad


def solution(mesh):
    n_dp, n_mp = mesh.devices.shape
    names = ("pair", "z", "core", "mp")
    split = Mesh(mesh.devices.reshape(2, n_dp // 4, 2, n_mp), names)
    dp = ("pair", "z", "core")
    return jax.shard_map(
        on_device,
        mesh=split,
        in_specs=(P(dp, "mp"), P((*dp, "mp"), None), P(dp, "mp"), P(dp)),
        out_specs=(P(dp, "mp"), P(dp, "mp"), P((*dp, "mp"), None)),
        check_vma=False,
    )
```
